32 devices in a mesh: dp: 4 (over z), seq: 8 (over y, x, core).
Axes of the slice: x: 2, y: 2, z: 4, core: 2. Of those that a mesh axis runs over, the one named last changes fastest.
Arguments:
- tokens: bfloat16 [8, 512, 2048], P('dp', 'seq'), may hold values from -6 to 6
- lengths: int32 [8], P('dp'), may hold values from 64 to 512, as said below
- norm_gain: float32 [2048], replicated, may hold values from 0.25 to 1.75
- mix_weight: bfloat16 [2048, 8224], P(('dp', 'seq')), may hold values from -0.125 to 0.125
- conv_weight: float32 [4, 6144], replicated, may hold values from -3 to 3
- decay_rate: float32 [16], replicated, may hold values from 0.0002 to 0.05
- out_gain: float32 [128], replicated, may hold values from 0.25 to 1.75
- out_weight: bfloat16 [2048, 2048], P(('dp', 'seq')), may hold values from -0.1875 to 0.1875
- mlp_gain: float32 [2048], replicated, may hold values from 0.25 to 1.75
- mlp_in_weight: bfloat16 [2048, 11264], P(('dp', 'seq')), may hold values from -0.125 to 0.125
- mlp_out_weight: bfloat16 [2048, 5632], P(('dp', 'seq')), may hold values from -0.15625 to 0.15625
- grad_out: bfloat16 [8, 512, 2048], P('dp', 'seq'), may hold values from -6 to 6
Outputs:
- result: bfloat16 [8, 512, 2048], P('dp', 'seq')
- grad_tokens: float32 [8, 512, 2048], P('dp', 'seq')
- grad_norm_gain: float32 [2048], replicated
- grad_mix_weight: float32 [2048, 8224], P(('dp', 'seq'))
- grad_conv_weight: float32 [4, 6144], replicated
- grad_decay_rate: float32 [16], replicated
- grad_out_gain: float32 [128], replicated
- grad_out_weight: float32 [2048, 2048], P(('dp', 'seq'))
- grad_mlp_gain: float32 [2048], replicated
- grad_mlp_in_weight: float32 [2048, 11264], P(('dp', 'seq'))
- grad_mlp_out_weight: float32 [2048, 5632], P(('dp', 'seq'))
The draws below stay inside these ranges and needn't reach their ends.
Inputs may be any that keep to these rules, and one draw needn't show every extreme that they name: `lengths`: in each data group of 2 consecutive sequences, one sequence drawn from the seed is valid over all 512 positions.
All inputs are finite; a program needn't handle non-finite values.
Results may differ from the reference program's by a relative error of at most 0.017.
Values may be sent and summed in bfloat16 or wider, within the bound.
No kernel may reach another device: no remote copies, remote signals or barrier semaphores. Data moves between devices by JAX's collectives and lax.ppermute only.
A program may use at most 704 MiB of HBM per device.

```python
from functools import partial
import jax
import jax.numpy as jnp
from jax import lax

D = 2048
HEADS = 16
HEAD_DIM = 128
FF = 5632
CONV = 4
BLOCK = 64
MICRO = 2
LENGTH = 512
SEQS = 8


def draw_lengths(key, part):
    key = jax.random.fold_in(key, 11)
    pick_key, length_key = jax.random.split(key)
    groups = SEQS // MICRO
    full_slot = jax.random.randint(pick_key, (groups, 1), 0, MICRO)
    drawn = jax.random.randint(length_key, (groups, MICRO), LENGTH // 8, LENGTH + 1)
    slot_index = jnp.arange(MICRO, dtype=jnp.int32)[None, :]
    chosen = jnp.where(slot_index == full_slot, LENGTH, drawn)
    return chosen.reshape(SEQS).astype(jnp.int32)


def draw_decay_rate(key, part):
    key = jax.random.fold_in(key, 23)
    low_end = 0.0002
    high_end = 0.05
    spread = jax.random.uniform(key, (HEADS,), jnp.float32, jnp.log(low_end), jnp.log(high_end))
    return jnp.exp(spread)


def steps_of(stream_key, dims, cuts, least, largest):
    level, own = 1.0, jax.random.fold_in(stream_key, 6)
    for position, blocks in cuts:
        steps = jnp.exp(jax.random.uniform(jax.random.fold_in(own, position), (blocks,), jnp.float32, least / len(cuts), largest / len(cuts)))
        level = level * jnp.repeat(steps, dims[position] // blocks).reshape([-1 if axis == position else 1 for axis in range(len(dims))])
    return level


def centred(key, shape, scale, bound, shards=(), kind=jnp.bfloat16):
    values = jax.random.normal(key, shape, jnp.float32) * scale
    if len(shards) > 0:
        values = steps_of(key, shape, shards, -0.22, 0.18) * values
    return jnp.clip(values, min=-bound, max=bound).astype(kind)


def setup_inputs(seed: int = 0) -> dict:
    key_list = jax.random.split(jax.random.key(seed), 13)
    tokens = centred(key_list[0], (SEQS, LENGTH, D), 1.0, 6.0, ((0, 4), (1, 8)))
    lengths = draw_lengths(jax.random.fold_in(key_list[12], 71), 0)
    norm_gain = jnp.clip(1.0 + 0.15 * jax.random.normal(key_list[2], (D,), jnp.float32), 0.25, 1.75)
    mix_weight = centred(key_list[3], (D, 4 * D + 2 * HEADS), D ** -0.5, 0.125, ((0, 32),))
    conv_weight = centred(key_list[4], (CONV, 3 * D), 0.5, 3.0, (), jnp.float32)
    decay_rate = draw_decay_rate(jax.random.fold_in(key_list[12], 71), 0)
    out_gain = jnp.clip(1.0 + 0.15 * jax.random.normal(key_list[6], (HEAD_DIM,), jnp.float32), 0.25, 1.75)
    out_weight = centred(key_list[7], (D, D), (D // 2) ** -0.5, 0.1875, ((0, 32),))
    mlp_gain = jnp.clip(1.0 + 0.15 * jax.random.normal(key_list[8], (D,), jnp.float32), 0.25, 1.75)
    mlp_in_weight = centred(key_list[9], (D, 2 * FF), D ** -0.5, 0.125, ((0, 32),))
    mlp_out_weight = centred(key_list[10], (D, FF), (FF // 4) ** -0.5, 0.15625, ((0, 32),))
    grad_out = centred(key_list[11], (SEQS, LENGTH, D), 1.0, 6.0, ((0, 4), (1, 8)))
    return dict(tokens=tokens, lengths=lengths, norm_gain=norm_gain, mix_weight=mix_weight, conv_weight=conv_weight, decay_rate=decay_rate, out_gain=out_gain, out_weight=out_weight, mlp_gain=mlp_gain, mlp_in_weight=mlp_in_weight, mlp_out_weight=mlp_out_weight, grad_out=grad_out)


eps_norm = 1e-05
eps_key = 1e-06
highest = lax.Precision.HIGHEST

@jax.custom_vjp
def low(v):
    return lax.optimization_barrier(v.astype(jnp.bfloat16)).astype(jnp.float32)

@jax.custom_vjp
def low_back(v):
    return v

def low_keep(v):
    return (low(v), None)

def low_pass(kept, grad):
    return (grad,)

def back_keep(v):
    return (v, None)

def back_low(kept, grad):
    return (low(grad),)
low.defvjp(low_keep, low_pass)
low_back.defvjp(back_keep, back_low)

def rms_scale(rows_in, gain):
    return rows_in * lax.rsqrt(lax.optimization_barrier(jnp.mean(rows_in * rows_in, axis=-1, keepdims=True)) + eps_norm) * gain

def key_norm(rows_in):
    return rows_in * lax.rsqrt(lax.optimization_barrier(jnp.sum(rows_in * rows_in, axis=-1, keepdims=True)) + eps_key)

def conv_mix(extended, conv_weight):
    conv_taps = conv_weight.shape[0]
    row_count = extended.shape[-2] - conv_taps + 1
    running = jnp.zeros(extended.shape[:-2] + (row_count, extended.shape[-1]), jnp.float32)
    for tap_index in range(conv_taps):
        running = running + extended[..., tap_index:tap_index + row_count, :] * conv_weight[tap_index]
    return running

def prepare(extended, conv_weight, head_count):
    mixed_rows = jax.nn.silu(conv_mix(extended, conv_weight))
    model_width = mixed_rows.shape[-1] // 3
    head_width = model_width // head_count
    head_shape = mixed_rows.shape[:-1] + (head_count, head_width)
    queries = key_norm(mixed_rows[..., :model_width].reshape(head_shape)) * float(head_width) ** (-0.5)
    key_rows = key_norm(mixed_rows[..., model_width:2 * model_width].reshape(head_shape))
    values = mixed_rows[..., 2 * model_width:].reshape(head_shape)
    return (queries, key_rows, values)

def finish(heads_out, gate_pre, out_gain):
    normed = rms_scale(heads_out, out_gain)
    return normed.reshape(gate_pre.shape) * jax.nn.silu(gate_pre)

def swiglu(gate_up):
    hidden_units = gate_up.shape[-1] // 2
    return jax.nn.silu(gate_up[..., :hidden_units]) * gate_up[..., hidden_units:]

def delta_block(state_now, block_in):
    queries, key_rows, values, logdecay, strength = block_in
    block_size = queries.shape[0]
    cumulative = jnp.cumsum(logdecay)
    spread = cumulative[:, None] - cumulative[None, :]
    row_index = lax.broadcasted_iota(jnp.int32, (block_size, block_size), 0)
    col_index = lax.broadcasted_iota(jnp.int32, (block_size, block_size), 1)
    below = (row_index > col_index).astype(jnp.float32)
    upto = (row_index >= col_index).astype(jnp.float32)
    fading = jnp.exp(jnp.minimum(spread, 0.0))
    lower_part = below * fading * strength[:, None] * jnp.dot(key_rows, key_rows.T, precision=highest)
    identity_block = jnp.eye(block_size, dtype=jnp.float32)
    inverse = identity_block - lower_part
    power_term = jnp.dot(lower_part, lower_part, precision=highest)
    factor_count = block_size.bit_length() - 2
    for factor_index in range(factor_count):
        inverse = jnp.dot(inverse, identity_block + power_term, precision=highest)
        if factor_index + 1 < factor_count:
            power_term = jnp.dot(power_term, power_term, precision=highest)
    growth = jnp.exp(cumulative)
    weighted = jnp.dot(inverse, key_rows * (strength * growth)[:, None], precision=highest)
    targets = jnp.dot(inverse, values * strength[:, None], precision=highest)
    fresh_values = targets - jnp.dot(weighted, state_now, precision=highest)
    scores = upto * fading * jnp.dot(queries, key_rows.T, precision=highest)
    output = jnp.dot(queries * growth[:, None], state_now, precision=highest) + jnp.dot(scores, fresh_values, precision=highest)
    last_decay = cumulative[-1]
    carried = jnp.exp(last_decay) * state_now + jnp.dot((key_rows * jnp.exp(last_decay - cumulative)[:, None]).T, fresh_values, precision=highest)
    return (carried, output)

def delta_rule(queries, key_rows, values, logit_decay, logit_strength, decay_scale, block_len):
    length, key_width = queries.shape
    value_width = values.shape[1]
    block_count = length // block_len
    logdecay = -decay_scale * jax.nn.softplus(logit_decay)
    strength = jax.nn.sigmoid(logit_strength)
    blocks = (queries.reshape(block_count, block_len, key_width), key_rows.reshape(block_count, block_len, key_width), values.reshape(block_count, block_len, value_width), logdecay.reshape(block_count, block_len), strength.reshape(block_count, block_len))
    initial = jnp.zeros((key_width, value_width), jnp.float32)
    final_state, outputs = lax.scan(jax.checkpoint(delta_block), initial, blocks)
    return outputs.reshape(length, value_width)

def forward(inputs, norm_gain, mix_weight, conv_weight, decay_rate, out_gain, out_weight, mlp_gain, mlp_in_weight, mlp_out_weight, valid_mask):
    model_width = inputs.shape[1]
    head_count = decay_rate.shape[0]
    qkv_width = 3 * model_width
    normed = low(rms_scale(inputs, norm_gain))
    projected = low(low_back(jnp.dot(normed, mix_weight, precision=highest)))
    mixed_in = projected[:, :qkv_width]
    gate_pre = projected[:, qkv_width:qkv_width + model_width]
    logit_decay = projected[:, qkv_width + model_width:qkv_width + model_width + head_count]
    logit_strength = projected[:, qkv_width + model_width + head_count:]
    extended = jnp.pad(mixed_in, ((conv_weight.shape[0] - 1, 0), (0, 0)))
    queries, key_rows, values = prepare(extended, conv_weight, head_count)
    queries = low(low_back(queries))
    key_rows = low(low_back(key_rows))
    values = low(low_back(values))
    per_head = jax.vmap(partial(delta_rule, block_len=BLOCK), in_axes=(1, 1, 1, 1, 1, 0), out_axes=1)
    heads_out = low(low_back(per_head(queries, key_rows, values, logit_decay, logit_strength, decay_rate)))
    mixed_rows = low(finish(heads_out, gate_pre, out_gain))
    hidden = inputs + low_back(jnp.dot(mixed_rows, out_weight, precision=highest))
    second = low(rms_scale(hidden, mlp_gain))
    gate_up = low(low_back(jnp.dot(second, mlp_in_weight, precision=highest)))
    activated = low(swiglu(gate_up))
    feed_out = low_back(jnp.dot(activated, mlp_out_weight.T, precision=highest))
    return valid_mask * (hidden + feed_out)

def reference(tokens, lengths, norm_gain, mix_weight, conv_weight, decay_rate, out_gain, out_weight, mlp_gain, mlp_in_weight, mlp_out_weight, grad_out):
    params = tuple((weight.astype(jnp.float32) for weight in (norm_gain, mix_weight, conv_weight, decay_rate, out_gain, out_weight, mlp_gain, mlp_in_weight, mlp_out_weight)))
    positions = jnp.arange(tokens.shape[1], dtype=jnp.int32)

    def per_sequence(totals, seq_item):
        seq_tokens, seq_length, seq_cot = seq_item
        valid_mask = (positions < seq_length).astype(jnp.float32)[:, None]
        inputs = seq_tokens.astype(jnp.float32)
        layer_out, pull_back = jax.vjp(partial(forward, valid_mask=valid_mask), inputs, *params)
        seq_grads = pull_back(seq_cot.astype(jnp.float32))
        totals = tuple((running + addend for running, addend in zip(totals, seq_grads[1:])))
        return (totals, (layer_out.astype(jnp.bfloat16), seq_grads[0]))
    zero_grads = tuple((jnp.zeros(weight.shape, jnp.float32) for weight in params))
    totals, (layer_out, grad_inputs) = lax.scan(per_sequence, zero_grads, (tokens, lengths, grad_out))
    return (layer_out, grad_inputs, totals[0], totals[1], totals[2], totals[3], totals[4], totals[5], totals[6], totals[7], totals[8])
```

```python
from functools import partial

import jax
import jax.numpy as jnp
from jax import lax
from jax.experimental import pallas as pl
from jax.experimental.pallas import tpu as pltpu
from jax.sharding import PartitionSpec as P

eps_norm = 1e-05
eps_key = 1e-06
LANES = 128
PAIR = 2
f32 = jnp.float32
low = jnp.bfloat16


def rms_scale(rows_in, gain):
    return (
        rows_in * lax.rsqrt(jnp.mean(rows_in * rows_in, axis=-1, keepdims=True) + eps_norm) * gain
    )


def swiglu(gate_up):
    hidden_units = gate_up.shape[-1] // 2
    return jax.nn.silu(gate_up[..., :hidden_units]) * gate_up[..., hidden_units:]


def mm(left, right):
    return jnp.dot(left.astype(low), right.astype(low), preferred_element_type=f32)


def mm_nt(left, right):
    return lax.dot_general(
        left.astype(low), right.astype(low), (((1,), (1,)), ((), ())), preferred_element_type=f32
    )


def halves(v):
    if isinstance(v, tuple):
        return v
    if v.dtype == low:
        return (v,)
    top = v.astype(low)
    return top, (v - top.astype(f32)).astype(low)


def dot_fine(left, right, dims):
    left, right = halves(left), halves(right)
    total = None
    for i, a in enumerate(left):
        for j, b in enumerate(right):
            if i + j < 2:
                term = lax.dot_general(a, b, (dims, ((), ())), preferred_element_type=f32)
                total = term if total is None else total + term
    return total


def fine(left, right):
    return dot_fine(left, right, ((1,), (0,)))


def fine_nt(left, right):
    return dot_fine(left, right, ((1,), (1,)))


def mm_exact(left, right):
    return jnp.dot(left, right, precision=lax.Precision.HIGHEST, preferred_element_type=f32)


def softplus(v):
    return jnp.maximum(v, 0.0) + jnp.log1p(jnp.exp(-jnp.abs(v)))


def grid_of(size):
    row = lax.broadcasted_iota(jnp.int32, (size, size), 0)
    col = lax.broadcasted_iota(jnp.int32, (size, size), 1)
    return row, col


def lower_inverses(parts, row, col):
    size = parts[0].shape[0]
    joined = (row // 2 == col // 2) & (row > col)
    unit = (row == col).astype(f32)
    inverses = [unit - jnp.where(joined, part, 0.0) for part in parts]
    width = 2
    while width < size:
        joined = (row // (2 * width) == col // (2 * width)) & (row // width > col // width)
        corners = [jnp.where(joined, part, 0.0) for part in parts]
        moved = [mm(corner, inverse) for corner, inverse in zip(corners, inverses)]
        steps = [mm(inverse, move) for inverse, move in zip(inverses, moved)]
        inverses = [inverse - change for inverse, change in zip(inverses, steps)]
        width *= 2
    return inverses


def fill_taps(ext, slot, m, proj, pos, prev, first, qkv):
    rows = proj.shape[2]
    ext[slot, 8 : 8 + rows, :] = proj[pos, m, :, :qkv].astype(f32)
    tail = proj[prev, m, rows - 16 :, :qkv].astype(f32)[8:]
    ext[slot, 0:8, :] = jnp.where(first, 0.0, tail)


def conv_rows(ext, m, conv, rows):
    taps = conv.shape[0]
    total = conv[0:1, :] * ext[m, 9 - taps : 9 - taps + rows, :]
    for j in range(1, taps):
        total = total + conv[j : j + 1, :] * ext[m, 9 - taps + j : 9 - taps + j + rows, :]
    return total


def forward_kernel(
    local_heads,
    perm,
    proj,
    logit,
    conv,
    rates,
    gain,
    mixed,
    heads_out,
    qkv_out,
    gates,
    inv_t,
    weighted_t,
    fresh,
    states,
    ext,
    targets,
    weighted,
    scores,
    keys_t,
    state,
):
    blocks, micro, rows, _ = proj.shape
    cols = local_heads * LANES
    qkv = 3 * cols
    row, col = grid_of(rows)
    upto = (row >= col).astype(f32)
    lane = lax.broadcasted_iota(jnp.int32, (rows, LANES), 1)
    scale = float(LANES) ** -0.5

    def prepare(i, carry):
        work = []
        for part in range(PAIR):
            b = i * PAIR + part
            pos, prev = perm[b], perm[jnp.maximum(b - 1, 0)]
            for m in range(micro):
                slot = part * micro + m
                fill_taps(ext, slot, m, proj, pos, prev, b == 0, qkv)
                conv_out = conv_rows(ext, slot, conv, rows)
                act = conv_out * jax.nn.sigmoid(conv_out)
                logits = logit[pos, m].astype(f32)
                decay = -rates[...] * softplus(logits)
                strength = jax.nn.sigmoid(logits)
                total = mm_exact(upto, decay)
                total_t = total.T
                gates[b, m] = jnp.where(lane < local_heads, total, strength)
                growth = jnp.exp(total)
                fade = jnp.exp(total[rows - 1 : rows, :] - total)
                for h in range(local_heads):
                    raw_q = act[:, h * LANES : (h + 1) * LANES]
                    raw_k = act[:, cols + h * LANES : cols + (h + 1) * LANES]
                    q = raw_q * (
                        lax.rsqrt(jnp.sum(raw_q * raw_q, axis=1, keepdims=True) + eps_key) * scale
                    )
                    k = raw_k * lax.rsqrt(jnp.sum(raw_k * raw_k, axis=1, keepdims=True) + eps_key)
                    q = q.astype(low)
                    k = k.astype(low)
                    v = act[:, 2 * cols + h * LANES : 2 * cols + (h + 1) * LANES].astype(low)
                    qkv_out[b, m, :, h * LANES : (h + 1) * LANES] = q
                    qkv_out[b, m, :, cols + h * LANES : cols + (h + 1) * LANES] = k
                    qkv_out[b, m, :, 2 * cols + h * LANES : 2 * cols + (h + 1) * LANES] = v
                    beta = strength[:, local_heads + h : local_heads + h + 1]
                    spread = jnp.exp(
                        jnp.minimum(total[:, h : h + 1] - total_t[h : h + 1, :], 0.0)
                    )
                    work.append(
                        (b, m * local_heads + h, q, k, v, beta, spread, growth[:, h : h + 1], fade[:, h : h + 1])
                    )
        same = [mm_nt(k, k) for _, _, _, k, *_ in work]
        cross = [mm_nt(q, k) for _, _, q, k, *_ in work]
        parts = [
            jnp.where(row > col, item[6] * item[5] * dots, 0.0) for item, dots in zip(work, same)
        ]
        inverses = lower_inverses(parts, row, col)
        keyed = [fine(inv, item[3].astype(f32) * (item[5] * item[7])) for inv, item in zip(inverses, work)]
        valued = [fine(inv, item[4].astype(f32) * item[5]) for inv, item in zip(inverses, work)]
        for n, (b, p, q, k, v, beta, spread, grow, shrink) in enumerate(work):
            inv_t[b, p] = inverses[n].T
            weighted[b, p] = keyed[n]
            weighted_t[b, p] = keyed[n].T
            targets[b, p] = valued[n]
            scores[b, p] = upto * spread * cross[n]
            keys_t[b, p] = (k.astype(f32) * shrink).T
        return carry

    lax.fori_loop(0, blocks // PAIR, prepare, 0)
    state[...] = jnp.zeros_like(state)

    def step(b, carry):
        pos = perm[b]
        growth = [jnp.exp(gates[b, m]) for m in range(micro)]
        chains = [(m, h, m * local_heads + h) for m in range(micro) for h in range(local_heads)]
        now = [state[p] for _, _, p in chains]
        now_halves = [halves(v) for v in now]
        new = [
            targets[b, p] - fine(weighted[b, p], parts) for (_, _, p), parts in zip(chains, now_halves)
        ]
        new_halves = [halves(v) for v in new]
        moved = [fine(keys_t[b, p], parts) for (_, _, p), parts in zip(chains, new_halves)]
        for (m, h, p), old, fed in zip(chains, now, moved):
            states[b, p] = old
            state[p] = growth[m][rows - 1 : rows, h : h + 1] * old + fed
        outs = []
        for (m, h, p), fill, parts in zip(chains, new_halves, now_halves):
            q = qkv_out[b, m, :, h * LANES : (h + 1) * LANES].astype(f32)
            outs.append(fine(q * growth[m][:, h : h + 1], parts) + fine(scores[b, p], fill))
        for (m, h, p), fill, out in zip(chains, new, outs):
            fresh[b, p] = fill
            out = out.astype(low)
            heads_out[b, m, :, h * LANES : (h + 1) * LANES] = out
            out = out.astype(f32)
            gate = proj[pos, m, :, 3 * cols + h * LANES : 3 * cols + (h + 1) * LANES].astype(f32)
            normed = out * lax.rsqrt(jnp.mean(out * out, axis=1, keepdims=True) + eps_norm) * gain[...]
            mixed[pos, m, :, h * LANES : (h + 1) * LANES] = (
                normed * (gate * jax.nn.sigmoid(gate))
            ).astype(low)
        return carry

    lax.fori_loop(0, blocks, step, 0)


def backward_kernel(
    local_heads,
    perm,
    grad_mixed,
    proj,
    logit,
    conv,
    rates,
    gain,
    heads_out,
    qkv_in,
    gates,
    inv_t,
    weighted_t,
    fresh,
    states,
    grad_proj,
    grad_logit,
    grad_conv,
    grad_rates,
    grad_gain,
    ext,
    dext,
    ahead,
    conv_sum,
    grad_out,
    value_part,
    state_part,
    grad_fresh,
    grad_states,
    grad_state,
):
    blocks, micro, rows, _ = proj.shape
    cols = local_heads * LANES
    qkv = 3 * cols
    taps = conv.shape[0]
    row, col = grid_of(rows)
    lane = lax.broadcasted_iota(jnp.int32, (rows, LANES), 1)
    last = lax.broadcasted_iota(jnp.int32, (rows, 1), 0) == rows - 1
    scale = float(LANES) ** -0.5
    upto_t = (col >= row).astype(f32)
    grad_gain[...] = jnp.zeros_like(grad_gain)
    grad_rates[...] = jnp.zeros_like(grad_rates)
    conv_sum[...] = jnp.zeros_like(conv_sum)
    ahead[...] = jnp.zeros_like(ahead)
    grad_state[...] = jnp.zeros_like(grad_state)

    def prepare(b, carry):
        pos = perm[b]
        work = []
        for m in range(micro):
            total = gates[b, m]
            growth = jnp.exp(total)
            total_t = total.T
            for h in range(local_heads):
                p = m * local_heads + h
                here = slice(h * LANES, (h + 1) * LANES)
                out = heads_out[b, m, :, here].astype(f32)
                gate = proj[pos, m, :, 3 * cols + h * LANES : 3 * cols + (h + 1) * LANES].astype(f32)
                dmixed = grad_mixed[pos, m, :, here].astype(f32)
                root = lax.rsqrt(jnp.mean(out * out, axis=1, keepdims=True) + eps_norm)
                unit = out * root
                sig = jax.nn.sigmoid(gate)
                dnormed = dmixed * (gate * sig)
                grad_proj[pos, m, :, 3 * cols + h * LANES : 3 * cols + (h + 1) * LANES] = (
                    dmixed * (unit * gain[...]) * (sig * (1.0 + gate * (1.0 - sig)))
                ).astype(low)
                grad_gain[...] += jnp.sum(dnormed * unit, axis=0, keepdims=True)
                dunit = dnormed * gain[...]
                dout = root * (dunit - unit * jnp.mean(unit * dunit, axis=1, keepdims=True))
                dout = dout.astype(low)
                grad_out[b, p] = dout.astype(grad_out.dtype)
                q = qkv_in[b, m, :, here]
                k = qkv_in[b, m, :, cols + h * LANES : cols + (h + 1) * LANES]
                spread_t = jnp.exp(jnp.minimum(total_t[h : h + 1, :] - total[:, h : h + 1], 0.0))
                grown_t = (q.astype(f32) * growth[:, h : h + 1]).T
                work.append((p, q, k, dout, upto_t * spread_t, grown_t))
        dots = [mm_nt(k, q) for _, q, k, *_ in work]
        parts = [fine(spread * dot, dout) for (_, _, _, dout, spread, _), dot in zip(work, dots)]
        fed = [fine(grown_t, dout) for _, _, _, dout, _, grown_t in work]
        for (p, *_), part, feed in zip(work, parts, fed):
            value_part[b, p] = part
            state_part[b, p] = feed
        return carry

    lax.fori_loop(0, blocks, prepare, 0)

    def step(i, carry):
        b = blocks - 1 - i
        chains = [(m, h, m * local_heads + h) for m in range(micro) for h in range(local_heads)]
        total = [gates[b, m] for m in range(micro)]
        fade = [jnp.exp(v[rows - 1 : rows, :] - v) for v in total]
        later = [grad_state[p] for _, _, p in chains]
        dnew = []
        for (m, h, p), grad in zip(chains, later):
            k = qkv_in[b, m, :, cols + h * LANES : cols + (h + 1) * LANES].astype(f32)
            dnew.append(value_part[b, p] + fine(k * fade[m][:, h : h + 1], grad))
        moved = [fine(weighted_t[b, p], grad) for (_, _, p), grad in zip(chains, dnew)]
        for (m, h, p), grad, fill, move in zip(chains, later, dnew, moved):
            grad_states[b, p] = grad
            grad_fresh[b, p] = fill
            carried = jnp.exp(total[m][rows - 1 : rows, h : h + 1])
            grad_state[p] = state_part[b, p] + carried * grad - move
        return carry

    lax.fori_loop(0, blocks, step, 0)

    def finish(i, carry):
        b = blocks - 1 - i
        pos, prev = perm[b], perm[jnp.maximum(b - 1, 0)]
        work = []
        for m in range(micro):
            total = gates[b, m]
            total_t = total.T
            growth = jnp.exp(total)
            fade = jnp.exp(total[rows - 1 : rows, :] - total)
            for h in range(local_heads):
                p = m * local_heads + h
                q = qkv_in[b, m, :, h * LANES : (h + 1) * LANES]
                k = qkv_in[b, m, :, cols + h * LANES : cols + (h + 1) * LANES]
                v = qkv_in[b, m, :, 2 * cols + h * LANES : 2 * cols + (h + 1) * LANES]
                beta = total[:, local_heads + h : local_heads + h + 1]
                spread = jnp.exp(jnp.minimum(total[:, h : h + 1] - total_t[h : h + 1, :], 0.0))
                work.append(
                    (p, q, k, v, beta, spread, growth[:, h : h + 1], fade[:, h : h + 1], growth[rows - 1 : rows, h : h + 1])
                )
        number = range(len(work))
        queries = [item[1] for item in work]
        keys = [item[2] for item in work]
        douts = [grad_out[b, item[0]].astype(low) for item in work]
        news = [halves(fresh[b, item[0]]) for item in work]
        nows = [halves(states[b, item[0]]) for item in work]
        laters = [halves(grad_states[b, item[0]]) for item in work]
        dright = [fine(inv_t[b, item[0]], grad_fresh[b, item[0]]) for item in work]
        dgrown = [fine_nt(douts[n], nows[n]) for n in number]
        dshrunk = [fine_nt(news[n], laters[n]) for n in number]
        dots = [mm_nt(queries[n], keys[n]) for n in number]
        same = [mm_nt(keys[n], keys[n]) for n in number]
        dscores = [fine_nt(douts[n], news[n]) for n in number]
        dright_halves = [halves(v) for v in dright]
        dweighted = [-fine_nt(dright_halves[n], nows[n]) for n in number]
        dbelow = [fine_nt(dright_halves[n], news[n]) for n in number]
        keyed, moved = [], []
        for n in number:
            beta, spread = work[n][4], work[n][5]
            dscores[n] = dscores[n] * jnp.where(row >= col, spread, 0.0)
            dbelow[n] = dbelow[n] * jnp.where(row > col, -spread, 0.0)
            keyed.append(dbelow[n] * same[n])
            moved.append(dscores[n] * dots[n] + keyed[n] * beta)
            dbelow[n] = dbelow[n] * beta
        dq = [fine(dscores[n], keys[n]) for n in number]
        dk = [fine(dscores[n].T, queries[n]) for n in number]
        dk_same = [fine(dbelow[n] + dbelow[n].T, keys[n]) for n in number]
        for m in range(micro):
            fill_taps(ext, m, m, proj, pos, prev, b == 0, qkv)
            conv_out = conv_rows(ext, m, conv, rows)
            sig = jax.nn.sigmoid(conv_out)
            act = conv_out * sig
            slope = sig * (1.0 + conv_out * (1.0 - sig))
            dtotal = jnp.zeros((rows, LANES), f32)
            dstrength = jnp.zeros((rows, LANES), f32)
            for h in range(local_heads):
                n = m * local_heads + h
                p, q, k, v, beta, spread, grow, shrink, carried = work[n]
                q32, k32, v32 = q.astype(f32), k.astype(f32), v.astype(f32)
                dquery = grow * dgrown[n] + dq[n]
                dkey = (beta * grow) * dweighted[n] + shrink * dshrunk[n] + dk[n] + dk_same[n]
                dvalue = beta * dright[n]
                weighed = dweighted[n] * k32 * grow
                shrunk = dshrunk[n] * k32 * shrink
                dstr = jnp.sum(dright[n] * v32 + weighed, axis=1, keepdims=True) + jnp.sum(
                    keyed[n], axis=1, keepdims=True
                )
                dtot = jnp.sum(
                    dgrown[n] * q32 * grow + weighed * beta - shrunk, axis=1, keepdims=True
                ) + jnp.sum(moved[n] - moved[n].T, axis=1, keepdims=True)
                end = jnp.sum(shrunk) + jnp.sum(carried * (states[b, p] * grad_states[b, p]))
                dtot = dtot + jnp.where(last, end, 0.0)
                dtotal = dtotal + jnp.where(lane == h, dtot, 0.0)
                dstrength = dstrength + jnp.where(lane == local_heads + h, dstr, 0.0)
                for part, grad in ((0, dquery), (1, dkey), (2, dvalue)):
                    at = part * cols + h * LANES
                    grad = grad.astype(low).astype(f32)
                    if part == 0:
                        grad = grad * scale
                    if part < 2:
                        raw = act[:, at : at + LANES]
                        root = lax.rsqrt(jnp.sum(raw * raw, axis=1, keepdims=True) + eps_key)
                        unit = raw * root
                        grad = root * (grad - unit * jnp.sum(unit * grad, axis=1, keepdims=True))
                    dext[m, 0:rows, at : at + LANES] = grad * slope[:, at : at + LANES]
            dext[m, rows : rows + 8, :] = ahead[m]
            dconv = dext[m, 0:rows, :]
            ahead[m] = dconv[0:8, :]
            du = conv[taps - 1 : taps, :] * dconv
            for j in range(taps - 1):
                du = du + conv[j : j + 1, :] * dext[m, taps - 1 - j : taps - 1 - j + rows, :]
            grad_proj[pos, m, :, :qkv] = du.astype(low)
            for j in range(taps):
                term = dconv * ext[m, 9 - taps + j : 9 - taps + j + rows, :]
                conv_sum[j] += jnp.sum(term.reshape(rows // 8, 8, qkv), axis=0)
            logits = logit[pos, m].astype(f32)
            ddecay = mm_exact(upto_t, dtotal)
            strength = gates[b, m]
            dlogit = jnp.where(
                lane < local_heads,
                -rates[...] * jax.nn.sigmoid(logits) * ddecay,
                strength * (1.0 - strength) * dstrength,
            )
            grad_logit[pos, m] = jnp.where(lane < 2 * local_heads, dlogit, 0.0).astype(low)
            grad_rates[...] -= jnp.sum(softplus(logits) * ddecay, axis=0, keepdims=True)
        return carry

    lax.fori_loop(0, blocks, finish, 0)
    for j in range(taps):
        grad_conv[j : j + 1, :] = jnp.sum(conv_sum[j], axis=0, keepdims=True)


def in_vmem():
    return pl.BlockSpec(memory_space=pltpu.VMEM)


def heads_forward(perm, proj, logit, conv, rates, gain, local_heads):
    blocks, micro, rows, _ = proj.shape
    cols = local_heads * LANES
    chains = micro * local_heads

    def shape(dims, kind):
        return jax.ShapeDtypeStruct(dims, kind)

    return pl.pallas_call(
        partial(forward_kernel, local_heads),
        out_shape=(
            shape((blocks, micro, rows, cols), low),
            shape((blocks, micro, rows, cols), low),
            shape((blocks, micro, rows, 3 * cols), low),
            shape((blocks, micro, rows, LANES), f32),
            shape((blocks, chains, rows, rows), f32),
            shape((blocks, chains, LANES, rows), f32),
            shape((blocks, chains, rows, LANES), f32),
            shape((blocks, chains, LANES, LANES), f32),
        ),
        in_specs=[pl.BlockSpec(memory_space=pltpu.SMEM)] + [in_vmem()] * 5,
        out_specs=(in_vmem(),) * 8,
        scratch_shapes=[
            pltpu.VMEM((PAIR * micro, rows + 8, 3 * cols), f32),
            pltpu.VMEM((blocks, chains, rows, LANES), f32),
            pltpu.VMEM((blocks, chains, rows, LANES), f32),
            pltpu.VMEM((blocks, chains, rows, rows), f32),
            pltpu.VMEM((blocks, chains, LANES, rows), f32),
            pltpu.VMEM((chains, LANES, LANES), f32),
        ],
        compiler_params=pltpu.CompilerParams(vmem_limit_bytes=50 * 1024 * 1024),
        name="heads_forward",
    )(perm, proj, logit, conv, rates, gain)


def heads_backward(perm, grad_mixed, proj, logit, conv, rates, gain, kept, local_heads):
    blocks, micro, rows, wide = proj.shape
    cols = local_heads * LANES
    chains = micro * local_heads
    taps = conv.shape[0]

    def shape(dims, kind):
        return jax.ShapeDtypeStruct(dims, kind)

    return pl.pallas_call(
        partial(backward_kernel, local_heads),
        out_shape=(
            shape((blocks, micro, rows, wide), low),
            shape((blocks, micro, rows, LANES), low),
            shape((taps, 3 * cols), f32),
            shape((1, LANES), f32),
            shape((1, LANES), f32),
        ),
        in_specs=[pl.BlockSpec(memory_space=pltpu.SMEM)] + [in_vmem()] * 13,
        out_specs=(in_vmem(),) * 5,
        scratch_shapes=[
            pltpu.VMEM((micro, rows + 8, 3 * cols), f32),
            pltpu.VMEM((micro, rows + 8, 3 * cols), f32),
            pltpu.VMEM((micro, 8, 3 * cols), f32),
            pltpu.VMEM((taps, 8, 3 * cols), f32),
            pltpu.VMEM((blocks, chains, rows, LANES), f32),
            pltpu.VMEM((blocks, chains, rows, LANES), f32),
            pltpu.VMEM((blocks, chains, LANES, LANES), f32),
            pltpu.VMEM((blocks, chains, rows, LANES), f32),
            pltpu.VMEM((blocks, chains, LANES, LANES), f32),
            pltpu.VMEM((chains, LANES, LANES), f32),
        ],
        compiler_params=pltpu.CompilerParams(vmem_limit_bytes=50 * 1024 * 1024),
        name="heads_backward",
    )(perm, grad_mixed, proj, logit, conv, rates, gain, *kept)


both = ("dp", "seq")


def swap(value, axis, bit):
    return lax.ppermute(value, axis, [(i, i ^ bit) for i in range(lax.axis_size(axis))])


def after(value, *others):
    return lax.optimization_barrier((value, *others))[0]


def gather_places():
    peers = lax.axis_size("seq")
    place = jnp.arange(peers, dtype=jnp.int32)
    if peers != 8:
        return place
    place = place ^ lax.axis_index("seq").astype(jnp.int32)
    return place // 2 + 4 * (place % 2)


def gather_seq(rows_in):
    if lax.axis_size("seq") != 8:
        return lax.all_gather(rows_in, "seq", axis=0, tiled=True)
    half = rows_in.shape[0] // 2
    top, bottom = rows_in[:half], rows_in[half:]
    top_x, bottom_y = swap(top, "seq", 2), swap(bottom, "seq", 4)
    top_y = swap(jnp.concatenate([top, top_x]), "seq", 4)
    bottom_x = swap(jnp.concatenate([bottom, bottom_y]), "seq", 2)
    near = jnp.concatenate(
        [top, bottom, top_x, bottom_x[:half], top_y[:half], bottom_y, top_y[half:], bottom_x[half:]]
    )
    return jnp.concatenate([near, swap(near, "seq", 1)])


def scatter_seq(partial_rows):
    peers = lax.axis_size("seq")
    if peers != 8:
        return lax.psum_scatter(
            partial_rows.astype(low), "seq", scatter_dimension=0, tiled=True
        ).astype(f32)
    terms = partial_rows.astype(low).reshape(peers, -1, partial_rows.shape[-1])
    half = terms.shape[1] // 2
    near = terms[:4].astype(f32) + swap(terms[4:], "seq", 1).astype(f32)
    top, bottom = near[:, :half].astype(low), near[:, half:].astype(low)
    top_x = swap(top[1::2], "seq", 2)
    bottom_y = swap(bottom[2:], "seq", 4)
    top = near[0::2, :half] + top_x.astype(f32)
    bottom = near[:2, half:] + bottom_y.astype(f32)
    top_y = swap(top[1].astype(low), "seq", 4)
    bottom_x = swap(bottom[1].astype(low), "seq", 2)
    return jnp.concatenate([top[0] + top_y.astype(f32), bottom[0] + bottom_x.astype(f32)])


def sum_all(value):
    for axis in both:
        bit = 1
        while bit < lax.axis_size(axis):
            value = value + swap(value, axis, bit)
            bit *= 2
    return value


def gather_dp_small(value):
    groups = lax.axis_size("dp")
    parts, bit = value[None], 1
    while bit < groups:
        parts = jnp.concatenate([parts, swap(parts, "dp", bit)])
        bit *= 2
    places = jnp.arange(groups, dtype=jnp.int32) ^ lax.axis_index("dp").astype(jnp.int32)
    return jnp.take(parts, places, axis=0)


def to_columns(pieces):
    rows_here = lax.all_to_all(pieces, "seq", split_axis=0, concat_axis=0, tiled=True)
    return rows_here.reshape(-1, pieces.shape[-1])


def gather_dp(rows_here):
    return lax.all_gather(rows_here, "dp", axis=0, tiled=True)


def columns_back(term):
    peers = lax.axis_size("seq")
    own = lax.psum_scatter(term.astype(low), "dp", scatter_dimension=0, tiled=True)
    own = own.reshape(peers, own.shape[0] // peers, own.shape[1])
    return lax.all_to_all(own, "seq", split_axis=0, concat_axis=0, tiled=True).transpose(1, 0, 2)


def row_pairs(inverse):
    groups, peers = lax.axis_size("dp"), lax.axis_size("seq")
    pairs = [(j * groups + d, d * peers + j) for d in range(groups) for j in range(peers)]
    return [(b, a) for a, b in pairs] if inverse else pairs


def dot32(left, right):
    return jnp.dot(left, right, preferred_element_type=f32)


def dot_t(left, right):
    return lax.dot_general(left, right, (((1,), (1,)), ((), ())), preferred_element_type=f32)


def t_dot(left, right):
    return lax.dot_general(left, right, (((0,), (0,)), ((), ())), preferred_element_type=f32)


def shards(
    tokens,
    lengths,
    norm_gain,
    mix_weight,
    conv_weight,
    decay_rate,
    out_gain,
    out_weight,
    mlp_gain,
    mlp_in_weight,
    mlp_out_weight,
    grad_out,
):
    micro, seq_rows, width = tokens.shape
    heads = decay_rate.shape[0]
    groups = lax.axis_size("dp")
    peers = lax.axis_size("seq")
    here = lax.axis_index("seq")
    local_heads = heads // peers
    taps = conv_weight.shape[0]
    units = mlp_out_weight.shape[1]
    local_units = units // peers
    own_rows = mix_weight.shape[0]
    cols = width // peers
    logit_cols = 2 * local_heads

    positions = here * seq_rows + lax.broadcasted_iota(jnp.int32, (micro, seq_rows), 1)
    valid = (positions < lengths[:, None]).astype(f32).reshape(-1, 1)
    inputs = tokens.reshape(-1, width).astype(f32)

    main = mix_weight[:, : 4 * width].reshape(own_rows, 4, peers, cols)
    logits = mix_weight[:, 4 * width :].reshape(own_rows, 2, peers, local_heads)
    mix_rows = to_columns(
        jnp.concatenate(
            [
                main.transpose(2, 0, 1, 3).reshape(peers, own_rows, 4 * cols),
                logits.transpose(2, 0, 1, 3).reshape(peers, own_rows, logit_cols),
                jnp.zeros((peers, own_rows, LANES - logit_cols), low),
            ],
            axis=2,
        )
    )
    mix_here = gather_dp(mix_rows[:, : 4 * cols])
    logit_here = gather_dp_small(mix_rows[:, 4 * cols :]).reshape(width, LANES)
    normed, norm_back = jax.vjp(rms_scale, inputs, norm_gain)
    normed_all = gather_seq(normed.astype(low))
    in_pieces = mlp_in_weight.reshape(own_rows, 2, peers, local_units).transpose(2, 0, 1, 3)
    in_rows = to_columns(
        after(in_pieces.reshape(peers, own_rows, 2 * local_units), mix_rows)
    )
    down_rows = to_columns(
        after(mlp_out_weight.reshape(own_rows, peers, local_units).transpose(1, 0, 2), mix_rows)
    )
    out_rows = lax.ppermute(after(out_weight, mix_rows), both, row_pairs(False))
    mix_here, in_rows, down_rows, out_rows = lax.optimization_barrier(
        (mix_here, in_rows, down_rows, out_rows)
    )
    out_here = gather_dp(out_rows)
    in_here = gather_dp(in_rows)
    down_here = gather_dp(down_rows)

    projected = dot32(normed_all, mix_here).astype(low).reshape(peers, micro, seq_rows, -1)
    logit_pre = dot32(normed_all, logit_here).astype(low).reshape(peers, micro, seq_rows, LANES)
    conv_here = lax.dynamic_index_in_dim(
        conv_weight.reshape(taps, 3, peers, cols), here, 2, keepdims=False
    ).reshape(taps, 3 * cols)
    rates_here = lax.dynamic_slice_in_dim(decay_rate, here * local_heads, local_heads)
    rate_lanes = jnp.pad(rates_here, (0, LANES - local_heads)).reshape(1, LANES)
    gain_row = out_gain.reshape(1, LANES)
    places = gather_places()
    mixed_rows, *kept = heads_forward(
        places, projected, logit_pre, conv_here, rate_lanes, gain_row, local_heads
    )
    mixed_low = mixed_rows.reshape(-1, cols)
    hidden = inputs + scatter_seq(dot32(mixed_low, out_here))

    second, second_back = jax.vjp(rms_scale, hidden, mlp_gain)
    second_all = gather_seq(second.astype(low))
    cotangent = valid * grad_out.reshape(-1, width).astype(f32)
    cot_all = gather_seq(after(cotangent.astype(low), second_all))
    gate_up = dot32(second_all, in_here).astype(low)
    activated, swiglu_back = jax.vjp(swiglu, gate_up.astype(f32))
    activated_low = activated.astype(low)
    (grad_gate_up,) = swiglu_back(dot32(cot_all, down_here))
    grad_gate_low = grad_gate_up.astype(low)
    grad_second = scatter_seq(dot_t(grad_gate_low, in_here))
    grad_hidden_norm, grad_mlp_gain = second_back(grad_second)
    grad_hidden = cotangent + grad_hidden_norm
    branch_all = gather_seq(grad_hidden.astype(low))
    grad_in = columns_back(t_dot(second_all, grad_gate_low))
    grad_down = columns_back(t_dot(cot_all, activated_low))

    grad_mixed = dot_t(branch_all, out_here).reshape(peers, micro, seq_rows, cols)
    grad_out_own = lax.ppermute(
        lax.psum_scatter(
            t_dot(mixed_low, branch_all).astype(low), "dp", scatter_dimension=0, tiled=True
        ),
        both,
        row_pairs(True),
    )
    grad_projected, grad_logits, grad_conv, rate_sums, gain_sums = heads_backward(
        places, grad_mixed, projected, logit_pre, conv_here, rate_lanes, gain_row, kept, local_heads
    )
    grad_projected = grad_projected.reshape(-1, 4 * cols)
    grad_logits = grad_logits.reshape(-1, LANES)
    grad_normed = scatter_seq(
        dot_t(grad_projected, mix_here) + dot_t(grad_logits, logit_here)
    )
    grad_inputs_norm, grad_norm_gain = norm_back(grad_normed)
    grad_tokens = grad_hidden + grad_inputs_norm
    grad_mix = columns_back(t_dot(normed_all, grad_projected))
    grad_mix_main = grad_mix.reshape(own_rows, peers, 4, cols).transpose(0, 2, 1, 3)
    logit_terms = t_dot(grad_logits[:, :logit_cols], normed_all)
    logit_terms = logit_terms.reshape(logit_cols, groups * peers, own_rows).transpose(1, 0, 2)
    logit_terms = lax.all_to_all(logit_terms, both, split_axis=0, concat_axis=0, tiled=True)
    logit_terms = logit_terms.reshape(groups, peers, 2, local_heads, own_rows).sum(0)
    grad_mix_logits = logit_terms.transpose(3, 1, 0, 2).reshape(own_rows, 2 * heads)

    feed_out = scatter_seq(dot_t(after(activated_low, grad_projected), down_here))
    result = (valid * (hidden + feed_out)).astype(low)

    conv_terms = lax.dynamic_update_slice(
        jnp.zeros((taps, 3, peers, cols), f32),
        grad_conv.reshape(taps, 3, 1, cols),
        (0, 0, here, 0),
    )
    rate_terms = lax.dynamic_update_slice(
        jnp.zeros((LANES,), f32), rate_sums[0, :local_heads], (here * local_heads,)
    )
    sizes = [width, width, LANES, LANES, taps * 3 * width]
    summed = sum_all(
        jnp.concatenate(
            [
                grad_norm_gain,
                grad_mlp_gain,
                gain_sums[0],
                rate_terms,
                conv_terms.reshape(-1),
            ]
        ).reshape(-1, LANES)
    ).reshape(-1)
    ends = [sum(sizes[: i + 1]) for i in range(len(sizes))]
    sums = [summed[end - size : end] for end, size in zip(ends, sizes)]
    return (
        result.reshape(tokens.shape),
        grad_tokens.reshape(tokens.shape),
        sums[0],
        jnp.concatenate(
            [grad_mix_main.reshape(own_rows, 4 * width).astype(f32), grad_mix_logits], axis=1
        ),
        sums[4].reshape(taps, 3 * width),
        sums[3][:heads],
        sums[2],
        grad_out_own.astype(f32),
        sums[1],
        grad_in.reshape(own_rows, peers, 2, local_units)
        .transpose(0, 2, 1, 3)
        .reshape(own_rows, 2 * units)
        .astype(f32),
        grad_down.reshape(own_rows, units).astype(f32),
    )


def solution(mesh):
    in_specs = (
        P("dp", "seq", None),
        P("dp"),
        P(),
        P(("dp", "seq"), None),
        P(),
        P(),
        P(),
        P(("dp", "seq"), None),
        P(),
        P(("dp", "seq"), None),
        P(("dp", "seq"), None),
        P("dp", "seq", None),
    )
    out_specs = (
        P("dp", "seq", None),
        P("dp", "seq", None),
        P(),
        P(("dp", "seq"), None),
        P(),
        P(),
        P(),
        P(("dp", "seq"), None),
        P(),
        P(("dp", "seq"), None),
        P(("dp", "seq"), None),
    )
    return jax.shard_map(shards, mesh=mesh, in_specs=in_specs, out_specs=out_specs, check_vma=False)
```

```python
from functools import partial

import jax
import jax.numpy as jnp
from jax import lax
from jax.experimental import pallas as pl
from jax.experimental.pallas import tpu as pltpu
from jax.sharding import PartitionSpec as P

eps_norm = 1e-05
eps_key = 1e-06
LANES = 128
PAIR = 2
f32 = jnp.float32
low = jnp.bfloat16


def rms_scale(rows_in, gain):
    return (
        rows_in * lax.rsqrt(jnp.mean(rows_in * rows_in, axis=-1, keepdims=True) + eps_norm) * gain
    )


def swiglu(gate_up):
    hidden_units = gate_up.shape[-1] // 2
    return jax.nn.silu(gate_up[..., :hidden_units]) * gate_up[..., hidden_units:]


def mm(left, right):
    return jnp.dot(left.astype(low), right.astype(low), preferred_element_type=f32)


def mm_nt(left, right):
    return lax.dot_general(
        left.astype(low), right.astype(low), (((1,), (1,)), ((), ())), preferred_element_type=f32
    )


def halves(v):
    if isinstance(v, tuple):
        return v
    if v.dtype == low:
        return (v,)
    top = v.astype(low)
    return top, (v - top.astype(f32)).astype(low)


def dot_fine(left, right, dims):
    left, right = halves(left), halves(right)
    total = None
    for i, a in enumerate(left):
        for j, b in enumerate(right):
            if i + j < 2:
                term = lax.dot_general(a, b, (dims, ((), ())), preferred_element_type=f32)
                total = term if total is None else total + term
    return total


def fine(left, right):
    return dot_fine(left, right, ((1,), (0,)))


def fine_nt(left, right):
    return dot_fine(left, right, ((1,), (1,)))


def mm_exact(left, right):
    return jnp.dot(left, right, precision=lax.Precision.HIGHEST, preferred_element_type=f32)


def softplus(v):
    return jnp.maximum(v, 0.0) + jnp.log1p(jnp.exp(-jnp.abs(v)))


def grid_of(size):
    row = lax.broadcasted_iota(jnp.int32, (size, size), 0)
    col = lax.broadcasted_iota(jnp.int32, (size, size), 1)
    return row, col


def lower_inverses(parts, row, col):
    size = parts[0].shape[0]
    joined = (row // 2 == col // 2) & (row > col)
    unit = (row == col).astype(f32)
    inverses = [unit - jnp.where(joined, part, 0.0) for part in parts]
    width = 2
    while width < size:
        joined = (row // (2 * width) == col // (2 * width)) & (row // width > col // width)
        corners = [jnp.where(joined, part, 0.0) for part in parts]
        moved = [mm(corner, inverse) for corner, inverse in zip(corners, inverses)]
        steps = [mm(inverse, move) for inverse, move in zip(inverses, moved)]
        inverses = [inverse - change for inverse, change in zip(inverses, steps)]
        width *= 2
    return inverses


def fill_taps(ext, slot, proj, pos, prev, first, qkv):
    rows = proj.shape[2]
    ext[slot, 8 : 8 + rows, :] = proj[*pos, :, :qkv].astype(f32)
    tail = proj[*prev, rows - 16 :, :qkv].astype(f32)[8:]
    ext[slot, 0:8, :] = jnp.where(first, 0.0, tail)


def conv_rows(ext, m, conv, rows):
    taps = conv.shape[0]
    total = conv[0:1, :] * ext[m, 9 - taps : 9 - taps + rows, :]
    for j in range(1, taps):
        total = total + conv[j : j + 1, :] * ext[m, 9 - taps + j : 9 - taps + j + rows, :]
    return total


def forward_kernel(
    local_heads,
    blocks,
    perm,
    proj,
    conv,
    rates,
    gain,
    mixed,
    heads_out,
    qkv_out,
    gates,
    inv_t,
    weighted_t,
    fresh,
    states,
    ext,
    targets,
    weighted,
    scores,
    keys_t,
    state,
):
    _, micro, rows, _ = proj.shape
    cols = local_heads * LANES
    qkv = 3 * cols
    row, col = grid_of(rows)
    upto = (row >= col).astype(f32)
    lane = lax.broadcasted_iota(jnp.int32, (rows, LANES), 1)
    scale = float(LANES) ** -0.5

    def prepare(i, carry):
        work = []
        for part in range(PAIR):
            b = i * PAIR + part
            for m in range(micro):
                slot = part * micro + m
                pos, prev = (perm[b], m), (perm[jnp.maximum(b - 1, 0)], m)
                fill_taps(ext, slot, proj, pos, prev, b == 0, qkv)
                conv_out = conv_rows(ext, slot, conv, rows)
                act = conv_out * jax.nn.sigmoid(conv_out)
                logits = proj[*pos, :, 4 * cols :].astype(f32)
                decay = -rates[...] * softplus(logits)
                strength = jax.nn.sigmoid(logits)
                total = mm_exact(upto, decay)
                total_t = total.T
                gates[b, m] = jnp.where(lane < local_heads, total, strength)
                growth = jnp.exp(total)
                fade = jnp.exp(total[rows - 1 : rows, :] - total)
                for h in range(local_heads):
                    raw_q = act[:, h * LANES : (h + 1) * LANES]
                    raw_k = act[:, cols + h * LANES : cols + (h + 1) * LANES]
                    q = raw_q * (
                        lax.rsqrt(jnp.sum(raw_q * raw_q, axis=1, keepdims=True) + eps_key) * scale
                    )
                    k = raw_k * lax.rsqrt(jnp.sum(raw_k * raw_k, axis=1, keepdims=True) + eps_key)
                    q = q.astype(low)
                    k = k.astype(low)
                    v = act[:, 2 * cols + h * LANES : 2 * cols + (h + 1) * LANES].astype(low)
                    qkv_out[b, m, :, h * LANES : (h + 1) * LANES] = q
                    qkv_out[b, m, :, cols + h * LANES : cols + (h + 1) * LANES] = k
                    qkv_out[b, m, :, 2 * cols + h * LANES : 2 * cols + (h + 1) * LANES] = v
                    beta = strength[:, local_heads + h : local_heads + h + 1]
                    spread = jnp.exp(
                        jnp.minimum(total[:, h : h + 1] - total_t[h : h + 1, :], 0.0)
                    )
                    work.append(
                        (b, m * local_heads + h, q, k, v, beta, spread, growth[:, h : h + 1], fade[:, h : h + 1])
                    )
        same = [mm_nt(k, k) for _, _, _, k, *_ in work]
        cross = [mm_nt(q, k) for _, _, q, k, *_ in work]
        parts = [
            jnp.where(row > col, item[6] * item[5] * dots, 0.0) for item, dots in zip(work, same)
        ]
        inverses = lower_inverses(parts, row, col)
        keyed = [fine(inv, item[3].astype(f32) * (item[5] * item[7])) for inv, item in zip(inverses, work)]
        valued = [fine(inv, item[4].astype(f32) * item[5]) for inv, item in zip(inverses, work)]
        for n, (b, p, q, k, v, beta, spread, grow, shrink) in enumerate(work):
            inv_t[b, p] = inverses[n].T
            weighted[b, p] = keyed[n]
            weighted_t[b, p] = keyed[n].T
            targets[b, p] = valued[n]
            scores[b, p] = upto * spread * cross[n]
            keys_t[b, p] = (k.astype(f32) * shrink).T
        return carry

    lax.fori_loop(0, blocks // PAIR, prepare, 0)
    state[...] = jnp.zeros_like(state)

    def step(b, carry):
        growth = [jnp.exp(gates[b, m]) for m in range(micro)]
        chains = [(m, h, m * local_heads + h) for m in range(micro) for h in range(local_heads)]
        now = [state[p] for _, _, p in chains]
        now_halves = [halves(v) for v in now]
        new = [
            targets[b, p] - fine(weighted[b, p], parts) for (_, _, p), parts in zip(chains, now_halves)
        ]
        new_halves = [halves(v) for v in new]
        moved = [fine(keys_t[b, p], parts) for (_, _, p), parts in zip(chains, new_halves)]
        for (m, h, p), old, fed in zip(chains, now, moved):
            states[b, p] = old
            state[p] = growth[m][rows - 1 : rows, h : h + 1] * old + fed
        outs = []
        for (m, h, p), fill, parts in zip(chains, new_halves, now_halves):
            q = qkv_out[b, m, :, h * LANES : (h + 1) * LANES].astype(f32)
            outs.append(fine(q * growth[m][:, h : h + 1], parts) + fine(scores[b, p], fill))
        for (m, h, p), fill, out in zip(chains, new, outs):
            fresh[b, p] = fill
            out = out.astype(low)
            heads_out[b, m, :, h * LANES : (h + 1) * LANES] = out
            out = out.astype(f32)
            pos = (perm[b], m)
            gate = proj[*pos, :, 3 * cols + h * LANES : 3 * cols + (h + 1) * LANES].astype(f32)
            normed = out * lax.rsqrt(jnp.mean(out * out, axis=1, keepdims=True) + eps_norm) * gain[...]
            done = (normed * (gate * jax.nn.sigmoid(gate))).astype(low)
            mixed[*pos, :, h * LANES : (h + 1) * LANES] = done
        return carry

    lax.fori_loop(0, blocks, step, 0)


def backward_kernel(
    local_heads,
    blocks,
    perm,
    grad_mixed,
    proj,
    conv,
    rates,
    gain,
    heads_out,
    qkv_in,
    gates,
    inv_t,
    weighted_t,
    fresh,
    states,
    grad_proj,
    grad_conv,
    grad_rates,
    grad_gain,
    ext,
    dext,
    ahead,
    conv_sum,
    grad_out,
    value_part,
    state_part,
    grad_fresh,
    grad_states,
    grad_state,
):
    _, micro, rows, _ = proj.shape
    cols = local_heads * LANES
    qkv = 3 * cols
    taps = conv.shape[0]
    row, col = grid_of(rows)
    lane = lax.broadcasted_iota(jnp.int32, (rows, LANES), 1)
    last = lax.broadcasted_iota(jnp.int32, (rows, 1), 0) == rows - 1
    scale = float(LANES) ** -0.5
    upto_t = (col >= row).astype(f32)
    grad_gain[...] = jnp.zeros_like(grad_gain)
    grad_rates[...] = jnp.zeros_like(grad_rates)
    conv_sum[...] = jnp.zeros_like(conv_sum)
    ahead[...] = jnp.zeros_like(ahead)
    grad_state[...] = jnp.zeros_like(grad_state)

    def prepare(b, carry):
        work = []
        for m in range(micro):
            pos = (perm[b], m)
            total = gates[b, m]
            growth = jnp.exp(total)
            total_t = total.T
            for h in range(local_heads):
                p = m * local_heads + h
                here = slice(h * LANES, (h + 1) * LANES)
                out = heads_out[b, m, :, here].astype(f32)
                gate = proj[*pos, :, 3 * cols + h * LANES : 3 * cols + (h + 1) * LANES].astype(f32)
                dmixed = grad_mixed[*pos, :, here].astype(f32)
                root = lax.rsqrt(jnp.mean(out * out, axis=1, keepdims=True) + eps_norm)
                unit = out * root
                sig = jax.nn.sigmoid(gate)
                dnormed = dmixed * (gate * sig)
                dgate = dmixed * (unit * gain[...]) * (sig * (1.0 + gate * (1.0 - sig)))
                at = slice(3 * cols + h * LANES, 3 * cols + (h + 1) * LANES)
                grad_proj[*pos, :, at] = dgate.astype(low)
                grad_gain[...] += jnp.sum(dnormed * unit, axis=0, keepdims=True)
                dunit = dnormed * gain[...]
                dout = root * (dunit - unit * jnp.mean(unit * dunit, axis=1, keepdims=True))
                dout = dout.astype(low)
                grad_out[b, p] = dout.astype(grad_out.dtype)
                q = qkv_in[b, m, :, here]
                k = qkv_in[b, m, :, cols + h * LANES : cols + (h + 1) * LANES]
                spread_t = jnp.exp(jnp.minimum(total_t[h : h + 1, :] - total[:, h : h + 1], 0.0))
                grown_t = (q.astype(f32) * growth[:, h : h + 1]).T
                work.append((p, q, k, dout, upto_t * spread_t, grown_t))
        dots = [mm_nt(k, q) for _, q, k, *_ in work]
        parts = [fine(spread * dot, dout) for (_, _, _, dout, spread, _), dot in zip(work, dots)]
        fed = [fine(grown_t, dout) for _, _, _, dout, _, grown_t in work]
        for (p, *_), part, feed in zip(work, parts, fed):
            value_part[b, p] = part
            state_part[b, p] = feed
        return carry

    lax.fori_loop(0, blocks, prepare, 0)

    def step(i, carry):
        b = blocks - 1 - i
        chains = [(m, h, m * local_heads + h) for m in range(micro) for h in range(local_heads)]
        total = [gates[b, m] for m in range(micro)]
        fade = [jnp.exp(v[rows - 1 : rows, :] - v) for v in total]
        later = [grad_state[p] for _, _, p in chains]
        dnew = []
        for (m, h, p), grad in zip(chains, later):
            k = qkv_in[b, m, :, cols + h * LANES : cols + (h + 1) * LANES].astype(f32)
            dnew.append(value_part[b, p] + fine(k * fade[m][:, h : h + 1], grad))
        moved = [fine(weighted_t[b, p], grad) for (_, _, p), grad in zip(chains, dnew)]
        for (m, h, p), grad, fill, move in zip(chains, later, dnew, moved):
            grad_states[b, p] = grad
            grad_fresh[b, p] = fill
            carried = jnp.exp(total[m][rows - 1 : rows, h : h + 1])
            grad_state[p] = state_part[b, p] + carried * grad - move
        return carry

    lax.fori_loop(0, blocks, step, 0)

    def finish(i, carry):
        b = blocks - 1 - i
        work = []
        for m in range(micro):
            total = gates[b, m]
            total_t = total.T
            growth = jnp.exp(total)
            fade = jnp.exp(total[rows - 1 : rows, :] - total)
            for h in range(local_heads):
                p = m * local_heads + h
                q = qkv_in[b, m, :, h * LANES : (h + 1) * LANES]
                k = qkv_in[b, m, :, cols + h * LANES : cols + (h + 1) * LANES]
                v = qkv_in[b, m, :, 2 * cols + h * LANES : 2 * cols + (h + 1) * LANES]
                beta = total[:, local_heads + h : local_heads + h + 1]
                spread = jnp.exp(jnp.minimum(total[:, h : h + 1] - total_t[h : h + 1, :], 0.0))
                work.append(
                    (p, q, k, v, beta, spread, growth[:, h : h + 1], fade[:, h : h + 1], growth[rows - 1 : rows, h : h + 1])
                )
        number = range(len(work))
        queries = [item[1] for item in work]
        keys = [item[2] for item in work]
        douts = [grad_out[b, item[0]].astype(low) for item in work]
        news = [halves(fresh[b, item[0]]) for item in work]
        nows = [halves(states[b, item[0]]) for item in work]
        laters = [halves(grad_states[b, item[0]]) for item in work]
        dright = [fine(inv_t[b, item[0]], grad_fresh[b, item[0]]) for item in work]
        dgrown = [fine_nt(douts[n], nows[n]) for n in number]
        dshrunk = [fine_nt(news[n], laters[n]) for n in number]
        dots = [mm_nt(queries[n], keys[n]) for n in number]
        same = [mm_nt(keys[n], keys[n]) for n in number]
        dscores = [fine_nt(douts[n], news[n]) for n in number]
        dright_halves = [halves(v) for v in dright]
        dweighted = [-fine_nt(dright_halves[n], nows[n]) for n in number]
        dbelow = [fine_nt(dright_halves[n], news[n]) for n in number]
        keyed, moved = [], []
        for n in number:
            beta, spread = work[n][4], work[n][5]
            dscores[n] = dscores[n] * jnp.where(row >= col, spread, 0.0)
            dbelow[n] = dbelow[n] * jnp.where(row > col, -spread, 0.0)
            keyed.append(dbelow[n] * same[n])
            moved.append(dscores[n] * dots[n] + keyed[n] * beta)
            dbelow[n] = dbelow[n] * beta
        dq = [fine(dscores[n], keys[n]) for n in number]
        dk = [fine(dscores[n].T, queries[n]) for n in number]
        dk_same = [fine(dbelow[n] + dbelow[n].T, keys[n]) for n in number]
        for m in range(micro):
            pos, prev = (perm[b], m), (perm[jnp.maximum(b - 1, 0)], m)
            fill_taps(ext, m, proj, pos, prev, b == 0, qkv)
            conv_out = conv_rows(ext, m, conv, rows)
            sig = jax.nn.sigmoid(conv_out)
            act = conv_out * sig
            slope = sig * (1.0 + conv_out * (1.0 - sig))
            dtotal = jnp.zeros((rows, LANES), f32)
            dstrength = jnp.zeros((rows, LANES), f32)
            for h in range(local_heads):
                n = m * local_heads + h
                p, q, k, v, beta, spread, grow, shrink, carried = work[n]
                q32, k32, v32 = q.astype(f32), k.astype(f32), v.astype(f32)
                dquery = grow * dgrown[n] + dq[n]
                dkey = (beta * grow) * dweighted[n] + shrink * dshrunk[n] + dk[n] + dk_same[n]
                dvalue = beta * dright[n]
                weighed = dweighted[n] * k32 * grow
                shrunk = dshrunk[n] * k32 * shrink
                dstr = jnp.sum(dright[n] * v32 + weighed, axis=1, keepdims=True) + jnp.sum(
                    keyed[n], axis=1, keepdims=True
                )
                dtot = jnp.sum(
                    dgrown[n] * q32 * grow + weighed * beta - shrunk, axis=1, keepdims=True
                ) + jnp.sum(moved[n] - moved[n].T, axis=1, keepdims=True)
                end = jnp.sum(shrunk) + jnp.sum(carried * (states[b, p] * grad_states[b, p]))
                dtot = dtot + jnp.where(last, end, 0.0)
                dtotal = dtotal + jnp.where(lane == h, dtot, 0.0)
                dstrength = dstrength + jnp.where(lane == local_heads + h, dstr, 0.0)
                for part, grad in ((0, dquery), (1, dkey), (2, dvalue)):
                    at = part * cols + h * LANES
                    grad = grad.astype(low).astype(f32)
                    if part == 0:
                        grad = grad * scale
                    if part < 2:
                        raw = act[:, at : at + LANES]
                        root = lax.rsqrt(jnp.sum(raw * raw, axis=1, keepdims=True) + eps_key)
                        unit = raw * root
                        grad = root * (grad - unit * jnp.sum(unit * grad, axis=1, keepdims=True))
                    dext[m, 0:rows, at : at + LANES] = grad * slope[:, at : at + LANES]
            dext[m, rows : rows + 8, :] = ahead[m]
            dconv = dext[m, 0:rows, :]
            ahead[m] = dconv[0:8, :]
            du = conv[taps - 1 : taps, :] * dconv
            for j in range(taps - 1):
                du = du + conv[j : j + 1, :] * dext[m, taps - 1 - j : taps - 1 - j + rows, :]
            grad_proj[*pos, :, :qkv] = du.astype(low)
            for j in range(taps):
                term = dconv * ext[m, 9 - taps + j : 9 - taps + j + rows, :]
                conv_sum[j] += jnp.sum(term.reshape(rows // 8, 8, qkv), axis=0)
            logits = proj[*pos, :, 4 * cols :].astype(f32)
            ddecay = mm_exact(upto_t, dtotal)
            strength = gates[b, m]
            dlogit = jnp.where(
                lane < local_heads,
                -rates[...] * jax.nn.sigmoid(logits) * ddecay,
                strength * (1.0 - strength) * dstrength,
            )
            dlogit = jnp.where(lane < 2 * local_heads, dlogit, 0.0).astype(low)
            grad_proj[*pos, :, 4 * cols :] = dlogit
            grad_rates[...] -= jnp.sum(softplus(logits) * ddecay, axis=0, keepdims=True)
        return carry

    lax.fori_loop(0, blocks, finish, 0)
    for j in range(taps):
        grad_conv[j : j + 1, :] = jnp.sum(conv_sum[j], axis=0, keepdims=True)


def in_vmem():
    return pl.BlockSpec(memory_space=pltpu.VMEM)


def heads_forward(perm, proj, conv, rates, gain, local_heads):
    blocks, micro, rows, _ = proj.shape
    cols = local_heads * LANES
    chains = micro * local_heads

    def shape(dims, kind):
        return jax.ShapeDtypeStruct(dims, kind)

    return pl.pallas_call(
        partial(forward_kernel, local_heads, perm.shape[0]),
        out_shape=(
            shape((blocks, micro, rows, cols), low),
            shape((blocks, micro, rows, cols), low),
            shape((blocks, micro, rows, 3 * cols), low),
            shape((blocks, micro, rows, LANES), f32),
            shape((blocks, chains, rows, rows), f32),
            shape((blocks, chains, LANES, rows), f32),
            shape((blocks, chains, rows, LANES), f32),
            shape((blocks, chains, LANES, LANES), f32),
        ),
        in_specs=[pl.BlockSpec(memory_space=pltpu.SMEM)] + [in_vmem()] * 4,
        out_specs=(in_vmem(),) * 8,
        scratch_shapes=[
            pltpu.VMEM((PAIR * micro, rows + 8, 3 * cols), f32),
            pltpu.VMEM((blocks, chains, rows, LANES), f32),
            pltpu.VMEM((blocks, chains, rows, LANES), f32),
            pltpu.VMEM((blocks, chains, rows, rows), f32),
            pltpu.VMEM((blocks, chains, LANES, rows), f32),
            pltpu.VMEM((chains, LANES, LANES), f32),
        ],
        compiler_params=pltpu.CompilerParams(vmem_limit_bytes=50 * 1024 * 1024),
        name="heads_forward",
    )(perm, proj, conv, rates, gain)


def heads_backward(perm, grad_mixed, proj, conv, rates, gain, kept, local_heads):
    blocks, micro, rows, wide = proj.shape
    cols = local_heads * LANES
    chains = micro * local_heads
    taps = conv.shape[0]

    def shape(dims, kind):
        return jax.ShapeDtypeStruct(dims, kind)

    return pl.pallas_call(
        partial(backward_kernel, local_heads, perm.shape[0]),
        out_shape=(
            shape((blocks, micro, rows, wide), low),
            shape((taps, 3 * cols), f32),
            shape((1, LANES), f32),
            shape((1, LANES), f32),
        ),
        in_specs=[pl.BlockSpec(memory_space=pltpu.SMEM)] + [in_vmem()] * 12,
        out_specs=(in_vmem(),) * 4,
        scratch_shapes=[
            pltpu.VMEM((micro, rows + 8, 3 * cols), f32),
            pltpu.VMEM((micro, rows + 8, 3 * cols), f32),
            pltpu.VMEM((micro, 8, 3 * cols), f32),
            pltpu.VMEM((taps, 8, 3 * cols), f32),
            pltpu.VMEM((blocks, chains, rows, LANES), f32),
            pltpu.VMEM((blocks, chains, rows, LANES), f32),
            pltpu.VMEM((blocks, chains, LANES, LANES), f32),
            pltpu.VMEM((blocks, chains, rows, LANES), f32),
            pltpu.VMEM((blocks, chains, LANES, LANES), f32),
            pltpu.VMEM((chains, LANES, LANES), f32),
        ],
        compiler_params=pltpu.CompilerParams(vmem_limit_bytes=50 * 1024 * 1024),
        name="heads_backward",
    )(perm, grad_mixed, proj, conv, rates, gain, *kept)


both = ("dp", "seq")


def swap(value, axis, bit):
    return lax.ppermute(value, axis, [(i, i ^ bit) for i in range(lax.axis_size(axis))])


def tie(*values):
    return lax.optimization_barrier(values)


def gather_places():
    peers = lax.axis_size("seq")
    place = jnp.arange(peers, dtype=jnp.int32)
    if peers != 8:
        return place
    place = place ^ lax.axis_index("seq").astype(jnp.int32)
    return place // 2 + 4 * (place % 2)


def gather_seq(rows_in):
    if lax.axis_size("seq") != 8:
        return lax.all_gather(rows_in, "seq", axis=0, tiled=True)
    half = rows_in.shape[0] // 2
    top, bottom = rows_in[:half], rows_in[half:]
    top_x, bottom_y = swap(top, "seq", 2), swap(bottom, "seq", 4)
    top_y = swap(jnp.concatenate([top, top_x]), "seq", 4)
    bottom_x = swap(jnp.concatenate([bottom, bottom_y]), "seq", 2)
    near = jnp.concatenate(
        [top, bottom, top_x, bottom_x[:half], top_y[:half], bottom_y, top_y[half:], bottom_x[half:]]
    )
    return jnp.concatenate([near, swap(near, "seq", 1)])


def scatter_seq(partial_rows, beside=None):
    peers = lax.axis_size("seq")
    if peers != 8:
        total = lax.psum_scatter(
            partial_rows.astype(low), "seq", scatter_dimension=0, tiled=True
        ).astype(f32)
        return total if beside is None else (total, beside)
    terms = partial_rows.astype(low).reshape(peers, -1, partial_rows.shape[-1])
    half = terms.shape[1] // 2
    near = terms[:4].astype(f32) + swap(terms[4:], "seq", 1).astype(f32)
    top, bottom = near[:, :half].astype(low), near[:, half:].astype(low)
    top_x = swap(top[1::2], "seq", 2)
    bottom_y = swap(bottom[2:], "seq", 4)
    top = near[0::2, :half] + top_x.astype(f32)
    bottom = near[:2, half:] + bottom_y.astype(f32)
    if beside is not None:
        top, bottom, beside = tie(top, bottom, beside)
    top_y = swap(top[1].astype(low), "seq", 4)
    bottom_x = swap(bottom[1].astype(low), "seq", 2)
    total = jnp.concatenate([top[0] + top_y.astype(f32), bottom[0] + bottom_x.astype(f32)])
    return total if beside is None else (total, beside)


def sum_all(value):
    for axis in both:
        bit = 1
        while bit < lax.axis_size(axis):
            value = value + swap(value, axis, bit)
            bit *= 2
    return value


def to_columns(pieces):
    rows_here = lax.all_to_all(pieces, "seq", split_axis=0, concat_axis=0, tiled=True)
    return rows_here.reshape(-1, pieces.shape[-1])


def gather_dp(rows_here):
    return lax.all_gather(rows_here, "dp", axis=0, tiled=True)


def sum_dp(term):
    return lax.psum_scatter(term.astype(low), "dp", scatter_dimension=0, tiled=True)


def to_owners(own):
    pieces = own.reshape(lax.axis_size("seq"), -1, own.shape[1])
    return lax.all_to_all(pieces, "seq", split_axis=0, concat_axis=0, tiled=True)


def widen(columns):
    extra = -columns.shape[-1] % LANES
    return jnp.pad(columns, [(0, 0)] * (columns.ndim - 1) + [(0, extra)])


def assemble_kernel(local_heads, pieces, whole):
    peers, _, wide = pieces.shape
    cols = (wide - LANES) // 4
    width = cols * peers
    logits = []
    for part in range(5):
        for j in range(peers):
            from_here = slice(part * cols, min((part + 1) * cols, wide))
            total = pieces[j, :, from_here].astype(f32)
            if part < 4:
                whole[:, part * width + j * cols : part * width + (j + 1) * cols] = total
            else:
                logits.append(total)
    for kind in range(2):
        here = slice(kind * local_heads, (kind + 1) * local_heads)
        for j in range(peers):
            at = 4 * width + kind * local_heads * peers + j * local_heads
            whole[:, at : at + local_heads] = logits[j][:, here]


def assemble(pieces, local_heads):
    peers, rows, wide = pieces.shape
    total = (wide - LANES) * peers + 2 * local_heads * peers
    return pl.pallas_call(
        partial(assemble_kernel, local_heads),
        out_shape=jax.ShapeDtypeStruct((rows, total), f32),
        in_specs=[in_vmem()],
        out_specs=in_vmem(),
        compiler_params=pltpu.CompilerParams(vmem_limit_bytes=30 * 1024 * 1024),
        name="assemble",
    )(pieces)


def row_pairs(inverse):
    groups, peers = lax.axis_size("dp"), lax.axis_size("seq")
    pairs = [(j * groups + d, d * peers + j) for d in range(groups) for j in range(peers)]
    return [(b, a) for a, b in pairs] if inverse else pairs


def dot32(left, right):
    return jnp.dot(left, right, preferred_element_type=f32)


def dot_t(left, right):
    return lax.dot_general(left, right, (((1,), (1,)), ((), ())), preferred_element_type=f32)


def t_dot(left, right):
    return lax.dot_general(left, right, (((0,), (0,)), ((), ())), preferred_element_type=f32)


def shards(
    tokens,
    lengths,
    norm_gain,
    mix_weight,
    conv_weight,
    decay_rate,
    out_gain,
    out_weight,
    mlp_gain,
    mlp_in_weight,
    mlp_out_weight,
    grad_out,
):
    micro, seq_rows, width = tokens.shape
    heads = decay_rate.shape[0]
    groups = lax.axis_size("dp")
    peers = lax.axis_size("seq")
    here = lax.axis_index("seq")
    local_heads = heads // peers
    taps = conv_weight.shape[0]
    units = mlp_out_weight.shape[1]
    own_units = units // peers
    own_rows = mix_weight.shape[0]
    cols = width // peers
    logit_cols = 2 * local_heads

    positions = here * seq_rows + lax.broadcasted_iota(jnp.int32, (micro, seq_rows), 1)
    valid = (positions < lengths[:, None]).astype(f32).reshape(-1, 1)
    inputs = tokens.reshape(-1, width).astype(f32)

    out_rows = lax.ppermute(out_weight, both, row_pairs(False))
    main = mix_weight[:, : 4 * width].reshape(own_rows, 4, peers, cols).transpose(2, 0, 1, 3)
    logits = mix_weight[:, 4 * width :].reshape(own_rows, 2, peers, local_heads)
    logits = logits.transpose(2, 0, 1, 3).reshape(peers, own_rows, logit_cols)
    mix_rows = to_columns(
        jnp.concatenate([main.reshape(peers, own_rows, 4 * cols), widen(logits)], axis=2)
    )
    wide_cols = mix_rows.shape[1]
    normed, norm_back = jax.vjp(rms_scale, inputs, norm_gain)
    mix_rows, normed_low, mlp_in_rows, mlp_out_rows = tie(
        mix_rows, normed.astype(low), mlp_in_weight, mlp_out_weight
    )
    mixer_here = gather_dp(
        jnp.concatenate([mix_rows, out_rows.reshape(mix_rows.shape[0], -1)], axis=1)
    )
    normed_all = gather_seq(normed_low)
    gate_up = mlp_in_rows.reshape(own_rows, 2, peers, own_units).transpose(2, 0, 1, 3)
    down = mlp_out_rows.reshape(own_rows, peers, 1, own_units).transpose(1, 0, 2, 3)
    mlp_pieces = jnp.concatenate([gate_up, down], axis=2).reshape(peers, own_rows, 3 * own_units)
    mlp_rows = to_columns(mlp_pieces)
    cotangent = valid * grad_out.reshape(-1, width).astype(f32)
    mixer_here, mlp_rows, normed_all, cot_low = tie(
        mixer_here, mlp_rows, normed_all, cotangent.astype(low)
    )
    in_here = gather_dp(mlp_rows[:, : 2 * own_units])
    down_here = gather_dp(mlp_rows[:, 2 * own_units :])
    mix_here = mixer_here[:, :wide_cols]
    out_here = mixer_here[:, wide_cols:].reshape(-1, width)

    projected = dot32(normed_all, mix_here).astype(low).reshape(peers, micro, seq_rows, -1)
    conv_here = lax.dynamic_index_in_dim(
        conv_weight.reshape(taps, 3, peers, cols), here, 2, keepdims=False
    ).reshape(taps, 3 * cols)
    rates_here = lax.dynamic_slice_in_dim(decay_rate, here * local_heads, local_heads)
    rate_lanes = jnp.pad(rates_here, (0, LANES - local_heads)).reshape(1, LANES)
    gain_row = out_gain.reshape(1, LANES)
    places = gather_places()
    mixed, *kept = heads_forward(
        places, projected, conv_here, rate_lanes, gain_row, local_heads
    )
    mixed, cot_low = tie(mixed, cot_low)
    mixed_low = mixed.reshape(-1, cols)
    branch, in_here = scatter_seq(dot32(mixed_low, out_here), in_here)
    hidden = inputs + branch

    second, second_back = jax.vjp(rms_scale, hidden, mlp_gain)
    second_all = gather_seq(second.astype(low))
    cot_all = gather_seq(cot_low)
    gate_up = dot32(second_all, in_here).astype(low)
    activated, swiglu_back = jax.vjp(swiglu, gate_up.astype(f32))
    activated_low = activated.astype(low)
    activated_low, down_here = tie(activated_low, down_here)
    grad_down_term = t_dot(cot_all, activated_low).astype(low)
    cot_all, grad_down_term = tie(cot_all, grad_down_term)
    (grad_gate_up,) = swiglu_back(dot32(cot_all, down_here))
    grad_gate_low = grad_gate_up.astype(low)
    grad_second = scatter_seq(dot_t(grad_gate_low, in_here))
    grad_hidden_norm, grad_mlp_gain = second_back(grad_second)
    grad_hidden = cotangent + grad_hidden_norm
    branch_all = gather_seq(grad_hidden.astype(low))
    grad_down = sum_dp(grad_down_term)
    grad_in = sum_dp(t_dot(second_all, grad_gate_low))

    grad_mixed = dot_t(branch_all, out_here).reshape(peers, micro, seq_rows, cols)
    grad_mixed, grad_down = tie(grad_mixed, grad_down)
    grad_out_term = t_dot(mixed_low, branch_all).astype(low)
    grad_projected, grad_conv, rate_sums, gain_sums = (
        heads_backward(
            places,
            grad_mixed,
            projected,
            conv_here,
            rate_lanes,
            gain_row,
            kept,
            local_heads,
        )
    )
    grad_projected = grad_projected.reshape(-1, wide_cols)
    grad_mix_term = t_dot(normed_all, grad_projected).astype(low)
    grad_mix_term, grad_projected, activated_low = tie(
        grad_mix_term, grad_projected, activated_low
    )
    mixer_own = sum_dp(
        jnp.concatenate([grad_mix_term, grad_out_term.reshape(width, -1)], axis=1)
    )
    grad_mix = to_owners(mixer_own[:, :wide_cols])
    grad_out_own = lax.ppermute(
        mixer_own[:, wide_cols:].reshape(own_rows, width), both, row_pairs(True)
    )
    grad_normed = scatter_seq(dot_t(grad_projected, mix_here))
    grad_inputs_norm, grad_norm_gain = norm_back(grad_normed)
    grad_tokens = grad_hidden + grad_inputs_norm
    feed_out = scatter_seq(dot_t(activated_low, down_here))
    result = (valid * (hidden + feed_out)).astype(low)

    conv_terms = lax.dynamic_update_slice(
        jnp.zeros((taps, 3, peers, cols), f32),
        grad_conv.reshape(taps, 3, 1, cols),
        (0, 0, here, 0),
    )
    rate_terms = lax.dynamic_update_slice(
        jnp.zeros((LANES,), f32), rate_sums[0, :local_heads], (here * local_heads,)
    )
    sizes = [width, width, LANES, LANES, taps * 3 * width]
    summed = sum_all(
        jnp.concatenate(
            [
                grad_norm_gain,
                grad_mlp_gain,
                gain_sums[0],
                rate_terms,
                conv_terms.reshape(-1),
            ]
        ).reshape(-1, LANES)
    ).reshape(-1)
    ends = [sum(sizes[: i + 1]) for i in range(len(sizes))]
    sums = [summed[end - size : end] for end, size in zip(ends, sizes)]
    grad_in = to_owners(grad_in).reshape(peers, own_rows, 2, own_units).transpose(1, 2, 0, 3)
    grad_down = to_owners(grad_down).transpose(1, 0, 2)
    return (
        result.reshape(tokens.shape),
        grad_tokens.reshape(tokens.shape),
        sums[0],
        assemble(grad_mix, local_heads),
        sums[4].reshape(taps, 3 * width),
        sums[3][:heads],
        sums[2],
        grad_out_own.astype(f32),
        sums[1],
        grad_in.reshape(own_rows, 2 * units).astype(f32),
        grad_down.reshape(own_rows, units).astype(f32),
    )


def solution(mesh):
    in_specs = (
        P("dp", "seq", None),
        P("dp"),
        P(),
        P(("dp", "seq"), None),
        P(),
        P(),
        P(),
        P(("dp", "seq"), None),
        P(),
        P(("dp", "seq"), None),
        P(("dp", "seq"), None),
        P("dp", "seq", None),
    )
    out_specs = (
        P("dp", "seq", None),
        P("dp", "seq", None),
        P(),
        P(("dp", "seq"), None),
        P(),
        P(),
        P(),
        P(("dp", "seq"), None),
        P(),
        P(("dp", "seq"), None),
        P(("dp", "seq"), None),
    )
    return jax.shard_map(shards, mesh=mesh, in_specs=in_specs, out_specs=out_specs, check_vma=False)
```

```python
from functools import partial

import jax
import jax.numpy as jnp
from jax import lax
from jax.experimental import pallas as pl
from jax.experimental.pallas import tpu as pltpu
from jax.sharding import PartitionSpec as P

eps_norm = 1e-05
eps_key = 1e-06
LANES = 128
PAIR = 2
f32 = jnp.float32
low = jnp.bfloat16


def rms_scale(rows_in, gain):
    return (
        rows_in * lax.rsqrt(jnp.mean(rows_in * rows_in, axis=-1, keepdims=True) + eps_norm) * gain
    )


def swiglu(gate_up):
    hidden_units = gate_up.shape[-1] // 2
    return jax.nn.silu(gate_up[..., :hidden_units]) * gate_up[..., hidden_units:]


def mm(left, right):
    return jnp.dot(left.astype(low), right.astype(low), preferred_element_type=f32)


def mm_nt(left, right):
    return lax.dot_general(
        left.astype(low), right.astype(low), (((1,), (1,)), ((), ())), preferred_element_type=f32
    )


def halves(v):
    if isinstance(v, tuple):
        return v
    if v.dtype == low:
        return (v,)
    top = v.astype(low)
    return top, (v - top.astype(f32)).astype(low)


def dot_fine(left, right, dims):
    left, right = halves(left), halves(right)
    total = None
    for i, a in enumerate(left):
        for j, b in enumerate(right):
            if i + j < 2:
                term = lax.dot_general(a, b, (dims, ((), ())), preferred_element_type=f32)
                total = term if total is None else total + term
    return total


def fine(left, right):
    return dot_fine(left, right, ((1,), (0,)))


def fine_nt(left, right):
    return dot_fine(left, right, ((1,), (1,)))


def mm_exact(left, right):
    return jnp.dot(left, right, precision=lax.Precision.HIGHEST, preferred_element_type=f32)


def softplus(v):
    return jnp.maximum(v, 0.0) + jnp.log1p(jnp.exp(-jnp.abs(v)))


def grid_of(size):
    row = lax.broadcasted_iota(jnp.int32, (size, size), 0)
    col = lax.broadcasted_iota(jnp.int32, (size, size), 1)
    return row, col


def lower_inverses(parts, row, col):
    size = parts[0].shape[0]
    joined = (row // 2 == col // 2) & (row > col)
    unit = (row == col).astype(f32)
    inverses = [unit - jnp.where(joined, part, 0.0) for part in parts]
    width = 2
    while width < size:
        joined = (row // (2 * width) == col // (2 * width)) & (row // width > col // width)
        corners = [jnp.where(joined, part, 0.0) for part in parts]
        moved = [mm(corner, inverse) for corner, inverse in zip(corners, inverses)]
        steps = [mm(inverse, move) for inverse, move in zip(inverses, moved)]
        inverses = [inverse - change for inverse, change in zip(inverses, steps)]
        width *= 2
    return inverses


def fill_taps(ext, slot, proj, pos, prev, first, qkv):
    rows = proj.shape[2]
    ext[slot, 8 : 8 + rows, :] = proj[*pos, :, :qkv].astype(f32)
    tail = proj[*prev, rows - 16 :, :qkv].astype(f32)[8:]
    ext[slot, 0:8, :] = jnp.where(first, 0.0, tail)


def conv_rows(ext, m, conv, rows):
    taps = conv.shape[0]
    total = conv[0:1, :] * ext[m, 9 - taps : 9 - taps + rows, :]
    for j in range(1, taps):
        total = total + conv[j : j + 1, :] * ext[m, 9 - taps + j : 9 - taps + j + rows, :]
    return total


def forward_kernel(
    local_heads,
    blocks,
    perm,
    proj,
    conv,
    rates,
    gain,
    mixed,
    heads_out,
    qkv_out,
    gates,
    inv_t,
    weighted_t,
    fresh,
    states,
    ext,
    targets,
    weighted,
    scores,
    keys_t,
    state,
):
    _, micro, rows, _ = proj.shape
    cols = local_heads * LANES
    qkv = 3 * cols
    row, col = grid_of(rows)
    upto = (row >= col).astype(f32)
    lane = lax.broadcasted_iota(jnp.int32, (rows, LANES), 1)
    scale = float(LANES) ** -0.5

    def prepare(i, carry):
        work = []
        for part in range(PAIR):
            b = i * PAIR + part
            for m in range(micro):
                slot = part * micro + m
                pos, prev = (perm[b], m), (perm[jnp.maximum(b - 1, 0)], m)
                fill_taps(ext, slot, proj, pos, prev, b == 0, qkv)
                conv_out = conv_rows(ext, slot, conv, rows)
                act = conv_out * jax.nn.sigmoid(conv_out)
                logits = proj[*pos, :, 4 * cols :].astype(f32)
                decay = -rates[...] * softplus(logits)
                strength = jax.nn.sigmoid(logits)
                total = mm_exact(upto, decay)
                total_t = total.T
                gates[b, m] = jnp.where(lane < local_heads, total, strength)
                growth = jnp.exp(total)
                fade = jnp.exp(total[rows - 1 : rows, :] - total)
                for h in range(local_heads):
                    raw_q = act[:, h * LANES : (h + 1) * LANES]
                    raw_k = act[:, cols + h * LANES : cols + (h + 1) * LANES]
                    q = raw_q * (
                        lax.rsqrt(jnp.sum(raw_q * raw_q, axis=1, keepdims=True) + eps_key) * scale
                    )
                    k = raw_k * lax.rsqrt(jnp.sum(raw_k * raw_k, axis=1, keepdims=True) + eps_key)
                    q = q.astype(low)
                    k = k.astype(low)
                    v = act[:, 2 * cols + h * LANES : 2 * cols + (h + 1) * LANES].astype(low)
                    qkv_out[b, m, :, h * LANES : (h + 1) * LANES] = q
                    qkv_out[b, m, :, cols + h * LANES : cols + (h + 1) * LANES] = k
                    qkv_out[b, m, :, 2 * cols + h * LANES : 2 * cols + (h + 1) * LANES] = v
                    beta = strength[:, local_heads + h : local_heads + h + 1]
                    spread = jnp.exp(
                        jnp.minimum(total[:, h : h + 1] - total_t[h : h + 1, :], 0.0)
                    )
                    work.append(
                        (b, m * local_heads + h, q, k, v, beta, spread, growth[:, h : h + 1], fade[:, h : h + 1])
                    )
        same = [mm_nt(k, k) for _, _, _, k, *_ in work]
        cross = [mm_nt(q, k) for _, _, q, k, *_ in work]
        parts = [
            jnp.where(row > col, item[6] * item[5] * dots, 0.0) for item, dots in zip(work, same)
        ]
        inverses = lower_inverses(parts, row, col)
        keyed = [fine(inv, item[3].astype(f32) * (item[5] * item[7])) for inv, item in zip(inverses, work)]
        valued = [fine(inv, item[4].astype(f32) * item[5]) for inv, item in zip(inverses, work)]
        for n, (b, p, q, k, v, beta, spread, grow, shrink) in enumerate(work):
            inv_t[b, p] = inverses[n].T
            weighted[b, p] = keyed[n]
            weighted_t[b, p] = keyed[n].T
            targets[b, p] = valued[n]
            scores[b, p] = upto * spread * cross[n]
            keys_t[b, p] = (k.astype(f32) * shrink).T
        return carry

    lax.fori_loop(0, blocks // PAIR, prepare, 0)
    state[...] = jnp.zeros_like(state)

    def step(b, carry):
        growth = [jnp.exp(gates[b, m]) for m in range(micro)]
        chains = [(m, h, m * local_heads + h) for m in range(micro) for h in range(local_heads)]
        now = [state[p] for _, _, p in chains]
        now_halves = [halves(v) for v in now]
        new = [
            targets[b, p] - fine(weighted[b, p], parts) for (_, _, p), parts in zip(chains, now_halves)
        ]
        new_halves = [halves(v) for v in new]
        moved = [fine(keys_t[b, p], parts) for (_, _, p), parts in zip(chains, new_halves)]
        for (m, h, p), old, fed in zip(chains, now, moved):
            states[b, p] = old
            state[p] = growth[m][rows - 1 : rows, h : h + 1] * old + fed
        outs = []
        for (m, h, p), fill, parts in zip(chains, new_halves, now_halves):
            q = qkv_out[b, m, :, h * LANES : (h + 1) * LANES].astype(f32)
            outs.append(fine(q * growth[m][:, h : h + 1], parts) + fine(scores[b, p], fill))
        for (m, h, p), fill, out in zip(chains, new, outs):
            fresh[b, p] = fill
            out = out.astype(low)
            heads_out[b, m, :, h * LANES : (h + 1) * LANES] = out
            out = out.astype(f32)
            pos = (perm[b], m)
            gate = proj[*pos, :, 3 * cols + h * LANES : 3 * cols + (h + 1) * LANES].astype(f32)
            normed = out * lax.rsqrt(jnp.mean(out * out, axis=1, keepdims=True) + eps_norm) * gain[...]
            done = (normed * (gate * jax.nn.sigmoid(gate))).astype(low)
            mixed[*pos, :, h * LANES : (h + 1) * LANES] = done
        return carry

    lax.fori_loop(0, blocks, step, 0)


def backward_kernel(
    local_heads,
    blocks,
    perm,
    grad_mixed,
    proj,
    conv,
    rates,
    gain,
    heads_out,
    qkv_in,
    gates,
    inv_t,
    weighted_t,
    fresh,
    states,
    grad_proj,
    grad_conv,
    grad_rates,
    grad_gain,
    ext,
    dext,
    ahead,
    conv_sum,
    grad_out,
    value_part,
    state_part,
    grad_fresh,
    grad_states,
    grad_state,
):
    _, micro, rows, _ = proj.shape
    cols = local_heads * LANES
    qkv = 3 * cols
    taps = conv.shape[0]
    row, col = grid_of(rows)
    lane = lax.broadcasted_iota(jnp.int32, (rows, LANES), 1)
    last = lax.broadcasted_iota(jnp.int32, (rows, 1), 0) == rows - 1
    scale = float(LANES) ** -0.5
    upto_t = (col >= row).astype(f32)
    grad_gain[...] = jnp.zeros_like(grad_gain)
    grad_rates[...] = jnp.zeros_like(grad_rates)
    conv_sum[...] = jnp.zeros_like(conv_sum)
    ahead[...] = jnp.zeros_like(ahead)
    grad_state[...] = jnp.zeros_like(grad_state)

    def prepare(b, carry):
        work = []
        for m in range(micro):
            pos = (perm[b], m)
            total = gates[b, m]
            growth = jnp.exp(total)
            total_t = total.T
            for h in range(local_heads):
                p = m * local_heads + h
                here = slice(h * LANES, (h + 1) * LANES)
                out = heads_out[b, m, :, here].astype(f32)
                gate = proj[*pos, :, 3 * cols + h * LANES : 3 * cols + (h + 1) * LANES].astype(f32)
                dmixed = grad_mixed[*pos, :, here].astype(f32)
                root = lax.rsqrt(jnp.mean(out * out, axis=1, keepdims=True) + eps_norm)
                unit = out * root
                sig = jax.nn.sigmoid(gate)
                dnormed = dmixed * (gate * sig)
                dgate = dmixed * (unit * gain[...]) * (sig * (1.0 + gate * (1.0 - sig)))
                at = slice(3 * cols + h * LANES, 3 * cols + (h + 1) * LANES)
                grad_proj[*pos, :, at] = dgate.astype(low)
                grad_gain[...] += jnp.sum(dnormed * unit, axis=0, keepdims=True)
                dunit = dnormed * gain[...]
                dout = root * (dunit - unit * jnp.mean(unit * dunit, axis=1, keepdims=True))
                dout = dout.astype(low)
                grad_out[b, p] = dout.astype(grad_out.dtype)
                q = qkv_in[b, m, :, here]
                k = qkv_in[b, m, :, cols + h * LANES : cols + (h + 1) * LANES]
                spread_t = jnp.exp(jnp.minimum(total_t[h : h + 1, :] - total[:, h : h + 1], 0.0))
                grown_t = (q.astype(f32) * growth[:, h : h + 1]).T
                work.append((p, q, k, dout, upto_t * spread_t, grown_t))
        dots = [mm_nt(k, q) for _, q, k, *_ in work]
        parts = [fine(spread * dot, dout) for (_, _, _, dout, spread, _), dot in zip(work, dots)]
        fed = [fine(grown_t, dout) for _, _, _, dout, _, grown_t in work]
        for (p, *_), part, feed in zip(work, parts, fed):
            value_part[b, p] = part
            state_part[b, p] = feed
        return carry

    lax.fori_loop(0, blocks, prepare, 0)

    def step(i, carry):
        b = blocks - 1 - i
        chains = [(m, h, m * local_heads + h) for m in range(micro) for h in range(local_heads)]
        total = [gates[b, m] for m in range(micro)]
        fade = [jnp.exp(v[rows - 1 : rows, :] - v) for v in total]
        later = [grad_state[p] for _, _, p in chains]
        dnew = []
        for (m, h, p), grad in zip(chains, later):
            k = qkv_in[b, m, :, cols + h * LANES : cols + (h + 1) * LANES].astype(f32)
            dnew.append(value_part[b, p] + fine(k * fade[m][:, h : h + 1], grad))
        moved = [fine(weighted_t[b, p], grad) for (_, _, p), grad in zip(chains, dnew)]
        for (m, h, p), grad, fill, move in zip(chains, later, dnew, moved):
            grad_states[b, p] = grad
            grad_fresh[b, p] = fill
            carried = jnp.exp(total[m][rows - 1 : rows, h : h + 1])
            grad_state[p] = state_part[b, p] + carried * grad - move
        return carry

    lax.fori_loop(0, blocks, step, 0)

    def finish(i, carry):
        b = blocks - 1 - i
        work = []
        for m in range(micro):
            total = gates[b, m]
            total_t = total.T
            growth = jnp.exp(total)
            fade = jnp.exp(total[rows - 1 : rows, :] - total)
            for h in range(local_heads):
                p = m * local_heads + h
                q = qkv_in[b, m, :, h * LANES : (h + 1) * LANES]
                k = qkv_in[b, m, :, cols + h * LANES : cols + (h + 1) * LANES]
                v = qkv_in[b, m, :, 2 * cols + h * LANES : 2 * cols + (h + 1) * LANES]
                beta = total[:, local_heads + h : local_heads + h + 1]
                spread = jnp.exp(jnp.minimum(total[:, h : h + 1] - total_t[h : h + 1, :], 0.0))
                work.append(
                    (p, q, k, v, beta, spread, growth[:, h : h + 1], fade[:, h : h + 1], growth[rows - 1 : rows, h : h + 1])
                )
        number = range(len(work))
        queries = [item[1] for item in work]
        keys = [item[2] for item in work]
        douts = [grad_out[b, item[0]].astype(low) for item in work]
        news = [halves(fresh[b, item[0]]) for item in work]
        nows = [halves(states[b, item[0]]) for item in work]
        laters = [halves(grad_states[b, item[0]]) for item in work]
        dright = [fine(inv_t[b, item[0]], grad_fresh[b, item[0]]) for item in work]
        dgrown = [fine_nt(douts[n], nows[n]) for n in number]
        dshrunk = [fine_nt(news[n], laters[n]) for n in number]
        dots = [mm_nt(queries[n], keys[n]) for n in number]
        same = [mm_nt(keys[n], keys[n]) for n in number]
        dscores = [fine_nt(douts[n], news[n]) for n in number]
        dright_halves = [halves(v) for v in dright]
        dweighted = [-fine_nt(dright_halves[n], nows[n]) for n in number]
        dbelow = [fine_nt(dright_halves[n], news[n]) for n in number]
        keyed, moved = [], []
        for n in number:
            beta, spread = work[n][4], work[n][5]
            dscores[n] = dscores[n] * jnp.where(row >= col, spread, 0.0)
            dbelow[n] = dbelow[n] * jnp.where(row > col, -spread, 0.0)
            keyed.append(dbelow[n] * same[n])
            moved.append(dscores[n] * dots[n] + keyed[n] * beta)
            dbelow[n] = dbelow[n] * beta
        dq = [fine(dscores[n], keys[n]) for n in number]
        dk = [fine(dscores[n].T, queries[n]) for n in number]
        dk_same = [fine(dbelow[n] + dbelow[n].T, keys[n]) for n in number]
        for m in range(micro):
            pos, prev = (perm[b], m), (perm[jnp.maximum(b - 1, 0)], m)
            fill_taps(ext, m, proj, pos, prev, b == 0, qkv)
            conv_out = conv_rows(ext, m, conv, rows)
            sig = jax.nn.sigmoid(conv_out)
            act = conv_out * sig
            slope = sig * (1.0 + conv_out * (1.0 - sig))
            dtotal = jnp.zeros((rows, LANES), f32)
            dstrength = jnp.zeros((rows, LANES), f32)
            for h in range(local_heads):
                n = m * local_heads + h
                p, q, k, v, beta, spread, grow, shrink, carried = work[n]
                q32, k32, v32 = q.astype(f32), k.astype(f32), v.astype(f32)
                dquery = grow * dgrown[n] + dq[n]
                dkey = (beta * grow) * dweighted[n] + shrink * dshrunk[n] + dk[n] + dk_same[n]
                dvalue = beta * dright[n]
                weighed = dweighted[n] * k32 * grow
                shrunk = dshrunk[n] * k32 * shrink
                dstr = jnp.sum(dright[n] * v32 + weighed, axis=1, keepdims=True) + jnp.sum(
                    keyed[n], axis=1, keepdims=True
                )
                dtot = jnp.sum(
                    dgrown[n] * q32 * grow + weighed * beta - shrunk, axis=1, keepdims=True
                ) + jnp.sum(moved[n] - moved[n].T, axis=1, keepdims=True)
                end = jnp.sum(shrunk) + jnp.sum(carried * (states[b, p] * grad_states[b, p]))
                dtot = dtot + jnp.where(last, end, 0.0)
                dtotal = dtotal + jnp.where(lane == h, dtot, 0.0)
                dstrength = dstrength + jnp.where(lane == local_heads + h, dstr, 0.0)
                for part, grad in ((0, dquery), (1, dkey), (2, dvalue)):
                    at = part * cols + h * LANES
                    grad = grad.astype(low).astype(f32)
                    if part == 0:
                        grad = grad * scale
                    if part < 2:
                        raw = act[:, at : at + LANES]
                        root = lax.rsqrt(jnp.sum(raw * raw, axis=1, keepdims=True) + eps_key)
                        unit = raw * root
                        grad = root * (grad - unit * jnp.sum(unit * grad, axis=1, keepdims=True))
                    dext[m, 0:rows, at : at + LANES] = grad * slope[:, at : at + LANES]
            dext[m, rows : rows + 8, :] = ahead[m]
            dconv = dext[m, 0:rows, :]
            ahead[m] = dconv[0:8, :]
            du = conv[taps - 1 : taps, :] * dconv
            for j in range(taps - 1):
                du = du + conv[j : j + 1, :] * dext[m, taps - 1 - j : taps - 1 - j + rows, :]
            grad_proj[*pos, :, :qkv] = du.astype(low)
            for j in range(taps):
                term = dconv * ext[m, 9 - taps + j : 9 - taps + j + rows, :]
                conv_sum[j] += jnp.sum(term.reshape(rows // 8, 8, qkv), axis=0)
            logits = proj[*pos, :, 4 * cols :].astype(f32)
            ddecay = mm_exact(upto_t, dtotal)
            strength = gates[b, m]
            dlogit = jnp.where(
                lane < local_heads,
                -rates[...] * jax.nn.sigmoid(logits) * ddecay,
                strength * (1.0 - strength) * dstrength,
            )
            dlogit = jnp.where(lane < 2 * local_heads, dlogit, 0.0).astype(low)
            grad_proj[*pos, :, 4 * cols :] = dlogit
            grad_rates[...] -= jnp.sum(softplus(logits) * ddecay, axis=0, keepdims=True)
        return carry

    lax.fori_loop(0, blocks, finish, 0)
    for j in range(taps):
        grad_conv[j : j + 1, :] = jnp.sum(conv_sum[j], axis=0, keepdims=True)


def in_vmem():
    return pl.BlockSpec(memory_space=pltpu.VMEM)


def heads_forward(perm, proj, conv, rates, gain, local_heads):
    blocks, micro, rows, _ = proj.shape
    cols = local_heads * LANES
    chains = micro * local_heads

    def shape(dims, kind):
        return jax.ShapeDtypeStruct(dims, kind)

    return pl.pallas_call(
        partial(forward_kernel, local_heads, perm.shape[0]),
        out_shape=(
            shape((blocks, micro, rows, cols), low),
            shape((blocks, micro, rows, cols), low),
            shape((blocks, micro, rows, 3 * cols), low),
            shape((blocks, micro, rows, LANES), f32),
            shape((blocks, chains, rows, rows), f32),
            shape((blocks, chains, LANES, rows), f32),
            shape((blocks, chains, rows, LANES), f32),
            shape((blocks, chains, LANES, LANES), f32),
        ),
        in_specs=[pl.BlockSpec(memory_space=pltpu.SMEM)] + [in_vmem()] * 4,
        out_specs=(in_vmem(),) * 8,
        scratch_shapes=[
            pltpu.VMEM((PAIR * micro, rows + 8, 3 * cols), f32),
            pltpu.VMEM((blocks, chains, rows, LANES), f32),
            pltpu.VMEM((blocks, chains, rows, LANES), f32),
            pltpu.VMEM((blocks, chains, rows, rows), f32),
            pltpu.VMEM((blocks, chains, LANES, rows), f32),
            pltpu.VMEM((chains, LANES, LANES), f32),
        ],
        compiler_params=pltpu.CompilerParams(vmem_limit_bytes=50 * 1024 * 1024),
        name="heads_forward",
    )(perm, proj, conv, rates, gain)


def heads_backward(perm, grad_mixed, proj, conv, rates, gain, kept, local_heads):
    blocks, micro, rows, wide = proj.shape
    cols = local_heads * LANES
    chains = micro * local_heads
    taps = conv.shape[0]

    def shape(dims, kind):
        return jax.ShapeDtypeStruct(dims, kind)

    return pl.pallas_call(
        partial(backward_kernel, local_heads, perm.shape[0]),
        out_shape=(
            shape((blocks, micro, rows, wide), low),
            shape((taps, 3 * cols), f32),
            shape((1, LANES), f32),
            shape((1, LANES), f32),
        ),
        in_specs=[pl.BlockSpec(memory_space=pltpu.SMEM)] + [in_vmem()] * 12,
        out_specs=(in_vmem(),) * 4,
        scratch_shapes=[
            pltpu.VMEM((micro, rows + 8, 3 * cols), f32),
            pltpu.VMEM((micro, rows + 8, 3 * cols), f32),
            pltpu.VMEM((micro, 8, 3 * cols), f32),
            pltpu.VMEM((taps, 8, 3 * cols), f32),
            pltpu.VMEM((blocks, chains, rows, LANES), f32),
            pltpu.VMEM((blocks, chains, rows, LANES), f32),
            pltpu.VMEM((blocks, chains, LANES, LANES), f32),
            pltpu.VMEM((blocks, chains, rows, LANES), f32),
            pltpu.VMEM((blocks, chains, LANES, LANES), f32),
            pltpu.VMEM((chains, LANES, LANES), f32),
        ],
        compiler_params=pltpu.CompilerParams(vmem_limit_bytes=50 * 1024 * 1024),
        name="heads_backward",
    )(perm, grad_mixed, proj, conv, rates, gain, *kept)


both = ("dp", "seq")


def swap(value, axis, bit):
    return lax.ppermute(value, axis, [(i, i ^ bit) for i in range(lax.axis_size(axis))])


def tie(*values):
    return lax.optimization_barrier(values)


def gather_places():
    peers = lax.axis_size("seq")
    place = jnp.arange(peers, dtype=jnp.int32)
    if peers != 8:
        return place
    place = place ^ lax.axis_index("seq").astype(jnp.int32)
    return place // 2 + 4 * (place % 2)


def gather_seq(rows_in):
    if lax.axis_size("seq") != 8:
        return lax.all_gather(rows_in, "seq", axis=0, tiled=True)
    half = rows_in.shape[0] // 2
    top, bottom = rows_in[:half], rows_in[half:]
    top_x, bottom_y = swap(top, "seq", 2), swap(bottom, "seq", 4)
    top_y = swap(jnp.concatenate([top, top_x]), "seq", 4)
    bottom_x = swap(jnp.concatenate([bottom, bottom_y]), "seq", 2)
    near = jnp.concatenate(
        [top, bottom, top_x, bottom_x[:half], top_y[:half], bottom_y, top_y[half:], bottom_x[half:]]
    )
    return jnp.concatenate([near, swap(near, "seq", 1)])


def scatter_seq(partial_rows, beside=None):
    peers = lax.axis_size("seq")
    if peers != 8:
        total = lax.psum_scatter(
            partial_rows.astype(low), "seq", scatter_dimension=0, tiled=True
        ).astype(f32)
        return total if beside is None else (total, beside)
    terms = partial_rows.astype(low).reshape(peers, -1, partial_rows.shape[-1])
    half = terms.shape[1] // 2
    near = terms[:4].astype(f32) + swap(terms[4:], "seq", 1).astype(f32)
    top, bottom = near[:, :half].astype(low), near[:, half:].astype(low)
    top_x = swap(top[1::2], "seq", 2)
    bottom_y = swap(bottom[2:], "seq", 4)
    top = near[0::2, :half] + top_x.astype(f32)
    bottom = near[:2, half:] + bottom_y.astype(f32)
    if beside is not None:
        top, bottom, beside = tie(top, bottom, beside)
    top_y = swap(top[1].astype(low), "seq", 4)
    bottom_x = swap(bottom[1].astype(low), "seq", 2)
    total = jnp.concatenate([top[0] + top_y.astype(f32), bottom[0] + bottom_x.astype(f32)])
    return total if beside is None else (total, beside)


def sum_all(value):
    for axis in both:
        size, bit = lax.axis_size(axis), 1
        if size.bit_length() % 2 == 0:
            value, bit = value + swap(value, axis, 1), 2
        while bit < size:
            one, two, three = (swap(value, axis, k * bit) for k in (1, 2, 3))
            value, bit = (value + one) + (two + three), 4 * bit
    return value


def to_columns(pieces):
    rows_here = lax.all_to_all(pieces, "seq", split_axis=0, concat_axis=0, tiled=True)
    return rows_here.reshape(-1, pieces.shape[-1])


def gather_dp(rows_here):
    return lax.all_gather(rows_here, "dp", axis=0, tiled=True)


def sum_dp(term):
    return lax.psum_scatter(term.astype(low), "dp", scatter_dimension=0, tiled=True)


def to_owners(own):
    pieces = own.reshape(lax.axis_size("seq"), -1, own.shape[1])
    return lax.all_to_all(pieces, "seq", split_axis=0, concat_axis=0, tiled=True)


def widen(columns):
    extra = -columns.shape[-1] % LANES
    return jnp.pad(columns, [(0, 0)] * (columns.ndim - 1) + [(0, extra)])


def assemble_kernel(local_heads, pieces, whole):
    peers, _, wide = pieces.shape
    cols = (wide - LANES) // 4
    width = cols * peers
    logits = []
    for part in range(5):
        for j in range(peers):
            from_here = slice(part * cols, min((part + 1) * cols, wide))
            total = pieces[j, :, from_here].astype(f32)
            if part < 4:
                whole[:, part * width + j * cols : part * width + (j + 1) * cols] = total
            else:
                logits.append(total)
    for kind in range(2):
        here = slice(kind * local_heads, (kind + 1) * local_heads)
        for j in range(peers):
            at = 4 * width + kind * local_heads * peers + j * local_heads
            whole[:, at : at + local_heads] = logits[j][:, here]


def assemble(pieces, local_heads):
    peers, rows, wide = pieces.shape
    total = (wide - LANES) * peers + 2 * local_heads * peers
    return pl.pallas_call(
        partial(assemble_kernel, local_heads),
        out_shape=jax.ShapeDtypeStruct((rows, total), f32),
        in_specs=[in_vmem()],
        out_specs=in_vmem(),
        compiler_params=pltpu.CompilerParams(vmem_limit_bytes=30 * 1024 * 1024),
        name="assemble",
    )(pieces)


def hop(step, back):
    groups, peers = lax.axis_size("dp"), lax.axis_size("seq")
    ratio = peers // groups
    pairs = [(s, (s + step) % groups * ratio + s // groups) for s in range(peers)]
    return [(b, a) for a, b in pairs] if back else pairs


def pick(parts, index):
    return lax.dynamic_index_in_dim(parts, index, 0, keepdims=False)


def out_rows_near(rows):
    return jnp.stack([rows] + [swap(rows, "dp", k) for k in range(1, lax.axis_size("dp"))])


def out_rows_here(parts):
    groups, ratio = lax.axis_size("dp"), lax.axis_size("seq") // lax.axis_size("dp")
    place, here = lax.axis_index("dp"), lax.axis_index("seq")
    got = jnp.stack(
        [
            lax.ppermute(pick(parts, (here + t) % groups ^ place), "seq", hop(t, False))
            for t in range(groups)
        ]
    )
    return jnp.concatenate([pick(got, (here // ratio - e) % groups) for e in range(groups)])


def out_rows_sent(term):
    groups, ratio = lax.axis_size("dp"), lax.axis_size("seq") // lax.axis_size("dp")
    here = lax.axis_index("seq")
    parts = term.reshape(groups, -1, term.shape[1])
    got = jnp.stack(
        [
            lax.ppermute(pick(parts, (here // ratio - t) % groups), "seq", hop(t, True))
            for t in range(groups)
        ]
    )
    return jnp.stack([pick(got, (z - here) % groups) for z in range(groups)])


def out_rows_sum(parts):
    place = lax.axis_index("dp")
    total = pick(parts, place).astype(f32)
    for k in range(1, lax.axis_size("dp")):
        total = total + swap(pick(parts, place ^ k), "dp", k).astype(f32)
    return total


def dot32(left, right):
    return jnp.dot(left, right, preferred_element_type=f32)


def dot_t(left, right):
    return lax.dot_general(left, right, (((1,), (1,)), ((), ())), preferred_element_type=f32)


def t_dot(left, right):
    return lax.dot_general(left, right, (((0,), (0,)), ((), ())), preferred_element_type=f32)


def shards(
    tokens,
    lengths,
    norm_gain,
    mix_weight,
    conv_weight,
    decay_rate,
    out_gain,
    out_weight,
    mlp_gain,
    mlp_in_weight,
    mlp_out_weight,
    grad_out,
):
    micro, seq_rows, width = tokens.shape
    heads = decay_rate.shape[0]
    groups = lax.axis_size("dp")
    peers = lax.axis_size("seq")
    here = lax.axis_index("seq")
    local_heads = heads // peers
    taps = conv_weight.shape[0]
    units = mlp_out_weight.shape[1]
    own_units = units // peers
    own_rows = mix_weight.shape[0]
    cols = width // peers
    logit_cols = 2 * local_heads

    positions = here * seq_rows + lax.broadcasted_iota(jnp.int32, (micro, seq_rows), 1)
    valid = (positions < lengths[:, None]).astype(f32).reshape(-1, 1)
    inputs = tokens.reshape(-1, width).astype(f32)

    out_parts = out_rows_near(out_weight)
    main = mix_weight[:, : 4 * width].reshape(own_rows, 4, peers, cols).transpose(2, 0, 1, 3)
    logits = mix_weight[:, 4 * width :].reshape(own_rows, 2, peers, local_heads)
    logits = logits.transpose(2, 0, 1, 3).reshape(peers, own_rows, logit_cols)
    mix_rows = to_columns(
        jnp.concatenate([main.reshape(peers, own_rows, 4 * cols), widen(logits)], axis=2)
    )
    wide_cols = mix_rows.shape[1]
    normed, norm_back = jax.vjp(rms_scale, inputs, norm_gain)
    gate_up = mlp_in_weight.reshape(own_rows, 2, peers, own_units).transpose(2, 0, 1, 3)
    down = mlp_out_weight.reshape(own_rows, peers, 1, own_units).transpose(1, 0, 2, 3)
    mlp_pieces = jnp.concatenate([gate_up, down], axis=2).reshape(peers, own_rows, 3 * own_units)
    mix_rows, normed_low, mlp_pieces, out_parts = tie(
        mix_rows, normed.astype(low), mlp_pieces, out_parts
    )
    mix_here = gather_dp(mix_rows)
    normed_all = gather_seq(normed_low)
    mlp_rows = to_columns(mlp_pieces)
    cotangent = valid * grad_out.reshape(-1, width).astype(f32)
    mix_here, out_parts, mlp_rows, normed_all, cot_low = tie(
        mix_here, out_parts, mlp_rows, normed_all, cotangent.astype(low)
    )
    out_here = out_rows_here(out_parts)
    in_here = gather_dp(mlp_rows[:, : 2 * own_units])
    down_here = gather_dp(mlp_rows[:, 2 * own_units :])

    projected = dot32(normed_all, mix_here).astype(low).reshape(peers, micro, seq_rows, -1)
    conv_here = lax.dynamic_index_in_dim(
        conv_weight.reshape(taps, 3, peers, cols), here, 2, keepdims=False
    ).reshape(taps, 3 * cols)
    rates_here = lax.dynamic_slice_in_dim(decay_rate, here * local_heads, local_heads)
    rate_lanes = jnp.pad(rates_here, (0, LANES - local_heads)).reshape(1, LANES)
    gain_row = out_gain.reshape(1, LANES)
    places = gather_places()
    mixed, *kept = heads_forward(
        places, projected, conv_here, rate_lanes, gain_row, local_heads
    )
    mixed, cot_low = tie(mixed, cot_low)
    mixed_low = mixed.reshape(-1, cols)
    branch, in_here = scatter_seq(dot32(mixed_low, out_here), in_here)
    hidden = inputs + branch

    second, second_back = jax.vjp(rms_scale, hidden, mlp_gain)
    second_all = gather_seq(second.astype(low))
    cot_all = gather_seq(cot_low)
    gate_up = dot32(second_all, in_here).astype(low)
    activated, swiglu_back = jax.vjp(swiglu, gate_up.astype(f32))
    activated_low = activated.astype(low)
    grad_down_term = t_dot(cot_all, activated_low).astype(low)
    cot_all, grad_down_term, down_here = tie(cot_all, grad_down_term, down_here)
    (grad_gate_up,) = swiglu_back(dot32(cot_all, down_here))
    grad_gate_low = grad_gate_up.astype(low)
    grad_second = scatter_seq(dot_t(grad_gate_low, in_here))
    grad_hidden_norm, grad_mlp_gain = second_back(grad_second)
    grad_hidden = cotangent + grad_hidden_norm
    branch_low = grad_hidden.astype(low)
    branch_all = gather_seq(branch_low)
    grad_down = sum_dp(grad_down_term)
    grad_in = sum_dp(t_dot(second_all, grad_gate_low))

    branch_all, activated_low = tie(branch_all, activated_low)
    grad_mixed = dot_t(branch_all, out_here).reshape(peers, micro, seq_rows, cols)
    grad_mixed, grad_down = tie(grad_mixed, grad_down)
    grad_out_term = t_dot(mixed_low, branch_all).astype(low)
    grad_projected, grad_conv, rate_sums, gain_sums = (
        heads_backward(
            places,
            grad_mixed,
            projected,
            conv_here,
            rate_lanes,
            gain_row,
            kept,
            local_heads,
        )
    )
    grad_projected = grad_projected.reshape(-1, wide_cols)
    grad_mix_term = t_dot(normed_all, grad_projected).astype(low)
    grad_mix_term, grad_projected = tie(grad_mix_term, grad_projected)
    mix_own = sum_dp(grad_mix_term)
    out_parts = out_rows_sent(grad_out_term)
    grad_normed, grad_in = scatter_seq(dot_t(grad_projected, mix_here), to_owners(grad_in))
    grad_down = to_owners(grad_down)
    grad_inputs_norm, grad_norm_gain = norm_back(grad_normed)
    grad_tokens = grad_hidden + grad_inputs_norm
    feed_out = scatter_seq(dot_t(activated_low, down_here))
    result = (valid * (hidden + feed_out)).astype(low)

    conv_terms = lax.dynamic_update_slice(
        jnp.zeros((taps, 3, peers, cols), f32),
        grad_conv.reshape(taps, 3, 1, cols),
        (0, 0, here, 0),
    )
    rate_terms = lax.dynamic_update_slice(
        jnp.zeros((LANES,), f32), rate_sums[0, :local_heads], (here * local_heads,)
    )
    sizes = [width, width, LANES, LANES, taps * 3 * width]
    summed = sum_all(
        jnp.concatenate(
            [
                grad_norm_gain,
                grad_mlp_gain,
                gain_sums[0],
                rate_terms,
                conv_terms.reshape(-1),
            ]
        ).reshape(-1, LANES)
    ).reshape(-1)
    mix_own, out_parts, summed, grad_in, grad_down = tie(
        mix_own, out_parts, summed, grad_in, grad_down
    )
    grad_mix = to_owners(mix_own)
    grad_out_own = out_rows_sum(out_parts)
    grad_in = grad_in.reshape(peers, own_rows, 2, own_units).transpose(1, 2, 0, 3)
    grad_in = grad_in.reshape(own_rows, 2 * units).astype(f32)
    grad_down = grad_down.transpose(1, 0, 2).reshape(own_rows, units).astype(f32)
    ends = [sum(sizes[: i + 1]) for i in range(len(sizes))]
    sums = [summed[end - size : end] for end, size in zip(ends, sizes)]
    return (
        result.reshape(tokens.shape),
        grad_tokens.reshape(tokens.shape),
        sums[0],
        assemble(grad_mix, local_heads),
        sums[4].reshape(taps, 3 * width),
        sums[3][:heads],
        sums[2],
        grad_out_own,
        sums[1],
        grad_in,
        grad_down,
    )


def solution(mesh):
    in_specs = (
        P("dp", "seq", None),
        P("dp"),
        P(),
        P(("dp", "seq"), None),
        P(),
        P(),
        P(),
        P(("dp", "seq"), None),
        P(),
        P(("dp", "seq"), None),
        P(("dp", "seq"), None),
        P("dp", "seq", None),
    )
    out_specs = (
        P("dp", "seq", None),
        P("dp", "seq", None),
        P(),
        P(("dp", "seq"), None),
        P(),
        P(),
        P(),
        P(("dp", "seq"), None),
        P(),
        P(("dp", "seq"), None),
        P(("dp", "seq"), None),
    )
    return jax.shard_map(shards, mesh=mesh, in_specs=in_specs, out_specs=out_specs, check_vma=False)
```

```python
from functools import partial

import jax
import jax.numpy as jnp
from jax import lax
from jax.experimental import pallas as pl
from jax.experimental.pallas import tpu as pltpu
from jax.sharding import PartitionSpec as P

eps_norm = 1e-05
eps_key = 1e-06
LANES = 128
PAIR = 2
f32 = jnp.float32
low = jnp.bfloat16


def rms_scale(rows_in, gain):
    return (
        rows_in * lax.rsqrt(jnp.mean(rows_in * rows_in, axis=-1, keepdims=True) + eps_norm) * gain
    )


def swiglu(gate_up):
    hidden_units = gate_up.shape[-1] // 2
    return jax.nn.silu(gate_up[..., :hidden_units]) * gate_up[..., hidden_units:]


def mm(left, right):
    return jnp.dot(left.astype(low), right.astype(low), preferred_element_type=f32)


def mm_nt(left, right):
    return lax.dot_general(
        left.astype(low), right.astype(low), (((1,), (1,)), ((), ())), preferred_element_type=f32
    )


def halves(v):
    if isinstance(v, tuple):
        return v
    if v.dtype == low:
        return (v,)
    top = v.astype(low)
    return top, (v - top.astype(f32)).astype(low)


def dot_fine(left, right, dims):
    left, right = halves(left), halves(right)
    total = None
    for i, a in enumerate(left):
        for j, b in enumerate(right):
            if i + j < 2:
                term = lax.dot_general(a, b, (dims, ((), ())), preferred_element_type=f32)
                total = term if total is None else total + term
    return total


def fine(left, right):
    return dot_fine(left, right, ((1,), (0,)))


def fine_nt(left, right):
    return dot_fine(left, right, ((1,), (1,)))


def mm_exact(left, right):
    return jnp.dot(left, right, precision=lax.Precision.HIGHEST, preferred_element_type=f32)


def softplus(v):
    return jnp.maximum(v, 0.0) + jnp.log1p(jnp.exp(-jnp.abs(v)))


def grid_of(size):
    row = lax.broadcasted_iota(jnp.int32, (size, size), 0)
    col = lax.broadcasted_iota(jnp.int32, (size, size), 1)
    return row, col


def lower_inverses(parts, row, col):
    size = parts[0].shape[0]
    joined = (row // 2 == col // 2) & (row > col)
    unit = (row == col).astype(f32)
    inverses = [unit - jnp.where(joined, part, 0.0) for part in parts]
    width = 2
    while width < size:
        joined = (row // (2 * width) == col // (2 * width)) & (row // width > col // width)
        corners = [jnp.where(joined, part, 0.0) for part in parts]
        moved = [mm(corner, inverse) for corner, inverse in zip(corners, inverses)]
        steps = [mm(inverse, move) for inverse, move in zip(inverses, moved)]
        inverses = [inverse - change for inverse, change in zip(inverses, steps)]
        width *= 2
    return inverses


def fill_taps(ext, slot, proj, pos, prev, first, qkv):
    rows = proj.shape[2]
    ext[slot, 8 : 8 + rows, :] = proj[*pos, :, :qkv].astype(f32)
    tail = proj[*prev, rows - 16 :, :qkv].astype(f32)[8:]
    ext[slot, 0:8, :] = jnp.where(first, 0.0, tail)


def conv_rows(ext, m, conv, rows):
    taps = conv.shape[0]
    total = conv[0:1, :] * ext[m, 9 - taps : 9 - taps + rows, :]
    for j in range(1, taps):
        total = total + conv[j : j + 1, :] * ext[m, 9 - taps + j : 9 - taps + j + rows, :]
    return total


def forward_kernel(
    local_heads,
    blocks,
    perm,
    proj,
    conv,
    rates,
    gain,
    mixed,
    heads_out,
    qkv_out,
    gates,
    inv_t,
    weighted_t,
    fresh,
    states,
    ext,
    targets,
    weighted,
    scores,
    keys_t,
    state,
):
    _, micro, rows, _ = proj.shape
    cols = local_heads * LANES
    qkv = 3 * cols
    row, col = grid_of(rows)
    upto = (row >= col).astype(f32)
    lane = lax.broadcasted_iota(jnp.int32, (rows, LANES), 1)
    scale = float(LANES) ** -0.5

    def prepare(i, carry):
        work = []
        for part in range(PAIR):
            b = i * PAIR + part
            for m in range(micro):
                slot = part * micro + m
                pos, prev = (perm[b], m), (perm[jnp.maximum(b - 1, 0)], m)
                fill_taps(ext, slot, proj, pos, prev, b == 0, qkv)
                conv_out = conv_rows(ext, slot, conv, rows)
                act = conv_out * jax.nn.sigmoid(conv_out)
                logits = proj[*pos, :, 4 * cols :].astype(f32)
                decay = -rates[...] * softplus(logits)
                strength = jax.nn.sigmoid(logits)
                total = mm_exact(upto, decay)
                total_t = total.T
                gates[b, m] = jnp.where(lane < local_heads, total, strength)
                growth = jnp.exp(total)
                fade = jnp.exp(total[rows - 1 : rows, :] - total)
                for h in range(local_heads):
                    raw_q = act[:, h * LANES : (h + 1) * LANES]
                    raw_k = act[:, cols + h * LANES : cols + (h + 1) * LANES]
                    q = raw_q * (
                        lax.rsqrt(jnp.sum(raw_q * raw_q, axis=1, keepdims=True) + eps_key) * scale
                    )
                    k = raw_k * lax.rsqrt(jnp.sum(raw_k * raw_k, axis=1, keepdims=True) + eps_key)
                    q = q.astype(low)
                    k = k.astype(low)
                    v = act[:, 2 * cols + h * LANES : 2 * cols + (h + 1) * LANES].astype(low)
                    qkv_out[b, m, :, h * LANES : (h + 1) * LANES] = q
                    qkv_out[b, m, :, cols + h * LANES : cols + (h + 1) * LANES] = k
                    qkv_out[b, m, :, 2 * cols + h * LANES : 2 * cols + (h + 1) * LANES] = v
                    beta = strength[:, local_heads + h : local_heads + h + 1]
                    spread = jnp.exp(
                        jnp.minimum(total[:, h : h + 1] - total_t[h : h + 1, :], 0.0)
                    )
                    work.append(
                        (b, m * local_heads + h, q, k, v, beta, spread, growth[:, h : h + 1], fade[:, h : h + 1])
                    )
        same = [mm_nt(k, k) for _, _, _, k, *_ in work]
        cross = [mm_nt(q, k) for _, _, q, k, *_ in work]
        parts = [
            jnp.where(row > col, item[6] * item[5] * dots, 0.0) for item, dots in zip(work, same)
        ]
        inverses = lower_inverses(parts, row, col)
        keyed = [fine(inv, item[3].astype(f32) * (item[5] * item[7])) for inv, item in zip(inverses, work)]
        valued = [fine(inv, item[4].astype(f32) * item[5]) for inv, item in zip(inverses, work)]
        for n, (b, p, q, k, v, beta, spread, grow, shrink) in enumerate(work):
            inv_t[b, p] = inverses[n].T
            weighted[b, p] = keyed[n]
            weighted_t[b, p] = keyed[n].T
            targets[b, p] = valued[n]
            scores[b, p] = upto * spread * cross[n]
            keys_t[b, p] = (k.astype(f32) * shrink).T
        return carry

    lax.fori_loop(0, blocks // PAIR, prepare, 0)
    state[...] = jnp.zeros_like(state)

    def step(b, carry):
        growth = [jnp.exp(gates[b, m]) for m in range(micro)]
        chains = [(m, h, m * local_heads + h) for m in range(micro) for h in range(local_heads)]
        now = [state[p] for _, _, p in chains]
        now_halves = [halves(v) for v in now]
        new = [
            targets[b, p] - fine(weighted[b, p], parts) for (_, _, p), parts in zip(chains, now_halves)
        ]
        new_halves = [halves(v) for v in new]
        moved = [fine(keys_t[b, p], parts) for (_, _, p), parts in zip(chains, new_halves)]
        for (m, h, p), old, fed in zip(chains, now, moved):
            states[b, p] = old
            state[p] = growth[m][rows - 1 : rows, h : h + 1] * old + fed
        outs = []
        for (m, h, p), fill, parts in zip(chains, new_halves, now_halves):
            q = qkv_out[b, m, :, h * LANES : (h + 1) * LANES].astype(f32)
            outs.append(fine(q * growth[m][:, h : h + 1], parts) + fine(scores[b, p], fill))
        for (m, h, p), fill, out in zip(chains, new, outs):
            fresh[b, p] = fill
            out = out.astype(low)
            heads_out[b, m, :, h * LANES : (h + 1) * LANES] = out
            out = out.astype(f32)
            pos = (perm[b], m)
            gate = proj[*pos, :, 3 * cols + h * LANES : 3 * cols + (h + 1) * LANES].astype(f32)
            normed = out * lax.rsqrt(jnp.mean(out * out, axis=1, keepdims=True) + eps_norm) * gain[...]
            done = (normed * (gate * jax.nn.sigmoid(gate))).astype(low)
            mixed[*pos, :, h * LANES : (h + 1) * LANES] = done
        return carry

    lax.fori_loop(0, blocks, step, 0)


def backward_kernel(
    local_heads,
    blocks,
    perm,
    grad_mixed,
    proj,
    conv,
    rates,
    gain,
    heads_out,
    qkv_in,
    gates,
    inv_t,
    weighted_t,
    fresh,
    states,
    grad_proj,
    grad_conv,
    grad_rates,
    grad_gain,
    ext,
    dext,
    ahead,
    conv_sum,
    grad_out,
    value_part,
    state_part,
    grad_fresh,
    grad_states,
    grad_state,
):
    _, micro, rows, _ = proj.shape
    cols = local_heads * LANES
    qkv = 3 * cols
    taps = conv.shape[0]
    row, col = grid_of(rows)
    lane = lax.broadcasted_iota(jnp.int32, (rows, LANES), 1)
    last = lax.broadcasted_iota(jnp.int32, (rows, 1), 0) == rows - 1
    scale = float(LANES) ** -0.5
    upto_t = (col >= row).astype(f32)
    grad_gain[...] = jnp.zeros_like(grad_gain)
    grad_rates[...] = jnp.zeros_like(grad_rates)
    conv_sum[...] = jnp.zeros_like(conv_sum)
    ahead[...] = jnp.zeros_like(ahead)
    grad_state[...] = jnp.zeros_like(grad_state)

    def prepare(b, carry):
        work = []
        for m in range(micro):
            pos = (perm[b], m)
            total = gates[b, m]
            growth = jnp.exp(total)
            total_t = total.T
            for h in range(local_heads):
                p = m * local_heads + h
                here = slice(h * LANES, (h + 1) * LANES)
                out = heads_out[b, m, :, here].astype(f32)
                gate = proj[*pos, :, 3 * cols + h * LANES : 3 * cols + (h + 1) * LANES].astype(f32)
                dmixed = grad_mixed[*pos, :, here].astype(f32)
                root = lax.rsqrt(jnp.mean(out * out, axis=1, keepdims=True) + eps_norm)
                unit = out * root
                sig = jax.nn.sigmoid(gate)
                dnormed = dmixed * (gate * sig)
                dgate = dmixed * (unit * gain[...]) * (sig * (1.0 + gate * (1.0 - sig)))
                at = slice(3 * cols + h * LANES, 3 * cols + (h + 1) * LANES)
                grad_proj[*pos, :, at] = dgate.astype(low)
                grad_gain[...] += jnp.sum(dnormed * unit, axis=0, keepdims=True)
                dunit = dnormed * gain[...]
                dout = root * (dunit - unit * jnp.mean(unit * dunit, axis=1, keepdims=True))
                dout = dout.astype(low)
                grad_out[b, p] = dout.astype(grad_out.dtype)
                q = qkv_in[b, m, :, here]
                k = qkv_in[b, m, :, cols + h * LANES : cols + (h + 1) * LANES]
                spread_t = jnp.exp(jnp.minimum(total_t[h : h + 1, :] - total[:, h : h + 1], 0.0))
                grown_t = (q.astype(f32) * growth[:, h : h + 1]).T
                work.append((p, q, k, dout, upto_t * spread_t, grown_t))
        dots = [mm_nt(k, q) for _, q, k, *_ in work]
        parts = [fine(spread * dot, dout) for (_, _, _, dout, spread, _), dot in zip(work, dots)]
        fed = [fine(grown_t, dout) for _, _, _, dout, _, grown_t in work]
        for (p, *_), part, feed in zip(work, parts, fed):
            value_part[b, p] = part
            state_part[b, p] = feed
        return carry

    lax.fori_loop(0, blocks, prepare, 0)

    def step(i, carry):
        b = blocks - 1 - i
        chains = [(m, h, m * local_heads + h) for m in range(micro) for h in range(local_heads)]
        total = [gates[b, m] for m in range(micro)]
        fade = [jnp.exp(v[rows - 1 : rows, :] - v) for v in total]
        later = [grad_state[p] for _, _, p in chains]
        dnew = []
        for (m, h, p), grad in zip(chains, later):
            k = qkv_in[b, m, :, cols + h * LANES : cols + (h + 1) * LANES].astype(f32)
            dnew.append(value_part[b, p] + fine(k * fade[m][:, h : h + 1], grad))
        moved = [fine(weighted_t[b, p], grad) for (_, _, p), grad in zip(chains, dnew)]
        for (m, h, p), grad, fill, move in zip(chains, later, dnew, moved):
            grad_states[b, p] = grad
            grad_fresh[b, p] = fill
            carried = jnp.exp(total[m][rows - 1 : rows, h : h + 1])
            grad_state[p] = state_part[b, p] + carried * grad - move
        return carry

    lax.fori_loop(0, blocks, step, 0)

    def finish(i, carry):
        b = blocks - 1 - i
        work = []
        for m in range(micro):
            total = gates[b, m]
            total_t = total.T
            growth = jnp.exp(total)
            fade = jnp.exp(total[rows - 1 : rows, :] - total)
            for h in range(local_heads):
                p = m * local_heads + h
                q = qkv_in[b, m, :, h * LANES : (h + 1) * LANES]
                k = qkv_in[b, m, :, cols + h * LANES : cols + (h + 1) * LANES]
                v = qkv_in[b, m, :, 2 * cols + h * LANES : 2 * cols + (h + 1) * LANES]
                beta = total[:, local_heads + h : local_heads + h + 1]
                spread = jnp.exp(jnp.minimum(total[:, h : h + 1] - total_t[h : h + 1, :], 0.0))
                work.append(
                    (p, q, k, v, beta, spread, growth[:, h : h + 1], fade[:, h : h + 1], growth[rows - 1 : rows, h : h + 1])
                )
        number = range(len(work))
        queries = [item[1] for item in work]
        keys = [item[2] for item in work]
        douts = [grad_out[b, item[0]].astype(low) for item in work]
        news = [halves(fresh[b, item[0]]) for item in work]
        nows = [halves(states[b, item[0]]) for item in work]
        laters = [halves(grad_states[b, item[0]]) for item in work]
        dright = [fine(inv_t[b, item[0]], grad_fresh[b, item[0]]) for item in work]
        dgrown = [fine_nt(douts[n], nows[n]) for n in number]
        dshrunk = [fine_nt(news[n], laters[n]) for n in number]
        dots = [mm_nt(queries[n], keys[n]) for n in number]
        same = [mm_nt(keys[n], keys[n]) for n in number]
        dscores = [fine_nt(douts[n], news[n]) for n in number]
        dright_halves = [halves(v) for v in dright]
        dweighted = [-fine_nt(dright_halves[n], nows[n]) for n in number]
        dbelow = [fine_nt(dright_halves[n], news[n]) for n in number]
        keyed, moved = [], []
        for n in number:
            beta, spread = work[n][4], work[n][5]
            dscores[n] = dscores[n] * jnp.where(row >= col, spread, 0.0)
            dbelow[n] = dbelow[n] * jnp.where(row > col, -spread, 0.0)
            keyed.append(dbelow[n] * same[n])
            moved.append(dscores[n] * dots[n] + keyed[n] * beta)
            dbelow[n] = dbelow[n] * beta
        dq = [fine(dscores[n], keys[n]) for n in number]
        dk = [fine(dscores[n].T, queries[n]) for n in number]
        dk_same = [fine(dbelow[n] + dbelow[n].T, keys[n]) for n in number]
        for m in range(micro):
            pos, prev = (perm[b], m), (perm[jnp.maximum(b - 1, 0)], m)
            fill_taps(ext, m, proj, pos, prev, b == 0, qkv)
            conv_out = conv_rows(ext, m, conv, rows)
            sig = jax.nn.sigmoid(conv_out)
            act = conv_out * sig
            slope = sig * (1.0 + conv_out * (1.0 - sig))
            dtotal = jnp.zeros((rows, LANES), f32)
            dstrength = jnp.zeros((rows, LANES), f32)
            for h in range(local_heads):
                n = m * local_heads + h
                p, q, k, v, beta, spread, grow, shrink, carried = work[n]
                q32, k32, v32 = q.astype(f32), k.astype(f32), v.astype(f32)
                dquery = grow * dgrown[n] + dq[n]
                dkey = (beta * grow) * dweighted[n] + shrink * dshrunk[n] + dk[n] + dk_same[n]
                dvalue = beta * dright[n]
                weighed = dweighted[n] * k32 * grow
                shrunk = dshrunk[n] * k32 * shrink
                dstr = jnp.sum(dright[n] * v32 + weighed, axis=1, keepdims=True) + jnp.sum(
                    keyed[n], axis=1, keepdims=True
                )
                dtot = jnp.sum(
                    dgrown[n] * q32 * grow + weighed * beta - shrunk, axis=1, keepdims=True
                ) + jnp.sum(moved[n] - moved[n].T, axis=1, keepdims=True)
                end = jnp.sum(shrunk) + jnp.sum(carried * (states[b, p] * grad_states[b, p]))
                dtot = dtot + jnp.where(last, end, 0.0)
                dtotal = dtotal + jnp.where(lane == h, dtot, 0.0)
                dstrength = dstrength + jnp.where(lane == local_heads + h, dstr, 0.0)
                for part, grad in ((0, dquery), (1, dkey), (2, dvalue)):
                    at = part * cols + h * LANES
                    grad = grad.astype(low).astype(f32)
                    if part == 0:
                        grad = grad * scale
                    if part < 2:
                        raw = act[:, at : at + LANES]
                        root = lax.rsqrt(jnp.sum(raw * raw, axis=1, keepdims=True) + eps_key)
                        unit = raw * root
                        grad = root * (grad - unit * jnp.sum(unit * grad, axis=1, keepdims=True))
                    dext[m, 0:rows, at : at + LANES] = grad * slope[:, at : at + LANES]
            dext[m, rows : rows + 8, :] = ahead[m]
            dconv = dext[m, 0:rows, :]
            ahead[m] = dconv[0:8, :]
            du = conv[taps - 1 : taps, :] * dconv
            for j in range(taps - 1):
                du = du + conv[j : j + 1, :] * dext[m, taps - 1 - j : taps - 1 - j + rows, :]
            grad_proj[*pos, :, :qkv] = du.astype(low)
            for j in range(taps):
                term = dconv * ext[m, 9 - taps + j : 9 - taps + j + rows, :]
                conv_sum[j] += jnp.sum(term.reshape(rows // 8, 8, qkv), axis=0)
            logits = proj[*pos, :, 4 * cols :].astype(f32)
            ddecay = mm_exact(upto_t, dtotal)
            strength = gates[b, m]
            dlogit = jnp.where(
                lane < local_heads,
                -rates[...] * jax.nn.sigmoid(logits) * ddecay,
                strength * (1.0 - strength) * dstrength,
            )
            dlogit = jnp.where(lane < 2 * local_heads, dlogit, 0.0).astype(low)
            grad_proj[*pos, :, 4 * cols :] = dlogit
            grad_rates[...] -= jnp.sum(softplus(logits) * ddecay, axis=0, keepdims=True)
        return carry

    lax.fori_loop(0, blocks, finish, 0)
    for j in range(taps):
        grad_conv[j : j + 1, :] = jnp.sum(conv_sum[j], axis=0, keepdims=True)


def in_vmem():
    return pl.BlockSpec(memory_space=pltpu.VMEM)


def heads_forward(perm, proj, conv, rates, gain, local_heads):
    blocks, micro, rows, _ = proj.shape
    cols = local_heads * LANES
    chains = micro * local_heads

    def shape(dims, kind):
        return jax.ShapeDtypeStruct(dims, kind)

    return pl.pallas_call(
        partial(forward_kernel, local_heads, perm.shape[0]),
        out_shape=(
            shape((blocks, micro, rows, cols), low),
            shape((blocks, micro, rows, cols), low),
            shape((blocks, micro, rows, 3 * cols), low),
            shape((blocks, micro, rows, LANES), f32),
            shape((blocks, chains, rows, rows), f32),
            shape((blocks, chains, LANES, rows), f32),
            shape((blocks, chains, rows, LANES), f32),
            shape((blocks, chains, LANES, LANES), f32),
        ),
        in_specs=[pl.BlockSpec(memory_space=pltpu.SMEM)] + [in_vmem()] * 4,
        out_specs=(in_vmem(),) * 8,
        scratch_shapes=[
            pltpu.VMEM((PAIR * micro, rows + 8, 3 * cols), f32),
            pltpu.VMEM((blocks, chains, rows, LANES), f32),
            pltpu.VMEM((blocks, chains, rows, LANES), f32),
            pltpu.VMEM((blocks, chains, rows, rows), f32),
            pltpu.VMEM((blocks, chains, LANES, rows), f32),
            pltpu.VMEM((chains, LANES, LANES), f32),
        ],
        compiler_params=pltpu.CompilerParams(vmem_limit_bytes=50 * 1024 * 1024),
        name="heads_forward",
    )(perm, proj, conv, rates, gain)


def heads_backward(perm, grad_mixed, proj, conv, rates, gain, kept, local_heads):
    blocks, micro, rows, wide = proj.shape
    cols = local_heads * LANES
    chains = micro * local_heads
    taps = conv.shape[0]

    def shape(dims, kind):
        return jax.ShapeDtypeStruct(dims, kind)

    return pl.pallas_call(
        partial(backward_kernel, local_heads, perm.shape[0]),
        out_shape=(
            shape((blocks, micro, rows, wide), low),
            shape((taps, 3 * cols), f32),
            shape((1, LANES), f32),
            shape((1, LANES), f32),
        ),
        in_specs=[pl.BlockSpec(memory_space=pltpu.SMEM)] + [in_vmem()] * 12,
        out_specs=(in_vmem(),) * 4,
        scratch_shapes=[
            pltpu.VMEM((micro, rows + 8, 3 * cols), f32),
            pltpu.VMEM((micro, rows + 8, 3 * cols), f32),
            pltpu.VMEM((micro, 8, 3 * cols), f32),
            pltpu.VMEM((taps, 8, 3 * cols), f32),
            pltpu.VMEM((blocks, chains, rows, LANES), f32),
            pltpu.VMEM((blocks, chains, rows, LANES), f32),
            pltpu.VMEM((blocks, chains, LANES, LANES), f32),
            pltpu.VMEM((blocks, chains, rows, LANES), f32),
            pltpu.VMEM((blocks, chains, LANES, LANES), f32),
            pltpu.VMEM((chains, LANES, LANES), f32),
        ],
        compiler_params=pltpu.CompilerParams(vmem_limit_bytes=50 * 1024 * 1024),
        name="heads_backward",
    )(perm, grad_mixed, proj, conv, rates, gain, *kept)


both = ("dp", "seq")


def swap(value, axis, bit):
    return lax.ppermute(value, axis, [(i, i ^ bit) for i in range(lax.axis_size(axis))])


def tie(*values):
    return lax.optimization_barrier(values)


def gather_places():
    peers = lax.axis_size("seq")
    place = jnp.arange(peers, dtype=jnp.int32)
    if peers != 8:
        return place
    place = place ^ lax.axis_index("seq").astype(jnp.int32)
    return place // 2 + 4 * (place % 2)


def gather_seq(rows_in):
    if lax.axis_size("seq") != 8:
        return lax.all_gather(rows_in, "seq", axis=0, tiled=True)
    half = rows_in.shape[0] // 2
    top, bottom = rows_in[:half], rows_in[half:]
    top_x, bottom_y = swap(top, "seq", 2), swap(bottom, "seq", 4)
    top_y = swap(jnp.concatenate([top, top_x]), "seq", 4)
    bottom_x = swap(jnp.concatenate([bottom, bottom_y]), "seq", 2)
    near = jnp.concatenate(
        [top, bottom, top_x, bottom_x[:half], top_y[:half], bottom_y, top_y[half:], bottom_x[half:]]
    )
    return jnp.concatenate([near, swap(near, "seq", 1)])


def scatter_seq(partial_rows, beside=None):
    peers = lax.axis_size("seq")
    if peers != 8:
        total = lax.psum_scatter(
            partial_rows.astype(low), "seq", scatter_dimension=0, tiled=True
        ).astype(f32)
        return total if beside is None else (total, *beside)
    terms = partial_rows.astype(low).reshape(peers, -1, partial_rows.shape[-1])
    half = terms.shape[1] // 2
    near = terms[:4].astype(f32) + swap(terms[4:], "seq", 1).astype(f32)
    top, bottom = near[:, :half].astype(low), near[:, half:].astype(low)
    top_x = swap(top[1::2], "seq", 2)
    bottom_y = swap(bottom[2:], "seq", 4)
    top = near[0::2, :half] + top_x.astype(f32)
    bottom = near[:2, half:] + bottom_y.astype(f32)
    if beside is not None:
        top, bottom, *beside = tie(top, bottom, *beside)
    top_y = swap(top[1].astype(low), "seq", 4)
    bottom_x = swap(bottom[1].astype(low), "seq", 2)
    total = jnp.concatenate([top[0] + top_y.astype(f32), bottom[0] + bottom_x.astype(f32)])
    return total if beside is None else (total, *beside)


def sum_all(value):
    for axis in both:
        size, bit = lax.axis_size(axis), 1
        if size.bit_length() % 2 == 0:
            value, bit = value + swap(value, axis, 1), 2
        while bit < size:
            one, two, three = (swap(value, axis, k * bit) for k in (1, 2, 3))
            value, bit = (value + one) + (two + three), 4 * bit
    return value


def to_columns(pieces):
    rows_here = lax.all_to_all(pieces, "seq", split_axis=0, concat_axis=0, tiled=True)
    return rows_here.reshape(-1, pieces.shape[-1])


def gather_dp(rows_here):
    return lax.all_gather(rows_here, "dp", axis=0, tiled=True)


def sum_dp(term):
    return lax.psum_scatter(term.astype(low), "dp", scatter_dimension=0, tiled=True)


def to_owners(own):
    pieces = own.reshape(lax.axis_size("seq"), -1, own.shape[1])
    return lax.all_to_all(pieces, "seq", split_axis=0, concat_axis=0, tiled=True)


def widen(columns):
    extra = -columns.shape[-1] % LANES
    return jnp.pad(columns, [(0, 0)] * (columns.ndim - 1) + [(0, extra)])


def assemble_kernel(local_heads, pieces, whole):
    peers, _, wide = pieces.shape
    cols = (wide - LANES) // 4
    width = cols * peers
    logits = []
    for part in range(5):
        for j in range(peers):
            from_here = slice(part * cols, min((part + 1) * cols, wide))
            total = pieces[j, :, from_here].astype(f32)
            if part < 4:
                whole[:, part * width + j * cols : part * width + (j + 1) * cols] = total
            else:
                logits.append(total)
    for kind in range(2):
        here = slice(kind * local_heads, (kind + 1) * local_heads)
        for j in range(peers):
            at = 4 * width + kind * local_heads * peers + j * local_heads
            whole[:, at : at + local_heads] = logits[j][:, here]


def assemble(pieces, local_heads):
    peers, rows, wide = pieces.shape
    total = (wide - LANES) * peers + 2 * local_heads * peers
    return pl.pallas_call(
        partial(assemble_kernel, local_heads),
        out_shape=jax.ShapeDtypeStruct((rows, total), f32),
        in_specs=[in_vmem()],
        out_specs=in_vmem(),
        compiler_params=pltpu.CompilerParams(vmem_limit_bytes=30 * 1024 * 1024),
        name="assemble",
    )(pieces)


def order_kernel(units, pieces, whole):
    peers, rows, _ = pieces.shape
    wide = units + LANES // 2
    middle = lax.broadcasted_iota(jnp.int32, (rows, LANES), 1) < LANES // 2
    for kind in range(2):
        for j in range(0, peers, 2):
            if kind == 0:
                one = pieces[j, :, :wide].astype(f32)
                two = pltpu.roll(pieces[j + 1, :, :wide].astype(f32), LANES // 2, axis=1)
            else:
                start = 2 * units - wide
                one = pltpu.roll(pieces[j, :, start:].astype(f32), wide - LANES // 2, axis=1)
                two = pieces[j + 1, :, start:].astype(f32)
            at = (kind * peers + j) * units
            whole[:, at : at + wide - LANES] = one[:, : wide - LANES]
            at = at + wide - LANES
            whole[:, at : at + LANES] = jnp.where(middle, one[:, wide - LANES :], two[:, :LANES])
            at = at + LANES
            whole[:, at : at + wide - LANES] = two[:, LANES:]


def order_units(pieces, units):
    peers, rows, _ = pieces.shape
    if units % LANES != LANES // 2 or peers % 2 != 0:
        whole = pieces.reshape(peers, rows, 2, units).transpose(1, 2, 0, 3)
        return whole.reshape(rows, 2 * units * peers).astype(f32)
    return pl.pallas_call(
        partial(order_kernel, units),
        out_shape=jax.ShapeDtypeStruct((rows, 2 * units * peers), f32),
        in_specs=[in_vmem()],
        out_specs=in_vmem(),
        compiler_params=pltpu.CompilerParams(vmem_limit_bytes=30 * 1024 * 1024),
        name="order_units",
    )(pieces)


def hop(step, back):
    groups, peers = lax.axis_size("dp"), lax.axis_size("seq")
    ratio = peers // groups
    pairs = [(s, (s + step) % groups * ratio + s // groups) for s in range(peers)]
    return [(b, a) for a, b in pairs] if back else pairs


def pick(parts, index):
    return lax.dynamic_index_in_dim(parts, index, 0, keepdims=False)


def out_rows_near(rows):
    return jnp.stack([rows] + [swap(rows, "dp", k) for k in range(1, lax.axis_size("dp"))])


def out_rows_here(parts):
    groups, ratio = lax.axis_size("dp"), lax.axis_size("seq") // lax.axis_size("dp")
    place, here = lax.axis_index("dp"), lax.axis_index("seq")
    got = jnp.stack(
        [
            lax.ppermute(pick(parts, (here + t) % groups ^ place), "seq", hop(t, False))
            for t in range(groups)
        ]
    )
    return jnp.concatenate([pick(got, (here // ratio - e) % groups) for e in range(groups)])


def out_rows_sent(term):
    groups, ratio = lax.axis_size("dp"), lax.axis_size("seq") // lax.axis_size("dp")
    here = lax.axis_index("seq")
    parts = term.reshape(groups, -1, term.shape[1])
    got = jnp.stack(
        [
            lax.ppermute(pick(parts, (here // ratio - t) % groups), "seq", hop(t, True))
            for t in range(groups)
        ]
    )
    return jnp.stack([pick(got, (z - here) % groups) for z in range(groups)])


def out_rows_sum(parts):
    place = lax.axis_index("dp")
    total = pick(parts, place).astype(f32)
    for k in range(1, lax.axis_size("dp")):
        total = total + swap(pick(parts, place ^ k), "dp", k).astype(f32)
    return total


def dot32(left, right):
    return jnp.dot(left, right, preferred_element_type=f32)


def dot_t(left, right):
    return lax.dot_general(left, right, (((1,), (1,)), ((), ())), preferred_element_type=f32)


def t_dot(left, right):
    return lax.dot_general(left, right, (((0,), (0,)), ((), ())), preferred_element_type=f32)


def shards(
    tokens,
    lengths,
    norm_gain,
    mix_weight,
    conv_weight,
    decay_rate,
    out_gain,
    out_weight,
    mlp_gain,
    mlp_in_weight,
    mlp_out_weight,
    grad_out,
):
    micro, seq_rows, width = tokens.shape
    heads = decay_rate.shape[0]
    groups = lax.axis_size("dp")
    peers = lax.axis_size("seq")
    here = lax.axis_index("seq")
    local_heads = heads // peers
    taps = conv_weight.shape[0]
    units = mlp_out_weight.shape[1]
    own_units = units // peers
    own_rows = mix_weight.shape[0]
    cols = width // peers
    logit_cols = 2 * local_heads

    positions = here * seq_rows + lax.broadcasted_iota(jnp.int32, (micro, seq_rows), 1)
    valid = (positions < lengths[:, None]).astype(f32).reshape(-1, 1)
    inputs = tokens.reshape(-1, width).astype(f32)

    main = mix_weight[:, : 4 * width].reshape(own_rows, 4, peers, cols).transpose(2, 0, 1, 3)
    logits = mix_weight[:, 4 * width :].reshape(own_rows, 2, peers, local_heads)
    logits = logits.transpose(2, 0, 1, 3).reshape(peers, own_rows, logit_cols)
    mix_rows = to_columns(
        jnp.concatenate([main.reshape(peers, own_rows, 4 * cols), widen(logits)], axis=2)
    )
    wide_cols = mix_rows.shape[1]
    normed, norm_back = jax.vjp(rms_scale, inputs, norm_gain)
    normed_low, out_mine = tie(normed.astype(low), out_weight)
    out_parts = out_rows_near(out_mine)
    mix_rows, normed_low, mlp_in_rows, mlp_out_rows, out_parts = tie(
        mix_rows, normed_low, mlp_in_weight, mlp_out_weight, out_parts
    )
    gate_up = mlp_in_rows.reshape(own_rows, 2, peers, own_units).transpose(2, 0, 1, 3)
    down = mlp_out_rows.reshape(own_rows, peers, 1, own_units).transpose(1, 0, 2, 3)
    mlp_pieces = jnp.concatenate([gate_up, down], axis=2).reshape(peers, own_rows, 3 * own_units)
    mix_here = gather_dp(mix_rows)
    normed_all = gather_seq(normed_low)
    mlp_rows = to_columns(mlp_pieces)
    cotangent = valid * grad_out.reshape(-1, width).astype(f32)
    mix_here, out_parts, mlp_rows, normed_all, cot_low = tie(
        mix_here, out_parts, mlp_rows, normed_all, cotangent.astype(low)
    )
    out_here = out_rows_here(out_parts)
    in_here = gather_dp(mlp_rows[:, : 2 * own_units])
    down_here = gather_dp(mlp_rows[:, 2 * own_units :])

    projected = dot32(normed_all, mix_here).astype(low).reshape(peers, micro, seq_rows, -1)
    conv_here = lax.dynamic_index_in_dim(
        conv_weight.reshape(taps, 3, peers, cols), here, 2, keepdims=False
    ).reshape(taps, 3 * cols)
    rates_here = lax.dynamic_slice_in_dim(decay_rate, here * local_heads, local_heads)
    rate_lanes = jnp.pad(rates_here, (0, LANES - local_heads)).reshape(1, LANES)
    gain_row = out_gain.reshape(1, LANES)
    places = gather_places()
    mixed, *kept = heads_forward(
        places, projected, conv_here, rate_lanes, gain_row, local_heads
    )
    mixed, cot_low = tie(mixed, cot_low)
    mixed_low = mixed.reshape(-1, cols)
    branch, in_here = scatter_seq(dot32(mixed_low, out_here), (in_here,))
    hidden = inputs + branch

    second, second_back = jax.vjp(rms_scale, hidden, mlp_gain)
    second_all = gather_seq(second.astype(low))
    cot_all = gather_seq(cot_low)
    gate_up = dot32(second_all, in_here).astype(low)
    activated, swiglu_back = jax.vjp(swiglu, gate_up.astype(f32))
    activated_low = activated.astype(low)
    grad_down_term = t_dot(cot_all, activated_low).astype(low)
    cot_all, grad_down_term, down_here = tie(cot_all, grad_down_term, down_here)
    (grad_gate_up,) = swiglu_back(dot32(cot_all, down_here))
    grad_gate_low = grad_gate_up.astype(low)
    grad_second = scatter_seq(dot_t(grad_gate_low, in_here))
    grad_hidden_norm, grad_mlp_gain = second_back(grad_second)
    grad_hidden = cotangent + grad_hidden_norm
    branch_low = grad_hidden.astype(low)
    branch_all = gather_seq(branch_low)
    grad_down = sum_dp(grad_down_term)
    grad_in = sum_dp(t_dot(second_all, grad_gate_low))

    branch_all, activated_low = tie(branch_all, activated_low)
    grad_mixed = dot_t(branch_all, out_here).reshape(peers, micro, seq_rows, cols)
    grad_mixed, grad_down = tie(grad_mixed, grad_down)
    grad_projected, grad_conv, rate_sums, gain_sums = (
        heads_backward(
            places,
            grad_mixed,
            projected,
            conv_here,
            rate_lanes,
            gain_row,
            kept,
            local_heads,
        )
    )
    grad_projected = grad_projected.reshape(-1, wide_cols)
    grad_mix_term = t_dot(normed_all, grad_projected).astype(low)
    grad_mix_term, grad_projected = tie(grad_mix_term, grad_projected)
    mix_own = sum_dp(grad_mix_term)
    grad_normed, grad_in, mixed_low = scatter_seq(
        dot_t(grad_projected, mix_here), (to_owners(grad_in), mixed_low)
    )
    grad_down = to_owners(grad_down)
    out_parts = out_rows_sent(t_dot(mixed_low, branch_all).astype(low))
    grad_inputs_norm, grad_norm_gain = norm_back(grad_normed)
    grad_tokens = grad_hidden + grad_inputs_norm
    feed_out = scatter_seq(dot_t(activated_low, down_here))
    result = (valid * (hidden + feed_out)).astype(low)

    conv_terms = lax.dynamic_update_slice(
        jnp.zeros((taps, 3, peers, cols), f32),
        grad_conv.reshape(taps, 3, 1, cols),
        (0, 0, here, 0),
    )
    rate_terms = lax.dynamic_update_slice(
        jnp.zeros((LANES,), f32), rate_sums[0, :local_heads], (here * local_heads,)
    )
    sizes = [width, width, LANES, LANES, taps * 3 * width]
    summed = sum_all(
        jnp.concatenate(
            [
                grad_norm_gain,
                grad_mlp_gain,
                gain_sums[0],
                rate_terms,
                conv_terms.reshape(-1),
            ]
        ).reshape(-1, LANES)
    ).reshape(-1)
    mix_own, out_parts, summed, grad_in, grad_down = tie(
        mix_own, out_parts, summed, grad_in, grad_down
    )
    grad_mix = to_owners(mix_own)
    grad_out_own = out_rows_sum(out_parts)
    grad_in = order_units(grad_in, own_units)
    grad_down = grad_down.transpose(1, 0, 2).reshape(own_rows, units).astype(f32)
    ends = [sum(sizes[: i + 1]) for i in range(len(sizes))]
    sums = [summed[end - size : end] for end, size in zip(ends, sizes)]
    return (
        result.reshape(tokens.shape),
        grad_tokens.reshape(tokens.shape),
        sums[0],
        assemble(grad_mix, local_heads),
        sums[4].reshape(taps, 3 * width),
        sums[3][:heads],
        sums[2],
        grad_out_own,
        sums[1],
        grad_in,
        grad_down,
    )


def solution(mesh):
    in_specs = (
        P("dp", "seq", None),
        P("dp"),
        P(),
        P(("dp", "seq"), None),
        P(),
        P(),
        P(),
        P(("dp", "seq"), None),
        P(),
        P(("dp", "seq"), None),
        P(("dp", "seq"), None),
        P("dp", "seq", None),
    )
    out_specs = (
        P("dp", "seq", None),
        P("dp", "seq", None),
        P(),
        P(("dp", "seq"), None),
        P(),
        P(),
        P(),
        P(("dp", "seq"), None),
        P(),
        P(("dp", "seq"), None),
        P(("dp", "seq"), None),
    )
    return jax.shard_map(shards, mesh=mesh, in_specs=in_specs, out_specs=out_specs, check_vma=False)
```

```python
from functools import partial

import jax
import jax.numpy as jnp
from jax import lax
from jax.experimental import pallas as pl
from jax.experimental.pallas import tpu as pltpu
from jax.sharding import PartitionSpec as P

eps_norm = 1e-05
eps_key = 1e-06
LANES = 128
PAIR = 2
f32 = jnp.float32
low = jnp.bfloat16


def rms_scale(rows_in, gain):
    return (
        rows_in * lax.rsqrt(jnp.mean(rows_in * rows_in, axis=-1, keepdims=True) + eps_norm) * gain
    )


def swiglu(gate_up):
    hidden_units = gate_up.shape[-1] // 2
    return jax.nn.silu(gate_up[..., :hidden_units]) * gate_up[..., hidden_units:]


def mm(left, right):
    return jnp.dot(left.astype(low), right.astype(low), preferred_element_type=f32)


def mm_nt(left, right):
    return lax.dot_general(
        left.astype(low), right.astype(low), (((1,), (1,)), ((), ())), preferred_element_type=f32
    )


def halves(v):
    if isinstance(v, tuple):
        return v
    if v.dtype == low:
        return (v,)
    top = v.astype(low)
    return top, (v - top.astype(f32)).astype(low)


def dot_fine(left, right, dims):
    left, right = halves(left), halves(right)
    total = None
    for i, a in enumerate(left):
        for j, b in enumerate(right):
            if i + j < 2:
                term = lax.dot_general(a, b, (dims, ((), ())), preferred_element_type=f32)
                total = term if total is None else total + term
    return total


def fine(left, right):
    return dot_fine(left, right, ((1,), (0,)))


def fine_nt(left, right):
    return dot_fine(left, right, ((1,), (1,)))


def mm_exact(left, right):
    return jnp.dot(left, right, precision=lax.Precision.HIGHEST, preferred_element_type=f32)


def softplus(v):
    return jnp.maximum(v, 0.0) + jnp.log1p(jnp.exp(-jnp.abs(v)))


def grid_of(size):
    row = lax.broadcasted_iota(jnp.int32, (size, size), 0)
    col = lax.broadcasted_iota(jnp.int32, (size, size), 1)
    return row, col


def lower_inverses(parts, row, col):
    size = parts[0].shape[0]
    joined = (row // 2 == col // 2) & (row > col)
    unit = (row == col).astype(f32)
    inverses = [unit - jnp.where(joined, part, 0.0) for part in parts]
    width = 2
    while width < size:
        joined = (row // (2 * width) == col // (2 * width)) & (row // width > col // width)
        corners = [jnp.where(joined, part, 0.0) for part in parts]
        moved = [mm(corner, inverse) for corner, inverse in zip(corners, inverses)]
        steps = [mm(inverse, move) for inverse, move in zip(inverses, moved)]
        inverses = [inverse - change for inverse, change in zip(inverses, steps)]
        width *= 2
    return inverses


def fill_taps(ext, slot, proj, pos, prev, first, qkv):
    rows = proj.shape[2]
    ext[slot, 8 : 8 + rows, :] = proj[*pos, :, :qkv].astype(f32)
    tail = proj[*prev, rows - 16 :, :qkv].astype(f32)[8:]
    ext[slot, 0:8, :] = jnp.where(first, 0.0, tail)


def conv_rows(ext, m, conv, rows):
    taps = conv.shape[0]
    total = conv[0:1, :] * ext[m, 9 - taps : 9 - taps + rows, :]
    for j in range(1, taps):
        total = total + conv[j : j + 1, :] * ext[m, 9 - taps + j : 9 - taps + j + rows, :]
    return total


def forward_kernel(
    local_heads,
    blocks,
    perm,
    proj,
    conv,
    rates,
    gain,
    mixed,
    heads_out,
    qkv_out,
    gates,
    inv_t,
    weighted_t,
    fresh,
    states,
    ext,
    targets,
    weighted,
    scores,
    keys_t,
    state,
):
    _, micro, rows, _ = proj.shape
    cols = local_heads * LANES
    qkv = 3 * cols
    row, col = grid_of(rows)
    upto = (row >= col).astype(f32)
    lane = lax.broadcasted_iota(jnp.int32, (rows, LANES), 1)
    scale = float(LANES) ** -0.5

    def prepare(i, carry):
        work = []
        for part in range(PAIR):
            b = i * PAIR + part
            for m in range(micro):
                slot = part * micro + m
                pos, prev = (perm[b], m), (perm[jnp.maximum(b - 1, 0)], m)
                fill_taps(ext, slot, proj, pos, prev, b == 0, qkv)
                conv_out = conv_rows(ext, slot, conv, rows)
                act = conv_out * jax.nn.sigmoid(conv_out)
                logits = proj[*pos, :, 4 * cols :].astype(f32)
                decay = -rates[...] * softplus(logits)
                strength = jax.nn.sigmoid(logits)
                total = mm_exact(upto, decay)
                total_t = total.T
                gates[b, m] = jnp.where(lane < local_heads, total, strength)
                growth = jnp.exp(total)
                fade = jnp.exp(total[rows - 1 : rows, :] - total)
                for h in range(local_heads):
                    raw_q = act[:, h * LANES : (h + 1) * LANES]
                    raw_k = act[:, cols + h * LANES : cols + (h + 1) * LANES]
                    q = raw_q * (
                        lax.rsqrt(jnp.sum(raw_q * raw_q, axis=1, keepdims=True) + eps_key) * scale
                    )
                    k = raw_k * lax.rsqrt(jnp.sum(raw_k * raw_k, axis=1, keepdims=True) + eps_key)
                    q = q.astype(low)
                    k = k.astype(low)
                    v = act[:, 2 * cols + h * LANES : 2 * cols + (h + 1) * LANES].astype(low)
                    qkv_out[b, m, :, h * LANES : (h + 1) * LANES] = q
                    qkv_out[b, m, :, cols + h * LANES : cols + (h + 1) * LANES] = k
                    qkv_out[b, m, :, 2 * cols + h * LANES : 2 * cols + (h + 1) * LANES] = v
                    beta = strength[:, local_heads + h : local_heads + h + 1]
                    spread = jnp.exp(
                        jnp.minimum(total[:, h : h + 1] - total_t[h : h + 1, :], 0.0)
                    )
                    work.append(
                        (b, m * local_heads + h, q, k, v, beta, spread, growth[:, h : h + 1], fade[:, h : h + 1])
                    )
        same = [mm_nt(k, k) for _, _, _, k, *_ in work]
        cross = [mm_nt(q, k) for _, _, q, k, *_ in work]
        parts = [
            jnp.where(row > col, item[6] * item[5] * dots, 0.0) for item, dots in zip(work, same)
        ]
        inverses = lower_inverses(parts, row, col)
        keyed = [fine(inv, item[3].astype(f32) * (item[5] * item[7])) for inv, item in zip(inverses, work)]
        valued = [fine(inv, item[4].astype(f32) * item[5]) for inv, item in zip(inverses, work)]
        for n, (b, p, q, k, v, beta, spread, grow, shrink) in enumerate(work):
            inv_t[b, p] = inverses[n].T
            weighted[b, p] = keyed[n]
            weighted_t[b, p] = keyed[n].T
            targets[b, p] = valued[n]
            scores[b, p] = upto * spread * cross[n]
            keys_t[b, p] = (k.astype(f32) * shrink).T
        return carry

    lax.fori_loop(0, blocks // PAIR, prepare, 0)
    state[...] = jnp.zeros_like(state)

    def step(b, carry):
        growth = [jnp.exp(gates[b, m]) for m in range(micro)]
        chains = [(m, h, m * local_heads + h) for m in range(micro) for h in range(local_heads)]
        now = [state[p] for _, _, p in chains]
        now_halves = [halves(v) for v in now]
        new = [
            targets[b, p] - fine(weighted[b, p], parts) for (_, _, p), parts in zip(chains, now_halves)
        ]
        new_halves = [halves(v) for v in new]
        moved = [fine(keys_t[b, p], parts) for (_, _, p), parts in zip(chains, new_halves)]
        for (m, h, p), old, fed in zip(chains, now, moved):
            states[b, p] = old
            state[p] = growth[m][rows - 1 : rows, h : h + 1] * old + fed
        outs = []
        for (m, h, p), fill, parts in zip(chains, new_halves, now_halves):
            q = qkv_out[b, m, :, h * LANES : (h + 1) * LANES].astype(f32)
            outs.append(fine(q * growth[m][:, h : h + 1], parts) + fine(scores[b, p], fill))
        for (m, h, p), fill, out in zip(chains, new, outs):
            fresh[b, p] = fill
            out = out.astype(low)
            heads_out[b, m, :, h * LANES : (h + 1) * LANES] = out
            out = out.astype(f32)
            pos = (perm[b], m)
            gate = proj[*pos, :, 3 * cols + h * LANES : 3 * cols + (h + 1) * LANES].astype(f32)
            normed = out * lax.rsqrt(jnp.mean(out * out, axis=1, keepdims=True) + eps_norm) * gain[...]
            done = (normed * (gate * jax.nn.sigmoid(gate))).astype(low)
            mixed[*pos, :, h * LANES : (h + 1) * LANES] = done
        return carry

    lax.fori_loop(0, blocks, step, 0)


def backward_kernel(
    local_heads,
    blocks,
    perm,
    grad_mixed,
    proj,
    conv,
    rates,
    gain,
    heads_out,
    qkv_in,
    gates,
    inv_t,
    weighted_t,
    fresh,
    states,
    grad_proj,
    grad_conv,
    grad_rates,
    grad_gain,
    ext,
    dext,
    ahead,
    conv_sum,
    grad_out,
    value_part,
    state_part,
    grad_fresh,
    grad_states,
    grad_state,
):
    _, micro, rows, _ = proj.shape
    cols = local_heads * LANES
    qkv = 3 * cols
    taps = conv.shape[0]
    row, col = grid_of(rows)
    lane = lax.broadcasted_iota(jnp.int32, (rows, LANES), 1)
    last = lax.broadcasted_iota(jnp.int32, (rows, 1), 0) == rows - 1
    scale = float(LANES) ** -0.5
    upto_t = (col >= row).astype(f32)
    grad_gain[...] = jnp.zeros_like(grad_gain)
    grad_rates[...] = jnp.zeros_like(grad_rates)
    conv_sum[...] = jnp.zeros_like(conv_sum)
    ahead[...] = jnp.zeros_like(ahead)
    grad_state[...] = jnp.zeros_like(grad_state)

    def prepare(b, carry):
        work = []
        for m in range(micro):
            pos = (perm[b], m)
            total = gates[b, m]
            growth = jnp.exp(total)
            total_t = total.T
            for h in range(local_heads):
                p = m * local_heads + h
                here = slice(h * LANES, (h + 1) * LANES)
                out = heads_out[b, m, :, here].astype(f32)
                gate = proj[*pos, :, 3 * cols + h * LANES : 3 * cols + (h + 1) * LANES].astype(f32)
                dmixed = grad_mixed[*pos, :, here].astype(f32)
                root = lax.rsqrt(jnp.mean(out * out, axis=1, keepdims=True) + eps_norm)
                unit = out * root
                sig = jax.nn.sigmoid(gate)
                dnormed = dmixed * (gate * sig)
                dgate = dmixed * (unit * gain[...]) * (sig * (1.0 + gate * (1.0 - sig)))
                at = slice(3 * cols + h * LANES, 3 * cols + (h + 1) * LANES)
                grad_proj[*pos, :, at] = dgate.astype(low)
                grad_gain[...] += jnp.sum(dnormed * unit, axis=0, keepdims=True)
                dunit = dnormed * gain[...]
                dout = root * (dunit - unit * jnp.mean(unit * dunit, axis=1, keepdims=True))
                dout = dout.astype(low)
                grad_out[b, p] = dout.astype(grad_out.dtype)
                q = qkv_in[b, m, :, here]
                k = qkv_in[b, m, :, cols + h * LANES : cols + (h + 1) * LANES]
                spread_t = jnp.exp(jnp.minimum(total_t[h : h + 1, :] - total[:, h : h + 1], 0.0))
                grown_t = (q.astype(f32) * growth[:, h : h + 1]).T
                work.append((p, q, k, dout, upto_t * spread_t, grown_t))
        dots = [mm_nt(k, q) for _, q, k, *_ in work]
        parts = [fine(spread * dot, dout) for (_, _, _, dout, spread, _), dot in zip(work, dots)]
        fed = [fine(grown_t, dout) for _, _, _, dout, _, grown_t in work]
        for (p, *_), part, feed in zip(work, parts, fed):
            value_part[b, p] = part
            state_part[b, p] = feed
        return carry

    lax.fori_loop(0, blocks, prepare, 0)

    def step(i, carry):
        b = blocks - 1 - i
        chains = [(m, h, m * local_heads + h) for m in range(micro) for h in range(local_heads)]
        total = [gates[b, m] for m in range(micro)]
        fade = [jnp.exp(v[rows - 1 : rows, :] - v) for v in total]
        later = [grad_state[p] for _, _, p in chains]
        dnew = []
        for (m, h, p), grad in zip(chains, later):
            k = qkv_in[b, m, :, cols + h * LANES : cols + (h + 1) * LANES].astype(f32)
            dnew.append(value_part[b, p] + fine(k * fade[m][:, h : h + 1], grad))
        moved = [fine(weighted_t[b, p], grad) for (_, _, p), grad in zip(chains, dnew)]
        for (m, h, p), grad, fill, move in zip(chains, later, dnew, moved):
            grad_states[b, p] = grad
            grad_fresh[b, p] = fill
            carried = jnp.exp(total[m][rows - 1 : rows, h : h + 1])
            grad_state[p] = state_part[b, p] + carried * grad - move
        return carry

    lax.fori_loop(0, blocks, step, 0)

    def finish(i, carry):
        b = blocks - 1 - i
        work = []
        for m in range(micro):
            total = gates[b, m]
            total_t = total.T
            growth = jnp.exp(total)
            fade = jnp.exp(total[rows - 1 : rows, :] - total)
            for h in range(local_heads):
                p = m * local_heads + h
                q = qkv_in[b, m, :, h * LANES : (h + 1) * LANES]
                k = qkv_in[b, m, :, cols + h * LANES : cols + (h + 1) * LANES]
                v = qkv_in[b, m, :, 2 * cols + h * LANES : 2 * cols + (h + 1) * LANES]
                beta = total[:, local_heads + h : local_heads + h + 1]
                spread = jnp.exp(jnp.minimum(total[:, h : h + 1] - total_t[h : h + 1, :], 0.0))
                work.append(
                    (p, q, k, v, beta, spread, growth[:, h : h + 1], fade[:, h : h + 1], growth[rows - 1 : rows, h : h + 1])
                )
        number = range(len(work))
        queries = [item[1] for item in work]
        keys = [item[2] for item in work]
        douts = [grad_out[b, item[0]].astype(low) for item in work]
        news = [halves(fresh[b, item[0]]) for item in work]
        nows = [halves(states[b, item[0]]) for item in work]
        laters = [halves(grad_states[b, item[0]]) for item in work]
        dright = [fine(inv_t[b, item[0]], grad_fresh[b, item[0]]) for item in work]
        dgrown = [fine_nt(douts[n], nows[n]) for n in number]
        dshrunk = [fine_nt(news[n], laters[n]) for n in number]
        dots = [mm_nt(queries[n], keys[n]) for n in number]
        same = [mm_nt(keys[n], keys[n]) for n in number]
        dscores = [fine_nt(douts[n], news[n]) for n in number]
        dright_halves = [halves(v) for v in dright]
        dweighted = [-fine_nt(dright_halves[n], nows[n]) for n in number]
        dbelow = [fine_nt(dright_halves[n], news[n]) for n in number]
        keyed, moved = [], []
        for n in number:
            beta, spread = work[n][4], work[n][5]
            dscores[n] = dscores[n] * jnp.where(row >= col, spread, 0.0)
            dbelow[n] = dbelow[n] * jnp.where(row > col, -spread, 0.0)
            keyed.append(dbelow[n] * same[n])
            moved.append(dscores[n] * dots[n] + keyed[n] * beta)
            dbelow[n] = dbelow[n] * beta
        dq = [fine(dscores[n], keys[n]) for n in number]
        dk = [fine(dscores[n].T, queries[n]) for n in number]
        dk_same = [fine(dbelow[n] + dbelow[n].T, keys[n]) for n in number]
        for m in range(micro):
            pos, prev = (perm[b], m), (perm[jnp.maximum(b - 1, 0)], m)
            fill_taps(ext, m, proj, pos, prev, b == 0, qkv)
            conv_out = conv_rows(ext, m, conv, rows)
            sig = jax.nn.sigmoid(conv_out)
            act = conv_out * sig
            slope = sig * (1.0 + conv_out * (1.0 - sig))
            dtotal = jnp.zeros((rows, LANES), f32)
            dstrength = jnp.zeros((rows, LANES), f32)
            for h in range(local_heads):
                n = m * local_heads + h
                p, q, k, v, beta, spread, grow, shrink, carried = work[n]
                q32, k32, v32 = q.astype(f32), k.astype(f32), v.astype(f32)
                dquery = grow * dgrown[n] + dq[n]
                dkey = (beta * grow) * dweighted[n] + shrink * dshrunk[n] + dk[n] + dk_same[n]
                dvalue = beta * dright[n]
                weighed = dweighted[n] * k32 * grow
                shrunk = dshrunk[n] * k32 * shrink
                dstr = jnp.sum(dright[n] * v32 + weighed, axis=1, keepdims=True) + jnp.sum(
                    keyed[n], axis=1, keepdims=True
                )
                dtot = jnp.sum(
                    dgrown[n] * q32 * grow + weighed * beta - shrunk, axis=1, keepdims=True
                ) + jnp.sum(moved[n] - moved[n].T, axis=1, keepdims=True)
                end = jnp.sum(shrunk) + jnp.sum(carried * (states[b, p] * grad_states[b, p]))
                dtot = dtot + jnp.where(last, end, 0.0)
                dtotal = dtotal + jnp.where(lane == h, dtot, 0.0)
                dstrength = dstrength + jnp.where(lane == local_heads + h, dstr, 0.0)
                for part, grad in ((0, dquery), (1, dkey), (2, dvalue)):
                    at = part * cols + h * LANES
                    grad = grad.astype(low).astype(f32)
                    if part == 0:
                        grad = grad * scale
                    if part < 2:
                        raw = act[:, at : at + LANES]
                        root = lax.rsqrt(jnp.sum(raw * raw, axis=1, keepdims=True) + eps_key)
                        unit = raw * root
                        grad = root * (grad - unit * jnp.sum(unit * grad, axis=1, keepdims=True))
                    dext[m, 0:rows, at : at + LANES] = grad * slope[:, at : at + LANES]
            dext[m, rows : rows + 8, :] = ahead[m]
            dconv = dext[m, 0:rows, :]
            ahead[m] = dconv[0:8, :]
            du = conv[taps - 1 : taps, :] * dconv
            for j in range(taps - 1):
                du = du + conv[j : j + 1, :] * dext[m, taps - 1 - j : taps - 1 - j + rows, :]
            grad_proj[*pos, :, :qkv] = du.astype(low)
            for j in range(taps):
                term = dconv * ext[m, 9 - taps + j : 9 - taps + j + rows, :]
                conv_sum[j] += jnp.sum(term.reshape(rows // 8, 8, qkv), axis=0)
            logits = proj[*pos, :, 4 * cols :].astype(f32)
            ddecay = mm_exact(upto_t, dtotal)
            strength = gates[b, m]
            dlogit = jnp.where(
                lane < local_heads,
                -rates[...] * jax.nn.sigmoid(logits) * ddecay,
                strength * (1.0 - strength) * dstrength,
            )
            dlogit = jnp.where(lane < 2 * local_heads, dlogit, 0.0).astype(low)
            grad_proj[*pos, :, 4 * cols :] = dlogit
            grad_rates[...] -= jnp.sum(softplus(logits) * ddecay, axis=0, keepdims=True)
        return carry

    lax.fori_loop(0, blocks, finish, 0)
    for j in range(taps):
        grad_conv[j : j + 1, :] = jnp.sum(conv_sum[j], axis=0, keepdims=True)


def in_vmem():
    return pl.BlockSpec(memory_space=pltpu.VMEM)


def heads_forward(perm, proj, conv, rates, gain, local_heads):
    blocks, micro, rows, _ = proj.shape
    cols = local_heads * LANES
    chains = micro * local_heads

    def shape(dims, kind):
        return jax.ShapeDtypeStruct(dims, kind)

    return pl.pallas_call(
        partial(forward_kernel, local_heads, perm.shape[0]),
        out_shape=(
            shape((blocks, micro, rows, cols), low),
            shape((blocks, micro, rows, cols), low),
            shape((blocks, micro, rows, 3 * cols), low),
            shape((blocks, micro, rows, LANES), f32),
            shape((blocks, chains, rows, rows), f32),
            shape((blocks, chains, LANES, rows), f32),
            shape((blocks, chains, rows, LANES), f32),
            shape((blocks, chains, LANES, LANES), f32),
        ),
        in_specs=[pl.BlockSpec(memory_space=pltpu.SMEM)] + [in_vmem()] * 4,
        out_specs=(in_vmem(),) * 8,
        scratch_shapes=[
            pltpu.VMEM((PAIR * micro, rows + 8, 3 * cols), f32),
            pltpu.VMEM((blocks, chains, rows, LANES), f32),
            pltpu.VMEM((blocks, chains, rows, LANES), f32),
            pltpu.VMEM((blocks, chains, rows, rows), f32),
            pltpu.VMEM((blocks, chains, LANES, rows), f32),
            pltpu.VMEM((chains, LANES, LANES), f32),
        ],
        compiler_params=pltpu.CompilerParams(vmem_limit_bytes=50 * 1024 * 1024),
        name="heads_forward",
    )(perm, proj, conv, rates, gain)


def heads_backward(perm, grad_mixed, proj, conv, rates, gain, kept, local_heads):
    blocks, micro, rows, wide = proj.shape
    cols = local_heads * LANES
    chains = micro * local_heads
    taps = conv.shape[0]

    def shape(dims, kind):
        return jax.ShapeDtypeStruct(dims, kind)

    return pl.pallas_call(
        partial(backward_kernel, local_heads, perm.shape[0]),
        out_shape=(
            shape((blocks, micro, rows, wide), low),
            shape((taps, 3 * cols), f32),
            shape((1, LANES), f32),
            shape((1, LANES), f32),
        ),
        in_specs=[pl.BlockSpec(memory_space=pltpu.SMEM)] + [in_vmem()] * 12,
        out_specs=(in_vmem(),) * 4,
        scratch_shapes=[
            pltpu.VMEM((micro, rows + 8, 3 * cols), f32),
            pltpu.VMEM((micro, rows + 8, 3 * cols), f32),
            pltpu.VMEM((micro, 8, 3 * cols), f32),
            pltpu.VMEM((taps, 8, 3 * cols), f32),
            pltpu.VMEM((blocks, chains, rows, LANES), f32),
            pltpu.VMEM((blocks, chains, rows, LANES), f32),
            pltpu.VMEM((blocks, chains, LANES, LANES), f32),
            pltpu.VMEM((blocks, chains, rows, LANES), f32),
            pltpu.VMEM((blocks, chains, LANES, LANES), f32),
            pltpu.VMEM((chains, LANES, LANES), f32),
        ],
        compiler_params=pltpu.CompilerParams(vmem_limit_bytes=50 * 1024 * 1024),
        name="heads_backward",
    )(perm, grad_mixed, proj, conv, rates, gain, *kept)


both = ("dp", "seq")


def swap(value, axis, bit):
    return lax.ppermute(value, axis, [(i, i ^ bit) for i in range(lax.axis_size(axis))])


def tie(*values):
    return lax.optimization_barrier(values)


def gather_places():
    peers = lax.axis_size("seq")
    place = jnp.arange(peers, dtype=jnp.int32)
    if peers != 8:
        return place
    place = place ^ lax.axis_index("seq").astype(jnp.int32)
    return place // 2 + 4 * (place % 2)


def gather_seq(rows_in):
    if lax.axis_size("seq") != 8:
        return lax.all_gather(rows_in, "seq", axis=0, tiled=True)
    half = rows_in.shape[0] // 2
    top, bottom = rows_in[:half], rows_in[half:]
    top_x, bottom_y = swap(top, "seq", 2), swap(bottom, "seq", 4)
    top_y = swap(jnp.concatenate([top, top_x]), "seq", 4)
    bottom_x = swap(jnp.concatenate([bottom, bottom_y]), "seq", 2)
    near = jnp.concatenate(
        [top, bottom, top_x, bottom_x[:half], top_y[:half], bottom_y, top_y[half:], bottom_x[half:]]
    )
    return jnp.concatenate([near, swap(near, "seq", 1)])


def scatter_seq(partial_rows, beside=None):
    peers = lax.axis_size("seq")
    if peers != 8:
        total = lax.psum_scatter(
            partial_rows.astype(low), "seq", scatter_dimension=0, tiled=True
        ).astype(f32)
        return total if beside is None else (total, *beside)
    terms = partial_rows.astype(low).reshape(peers, -1, partial_rows.shape[-1])
    half = terms.shape[1] // 2
    near = terms[:4].astype(f32) + swap(terms[4:], "seq", 1).astype(f32)
    top, bottom = near[:, :half].astype(low), near[:, half:].astype(low)
    top_x = swap(top[1::2], "seq", 2)
    bottom_y = swap(bottom[2:], "seq", 4)
    top = near[0::2, :half] + top_x.astype(f32)
    bottom = near[:2, half:] + bottom_y.astype(f32)
    if beside is not None:
        top, bottom, *beside = tie(top, bottom, *beside)
    top_y = swap(top[1].astype(low), "seq", 4)
    bottom_x = swap(bottom[1].astype(low), "seq", 2)
    total = jnp.concatenate([top[0] + top_y.astype(f32), bottom[0] + bottom_x.astype(f32)])
    return total if beside is None else (total, *beside)


def sum_all(value):
    for axis in both:
        size, bit = lax.axis_size(axis), 1
        if size.bit_length() % 2 == 0:
            value, bit = value + swap(value, axis, 1), 2
        while bit < size:
            one, two, three = (swap(value, axis, k * bit) for k in (1, 2, 3))
            value, bit = (value + one) + (two + three), 4 * bit
    return value


def to_columns(pieces):
    rows_here = lax.all_to_all(pieces, "seq", split_axis=0, concat_axis=0, tiled=True)
    return rows_here.reshape(-1, pieces.shape[-1])


def gather_dp(rows_here):
    return lax.all_gather(rows_here, "dp", axis=0, tiled=True)


def sum_dp(term):
    return lax.psum_scatter(term.astype(low), "dp", scatter_dimension=0, tiled=True)


def to_owners(own):
    pieces = own.reshape(lax.axis_size("seq"), -1, own.shape[1])
    return lax.all_to_all(pieces, "seq", split_axis=0, concat_axis=0, tiled=True)


def widen(columns):
    extra = -columns.shape[-1] % LANES
    return jnp.pad(columns, [(0, 0)] * (columns.ndim - 1) + [(0, extra)])


def assemble_kernel(local_heads, pieces, whole):
    peers, _, wide = pieces.shape
    cols = (wide - LANES) // 4
    width = cols * peers
    logits = []
    for part in range(5):
        for j in range(peers):
            from_here = slice(part * cols, min((part + 1) * cols, wide))
            total = pieces[j, :, from_here].astype(f32)
            if part < 4:
                whole[:, part * width + j * cols : part * width + (j + 1) * cols] = total
            else:
                logits.append(total)
    for kind in range(2):
        here = slice(kind * local_heads, (kind + 1) * local_heads)
        for j in range(peers):
            at = 4 * width + kind * local_heads * peers + j * local_heads
            whole[:, at : at + local_heads] = logits[j][:, here]


def assemble(pieces, local_heads):
    peers, rows, wide = pieces.shape
    total = (wide - LANES) * peers + 2 * local_heads * peers
    return pl.pallas_call(
        partial(assemble_kernel, local_heads),
        out_shape=jax.ShapeDtypeStruct((rows, total), f32),
        in_specs=[in_vmem()],
        out_specs=in_vmem(),
        compiler_params=pltpu.CompilerParams(vmem_limit_bytes=30 * 1024 * 1024),
        name="assemble",
    )(pieces)


def order_kernel(units, pieces, whole):
    peers, rows, _ = pieces.shape
    wide = units + LANES // 2
    middle = lax.broadcasted_iota(jnp.int32, (rows, LANES), 1) < LANES // 2
    for kind in range(2):
        for j in range(0, peers, 2):
            if kind == 0:
                one = pieces[j, :, :wide].astype(f32)
                two = pltpu.roll(pieces[j + 1, :, :wide].astype(f32), LANES // 2, axis=1)
            else:
                start = 2 * units - wide
                one = pltpu.roll(pieces[j, :, start:].astype(f32), wide - LANES // 2, axis=1)
                two = pieces[j + 1, :, start:].astype(f32)
            at = (kind * peers + j) * units
            whole[:, at : at + wide - LANES] = one[:, : wide - LANES]
            at = at + wide - LANES
            whole[:, at : at + LANES] = jnp.where(middle, one[:, wide - LANES :], two[:, :LANES])
            at = at + LANES
            whole[:, at : at + wide - LANES] = two[:, LANES:]


def order_units(pieces, units):
    peers, rows, _ = pieces.shape
    if units % LANES != LANES // 2 or peers % 2 != 0:
        whole = pieces.reshape(peers, rows, 2, units).transpose(1, 2, 0, 3)
        return whole.reshape(rows, 2 * units * peers).astype(f32)
    return pl.pallas_call(
        partial(order_kernel, units),
        out_shape=jax.ShapeDtypeStruct((rows, 2 * units * peers), f32),
        in_specs=[in_vmem()],
        out_specs=in_vmem(),
        compiler_params=pltpu.CompilerParams(vmem_limit_bytes=30 * 1024 * 1024),
        name="order_units",
    )(pieces)


def pack_rows(blocks, logit_cols):
    rows, cols = blocks.shape[1], blocks.shape[2] - LANES
    below = blocks[:, :, cols : cols + logit_cols].swapaxes(1, 2)
    below = jnp.pad(below, ((0, 0), (0, 16 - logit_cols), (0, cols - rows)))
    return jnp.concatenate([blocks[:, :, :cols], below], axis=1).reshape(-1, cols)


def unpack_rows(packed, count):
    blocks = packed.reshape(count, -1, packed.shape[1])
    rows = blocks.shape[1] - 16
    logits = blocks[:, rows:, :rows].swapaxes(1, 2)
    logits = jnp.pad(logits, ((0, 0), (0, 0), (0, LANES - 16)))
    blocks = jnp.concatenate([blocks[:, :rows], logits], axis=2)
    return blocks.reshape(-1, blocks.shape[2])


def hop(step, back):
    groups, peers = lax.axis_size("dp"), lax.axis_size("seq")
    ratio = peers // groups
    pairs = [(s, (s + step) % groups * ratio + s // groups) for s in range(peers)]
    return [(b, a) for a, b in pairs] if back else pairs


def pick(parts, index):
    return lax.dynamic_index_in_dim(parts, index, 0, keepdims=False)


def out_rows_near(rows):
    return jnp.stack([rows] + [swap(rows, "dp", k) for k in range(1, lax.axis_size("dp"))])


def out_rows_here(parts):
    groups, ratio = lax.axis_size("dp"), lax.axis_size("seq") // lax.axis_size("dp")
    place, here = lax.axis_index("dp"), lax.axis_index("seq")
    got = jnp.stack(
        [
            lax.ppermute(pick(parts, (here + t) % groups ^ place), "seq", hop(t, False))
            for t in range(groups)
        ]
    )
    return jnp.concatenate([pick(got, (here // ratio - e) % groups) for e in range(groups)])


def out_rows_sent(term):
    groups, ratio = lax.axis_size("dp"), lax.axis_size("seq") // lax.axis_size("dp")
    here = lax.axis_index("seq")
    parts = term.reshape(groups, -1, term.shape[1])
    got = jnp.stack(
        [
            lax.ppermute(pick(parts, (here // ratio - t) % groups), "seq", hop(t, True))
            for t in range(groups)
        ]
    )
    return jnp.stack([pick(got, (z - here) % groups) for z in range(groups)])


def out_rows_sum(parts):
    place = lax.axis_index("dp")
    total = pick(parts, place).astype(f32)
    for k in range(1, lax.axis_size("dp")):
        total = total + swap(pick(parts, place ^ k), "dp", k).astype(f32)
    return total


def dot32(left, right):
    return jnp.dot(left, right, preferred_element_type=f32)


def dot_t(left, right):
    return lax.dot_general(left, right, (((1,), (1,)), ((), ())), preferred_element_type=f32)


def t_dot(left, right):
    return lax.dot_general(left, right, (((0,), (0,)), ((), ())), preferred_element_type=f32)


def shards(
    tokens,
    lengths,
    norm_gain,
    mix_weight,
    conv_weight,
    decay_rate,
    out_gain,
    out_weight,
    mlp_gain,
    mlp_in_weight,
    mlp_out_weight,
    grad_out,
):
    micro, seq_rows, width = tokens.shape
    heads = decay_rate.shape[0]
    groups = lax.axis_size("dp")
    peers = lax.axis_size("seq")
    here = lax.axis_index("seq")
    local_heads = heads // peers
    taps = conv_weight.shape[0]
    units = mlp_out_weight.shape[1]
    own_units = units // peers
    own_rows = mix_weight.shape[0]
    cols = width // peers
    logit_cols = 2 * local_heads

    positions = here * seq_rows + lax.broadcasted_iota(jnp.int32, (micro, seq_rows), 1)
    valid = (positions < lengths[:, None]).astype(f32).reshape(-1, 1)
    inputs = tokens.reshape(-1, width).astype(f32)

    main = mix_weight[:, : 4 * width].reshape(own_rows, 4, peers, cols).transpose(2, 0, 1, 3)
    logits = mix_weight[:, 4 * width :].reshape(own_rows, 2, peers, local_heads)
    logits = logits.transpose(2, 0, 1, 3).reshape(peers, own_rows, logit_cols)
    mix_rows = to_columns(
        jnp.concatenate([main.reshape(peers, own_rows, 4 * cols), widen(logits)], axis=2)
    )
    wide_cols = mix_rows.shape[1]
    normed, norm_back = jax.vjp(rms_scale, inputs, norm_gain)
    normed_low, out_mine = tie(normed.astype(low), out_weight)
    out_parts = out_rows_near(out_mine)
    mix_rows, normed_low, mlp_in_rows, mlp_out_rows, out_parts = tie(
        mix_rows, normed_low, mlp_in_weight, mlp_out_weight, out_parts
    )
    gate_up = mlp_in_rows.reshape(own_rows, 2, peers, own_units).transpose(2, 0, 1, 3)
    down = mlp_out_rows.reshape(own_rows, peers, 1, own_units).transpose(1, 0, 2, 3)
    mlp_pieces = jnp.concatenate([gate_up, down], axis=2).reshape(peers, own_rows, 3 * own_units)
    mix_here = gather_dp(pack_rows(mix_rows[None], logit_cols))
    normed_all = gather_seq(normed_low)
    mlp_rows = to_columns(mlp_pieces)
    cotangent = valid * grad_out.reshape(-1, width).astype(f32)
    mix_here, out_parts, mlp_rows, normed_all, cot_low = tie(
        mix_here, out_parts, mlp_rows, normed_all, cotangent.astype(low)
    )
    mix_here = unpack_rows(mix_here, groups)
    out_here = out_rows_here(out_parts)
    in_here = gather_dp(mlp_rows[:, : 2 * own_units])
    down_here = gather_dp(mlp_rows[:, 2 * own_units :])

    projected = dot32(normed_all, mix_here).astype(low).reshape(peers, micro, seq_rows, -1)
    conv_here = lax.dynamic_index_in_dim(
        conv_weight.reshape(taps, 3, peers, cols), here, 2, keepdims=False
    ).reshape(taps, 3 * cols)
    rates_here = lax.dynamic_slice_in_dim(decay_rate, here * local_heads, local_heads)
    rate_lanes = jnp.pad(rates_here, (0, LANES - local_heads)).reshape(1, LANES)
    gain_row = out_gain.reshape(1, LANES)
    places = gather_places()
    mixed, *kept = heads_forward(
        places, projected, conv_here, rate_lanes, gain_row, local_heads
    )
    mixed, cot_low = tie(mixed, cot_low)
    mixed_low = mixed.reshape(-1, cols)
    branch, in_here = scatter_seq(dot32(mixed_low, out_here), (in_here,))
    hidden = inputs + branch

    second, second_back = jax.vjp(rms_scale, hidden, mlp_gain)
    second_all = gather_seq(second.astype(low))
    cot_all = gather_seq(cot_low)
    gate_up = dot32(second_all, in_here).astype(low)
    activated, swiglu_back = jax.vjp(swiglu, gate_up.astype(f32))
    activated_low = activated.astype(low)
    grad_down_term = t_dot(cot_all, activated_low).astype(low)
    cot_all, grad_down_term, down_here = tie(cot_all, grad_down_term, down_here)
    (grad_gate_up,) = swiglu_back(dot32(cot_all, down_here))
    grad_gate_low = grad_gate_up.astype(low)
    grad_second = scatter_seq(dot_t(grad_gate_low, in_here))
    grad_hidden_norm, grad_mlp_gain = second_back(grad_second)
    grad_hidden = cotangent + grad_hidden_norm
    branch_low = grad_hidden.astype(low)
    branch_all = gather_seq(branch_low)
    grad_down = sum_dp(grad_down_term)
    grad_in = sum_dp(t_dot(second_all, grad_gate_low))

    branch_all, activated_low = tie(branch_all, activated_low)
    grad_mixed = dot_t(branch_all, out_here).reshape(peers, micro, seq_rows, cols)
    grad_mixed, grad_down = tie(grad_mixed, grad_down)
    grad_projected, grad_conv, rate_sums, gain_sums = (
        heads_backward(
            places,
            grad_mixed,
            projected,
            conv_here,
            rate_lanes,
            gain_row,
            kept,
            local_heads,
        )
    )
    grad_projected = grad_projected.reshape(-1, wide_cols)
    grad_mix_term = t_dot(normed_all, grad_projected).astype(low)
    grad_mix_term, grad_projected = tie(grad_mix_term, grad_projected)
    mix_own = sum_dp(pack_rows(grad_mix_term.reshape(groups, -1, wide_cols), logit_cols))
    grad_normed, mixed_low = scatter_seq(dot_t(grad_projected, mix_here), (mixed_low,))
    grad_in = to_owners(grad_in)
    grad_down = to_owners(grad_down)
    out_parts = out_rows_sent(t_dot(mixed_low, branch_all).astype(low))
    grad_inputs_norm, grad_norm_gain = norm_back(grad_normed)
    grad_tokens = grad_hidden + grad_inputs_norm
    feed_out = scatter_seq(dot_t(activated_low, down_here))
    result = (valid * (hidden + feed_out)).astype(low)

    conv_terms = lax.dynamic_update_slice(
        jnp.zeros((taps, 3, peers, cols), f32),
        grad_conv.reshape(taps, 3, 1, cols),
        (0, 0, here, 0),
    )
    rate_terms = lax.dynamic_update_slice(
        jnp.zeros((LANES,), f32), rate_sums[0, :local_heads], (here * local_heads,)
    )
    sizes = [width, width, LANES, LANES, taps * 3 * width]
    summed = sum_all(
        jnp.concatenate(
            [
                grad_norm_gain,
                grad_mlp_gain,
                gain_sums[0],
                rate_terms,
                conv_terms.reshape(-1),
            ]
        ).reshape(-1, LANES)
    ).reshape(-1)
    mix_own, out_parts, summed, grad_in, grad_down = tie(
        mix_own, out_parts, summed, grad_in, grad_down
    )
    grad_mix = to_owners(unpack_rows(mix_own, 1))
    grad_out_own = out_rows_sum(out_parts)
    grad_in = order_units(grad_in, own_units)
    grad_down = grad_down.transpose(1, 0, 2).reshape(own_rows, units).astype(f32)
    ends = [sum(sizes[: i + 1]) for i in range(len(sizes))]
    sums = [summed[end - size : end] for end, size in zip(ends, sizes)]
    return (
        result.reshape(tokens.shape),
        grad_tokens.reshape(tokens.shape),
        sums[0],
        assemble(grad_mix, local_heads),
        sums[4].reshape(taps, 3 * width),
        sums[3][:heads],
        sums[2],
        grad_out_own,
        sums[1],
        grad_in,
        grad_down,
    )


def solution(mesh):
    in_specs = (
        P("dp", "seq", None),
        P("dp"),
        P(),
        P(("dp", "seq"), None),
        P(),
        P(),
        P(),
        P(("dp", "seq"), None),
        P(),
        P(("dp", "seq"), None),
        P(("dp", "seq"), None),
        P("dp", "seq", None),
    )
    out_specs = (
        P("dp", "seq", None),
        P("dp", "seq", None),
        P(),
        P(("dp", "seq"), None),
        P(),
        P(),
        P(),
        P(("dp", "seq"), None),
        P(),
        P(("dp", "seq"), None),
        P(("dp", "seq"), None),
    )
    return jax.shard_map(shards, mesh=mesh, in_specs=in_specs, out_specs=out_specs, check_vma=False)
```

```python
from functools import partial

import jax
import jax.numpy as jnp
from jax import lax
from jax.experimental import pallas as pl
from jax.experimental.pallas import tpu as pltpu
from jax.sharding import PartitionSpec as P

eps_norm = 1e-05
eps_key = 1e-06
LANES = 128
PAIR = 2
f32 = jnp.float32
low = jnp.bfloat16


def rms_scale(rows_in, gain):
    return (
        rows_in * lax.rsqrt(jnp.mean(rows_in * rows_in, axis=-1, keepdims=True) + eps_norm) * gain
    )


def swiglu(gate_up):
    hidden_units = gate_up.shape[-1] // 2
    return jax.nn.silu(gate_up[..., :hidden_units]) * gate_up[..., hidden_units:]


def mm(left, right):
    return jnp.dot(left.astype(low), right.astype(low), preferred_element_type=f32)


def mm_nt(left, right):
    return lax.dot_general(
        left.astype(low), right.astype(low), (((1,), (1,)), ((), ())), preferred_element_type=f32
    )


def halves(v):
    if isinstance(v, tuple):
        return v
    if v.dtype == low:
        return (v,)
    top = v.astype(low)
    return top, (v - top.astype(f32)).astype(low)


def dot_fine(left, right, dims):
    left, right = halves(left), halves(right)
    total = None
    for i, a in enumerate(left):
        for j, b in enumerate(right):
            if i + j < 2:
                term = lax.dot_general(a, b, (dims, ((), ())), preferred_element_type=f32)
                total = term if total is None else total + term
    return total


def fine(left, right):
    return dot_fine(left, right, ((1,), (0,)))


def fine_nt(left, right):
    return dot_fine(left, right, ((1,), (1,)))


def mm_exact(left, right):
    return jnp.dot(left, right, precision=lax.Precision.HIGHEST, preferred_element_type=f32)


def softplus(v):
    return jnp.maximum(v, 0.0) + jnp.log1p(jnp.exp(-jnp.abs(v)))


def grid_of(size):
    row = lax.broadcasted_iota(jnp.int32, (size, size), 0)
    col = lax.broadcasted_iota(jnp.int32, (size, size), 1)
    return row, col


def lower_inverses(parts, row, col):
    size = parts[0].shape[0]
    joined = (row // 2 == col // 2) & (row > col)
    unit = (row == col).astype(f32)
    inverses = [unit - jnp.where(joined, part, 0.0) for part in parts]
    width = 2
    while width < size:
        joined = (row // (2 * width) == col // (2 * width)) & (row // width > col // width)
        corners = [jnp.where(joined, part, 0.0) for part in parts]
        moved = [mm(corner, inverse) for corner, inverse in zip(corners, inverses)]
        steps = [mm(inverse, move) for inverse, move in zip(inverses, moved)]
        inverses = [inverse - change for inverse, change in zip(inverses, steps)]
        width *= 2
    return inverses


def fill_taps(ext, slot, proj, pos, prev, first, qkv):
    rows = proj.shape[2]
    ext[slot, 8 : 8 + rows, :] = proj[*pos, :, :qkv].astype(f32)
    tail = proj[*prev, rows - 16 :, :qkv].astype(f32)[8:]
    ext[slot, 0:8, :] = jnp.where(first, 0.0, tail)


def conv_rows(ext, m, conv, rows):
    taps = conv.shape[0]
    total = conv[0:1, :] * ext[m, 9 - taps : 9 - taps + rows, :]
    for j in range(1, taps):
        total = total + conv[j : j + 1, :] * ext[m, 9 - taps + j : 9 - taps + j + rows, :]
    return total


def forward_kernel(
    local_heads,
    blocks,
    perm,
    proj,
    conv,
    rates,
    gain,
    mixed,
    heads_out,
    qkv_out,
    gates,
    inv_t,
    weighted_t,
    fresh,
    states,
    ext,
    targets,
    weighted,
    scores,
    keys_t,
    state,
):
    _, micro, rows, _ = proj.shape
    cols = local_heads * LANES
    qkv = 3 * cols
    row, col = grid_of(rows)
    upto = (row >= col).astype(f32)
    lane = lax.broadcasted_iota(jnp.int32, (rows, LANES), 1)
    scale = float(LANES) ** -0.5

    def prepare(i, carry):
        work = []
        for part in range(PAIR):
            b = i * PAIR + part
            for m in range(micro):
                slot = part * micro + m
                pos, prev = (perm[b], m), (perm[jnp.maximum(b - 1, 0)], m)
                fill_taps(ext, slot, proj, pos, prev, b == 0, qkv)
                conv_out = conv_rows(ext, slot, conv, rows)
                act = conv_out * jax.nn.sigmoid(conv_out)
                logits = proj[*pos, :, 4 * cols :].astype(f32)
                decay = -rates[...] * softplus(logits)
                strength = jax.nn.sigmoid(logits)
                total = mm_exact(upto, decay)
                total_t = total.T
                gates[b, m] = jnp.where(lane < local_heads, total, strength)
                growth = jnp.exp(total)
                fade = jnp.exp(total[rows - 1 : rows, :] - total)
                for h in range(local_heads):
                    raw_q = act[:, h * LANES : (h + 1) * LANES]
                    raw_k = act[:, cols + h * LANES : cols + (h + 1) * LANES]
                    q = raw_q * (
                        lax.rsqrt(jnp.sum(raw_q * raw_q, axis=1, keepdims=True) + eps_key) * scale
                    )
                    k = raw_k * lax.rsqrt(jnp.sum(raw_k * raw_k, axis=1, keepdims=True) + eps_key)
                    q = q.astype(low)
                    k = k.astype(low)
                    v = act[:, 2 * cols + h * LANES : 2 * cols + (h + 1) * LANES].astype(low)
                    qkv_out[b, m, :, h * LANES : (h + 1) * LANES] = q
                    qkv_out[b, m, :, cols + h * LANES : cols + (h + 1) * LANES] = k
                    qkv_out[b, m, :, 2 * cols + h * LANES : 2 * cols + (h + 1) * LANES] = v
                    beta = strength[:, local_heads + h : local_heads + h + 1]
                    spread = jnp.exp(
                        jnp.minimum(total[:, h : h + 1] - total_t[h : h + 1, :], 0.0)
                    )
                    work.append(
                        (b, m * local_heads + h, q, k, v, beta, spread, growth[:, h : h + 1], fade[:, h : h + 1])
                    )
        same = [mm_nt(k, k) for _, _, _, k, *_ in work]
        cross = [mm_nt(q, k) for _, _, q, k, *_ in work]
        parts = [
            jnp.where(row > col, item[6] * item[5] * dots, 0.0) for item, dots in zip(work, same)
        ]
        inverses = lower_inverses(parts, row, col)
        keyed = [fine(inv, item[3].astype(f32) * (item[5] * item[7])) for inv, item in zip(inverses, work)]
        valued = [fine(inv, item[4].astype(f32) * item[5]) for inv, item in zip(inverses, work)]
        for n, (b, p, q, k, v, beta, spread, grow, shrink) in enumerate(work):
            inv_t[b, p] = inverses[n].T
            weighted[b, p] = keyed[n]
            weighted_t[b, p] = keyed[n].T
            targets[b, p] = valued[n]
            scores[b, p] = upto * spread * cross[n]
            keys_t[b, p] = (k.astype(f32) * shrink).T
        return carry

    lax.fori_loop(0, blocks // PAIR, prepare, 0)
    state[...] = jnp.zeros_like(state)

    def step(b, carry):
        growth = [jnp.exp(gates[b, m]) for m in range(micro)]
        chains = [(m, h, m * local_heads + h) for m in range(micro) for h in range(local_heads)]
        now = [state[p] for _, _, p in chains]
        now_halves = [halves(v) for v in now]
        new = [
            targets[b, p] - fine(weighted[b, p], parts) for (_, _, p), parts in zip(chains, now_halves)
        ]
        new_halves = [halves(v) for v in new]
        moved = [fine(keys_t[b, p], parts) for (_, _, p), parts in zip(chains, new_halves)]
        for (m, h, p), old, fed in zip(chains, now, moved):
            states[b, p] = old
            state[p] = growth[m][rows - 1 : rows, h : h + 1] * old + fed
        outs = []
        for (m, h, p), fill, parts in zip(chains, new_halves, now_halves):
            q = qkv_out[b, m, :, h * LANES : (h + 1) * LANES].astype(f32)
            outs.append(fine(q * growth[m][:, h : h + 1], parts) + fine(scores[b, p], fill))
        for (m, h, p), fill, out in zip(chains, new, outs):
            fresh[b, p] = fill
            out = out.astype(low)
            heads_out[b, m, :, h * LANES : (h + 1) * LANES] = out
            out = out.astype(f32)
            pos = (perm[b], m)
            gate = proj[*pos, :, 3 * cols + h * LANES : 3 * cols + (h + 1) * LANES].astype(f32)
            normed = out * lax.rsqrt(jnp.mean(out * out, axis=1, keepdims=True) + eps_norm) * gain[...]
            done = (normed * (gate * jax.nn.sigmoid(gate))).astype(low)
            mixed[*pos, :, h * LANES : (h + 1) * LANES] = done
        return carry

    lax.fori_loop(0, blocks, step, 0)


def backward_kernel(
    local_heads,
    blocks,
    perm,
    grad_mixed,
    proj,
    conv,
    rates,
    gain,
    heads_out,
    qkv_in,
    gates,
    inv_t,
    weighted_t,
    fresh,
    states,
    grad_proj,
    grad_conv,
    grad_rates,
    grad_gain,
    ext,
    dext,
    ahead,
    conv_sum,
    grad_out,
    value_part,
    state_part,
    grad_fresh,
    grad_states,
    grad_state,
):
    _, micro, rows, _ = proj.shape
    cols = local_heads * LANES
    qkv = 3 * cols
    taps = conv.shape[0]
    row, col = grid_of(rows)
    lane = lax.broadcasted_iota(jnp.int32, (rows, LANES), 1)
    last = lax.broadcasted_iota(jnp.int32, (rows, 1), 0) == rows - 1
    scale = float(LANES) ** -0.5
    upto_t = (col >= row).astype(f32)
    grad_gain[...] = jnp.zeros_like(grad_gain)
    grad_rates[...] = jnp.zeros_like(grad_rates)
    conv_sum[...] = jnp.zeros_like(conv_sum)
    ahead[...] = jnp.zeros_like(ahead)
    grad_state[...] = jnp.zeros_like(grad_state)

    def prepare(b, carry):
        work = []
        for m in range(micro):
            pos = (perm[b], m)
            total = gates[b, m]
            growth = jnp.exp(total)
            total_t = total.T
            for h in range(local_heads):
                p = m * local_heads + h
                here = slice(h * LANES, (h + 1) * LANES)
                out = heads_out[b, m, :, here].astype(f32)
                gate = proj[*pos, :, 3 * cols + h * LANES : 3 * cols + (h + 1) * LANES].astype(f32)
                dmixed = grad_mixed[*pos, :, here].astype(f32)
                root = lax.rsqrt(jnp.mean(out * out, axis=1, keepdims=True) + eps_norm)
                unit = out * root
                sig = jax.nn.sigmoid(gate)
                dnormed = dmixed * (gate * sig)
                dgate = dmixed * (unit * gain[...]) * (sig * (1.0 + gate * (1.0 - sig)))
                at = slice(3 * cols + h * LANES, 3 * cols + (h + 1) * LANES)
                grad_proj[*pos, :, at] = dgate.astype(low)
                grad_gain[...] += jnp.sum(dnormed * unit, axis=0, keepdims=True)
                dunit = dnormed * gain[...]
                dout = root * (dunit - unit * jnp.mean(unit * dunit, axis=1, keepdims=True))
                dout = dout.astype(low)
                grad_out[b, p] = dout.astype(grad_out.dtype)
                q = qkv_in[b, m, :, here]
                k = qkv_in[b, m, :, cols + h * LANES : cols + (h + 1) * LANES]
                spread_t = jnp.exp(jnp.minimum(total_t[h : h + 1, :] - total[:, h : h + 1], 0.0))
                grown_t = (q.astype(f32) * growth[:, h : h + 1]).T
                work.append((p, q, k, dout, upto_t * spread_t, grown_t))
        dots = [mm_nt(k, q) for _, q, k, *_ in work]
        parts = [fine(spread * dot, dout) for (_, _, _, dout, spread, _), dot in zip(work, dots)]
        fed = [fine(grown_t, dout) for _, _, _, dout, _, grown_t in work]
        for (p, *_), part, feed in zip(work, parts, fed):
            value_part[b, p] = part
            state_part[b, p] = feed
        return carry

    lax.fori_loop(0, blocks, prepare, 0)

    def step(i, carry):
        b = blocks - 1 - i
        chains = [(m, h, m * local_heads + h) for m in range(micro) for h in range(local_heads)]
        total = [gates[b, m] for m in range(micro)]
        fade = [jnp.exp(v[rows - 1 : rows, :] - v) for v in total]
        later = [grad_state[p] for _, _, p in chains]
        dnew = []
        for (m, h, p), grad in zip(chains, later):
            k = qkv_in[b, m, :, cols + h * LANES : cols + (h + 1) * LANES].astype(f32)
            dnew.append(value_part[b, p] + fine(k * fade[m][:, h : h + 1], grad))
        moved = [fine(weighted_t[b, p], grad) for (_, _, p), grad in zip(chains, dnew)]
        for (m, h, p), grad, fill, move in zip(chains, later, dnew, moved):
            grad_states[b, p] = grad
            grad_fresh[b, p] = fill
            carried = jnp.exp(total[m][rows - 1 : rows, h : h + 1])
            grad_state[p] = state_part[b, p] + carried * grad - move
        return carry

    lax.fori_loop(0, blocks, step, 0)

    def finish(i, carry):
        b = blocks - 1 - i
        work = []
        for m in range(micro):
            total = gates[b, m]
            total_t = total.T
            growth = jnp.exp(total)
            fade = jnp.exp(total[rows - 1 : rows, :] - total)
            for h in range(local_heads):
                p = m * local_heads + h
                q = qkv_in[b, m, :, h * LANES : (h + 1) * LANES]
                k = qkv_in[b, m, :, cols + h * LANES : cols + (h + 1) * LANES]
                v = qkv_in[b, m, :, 2 * cols + h * LANES : 2 * cols + (h + 1) * LANES]
                beta = total[:, local_heads + h : local_heads + h + 1]
                spread = jnp.exp(jnp.minimum(total[:, h : h + 1] - total_t[h : h + 1, :], 0.0))
                work.append(
                    (p, q, k, v, beta, spread, growth[:, h : h + 1], fade[:, h : h + 1], growth[rows - 1 : rows, h : h + 1])
                )
        number = range(len(work))
        queries = [item[1] for item in work]
        keys = [item[2] for item in work]
        douts = [grad_out[b, item[0]].astype(low) for item in work]
        news = [halves(fresh[b, item[0]]) for item in work]
        nows = [halves(states[b, item[0]]) for item in work]
        laters = [halves(grad_states[b, item[0]]) for item in work]
        dright = [fine(inv_t[b, item[0]], grad_fresh[b, item[0]]) for item in work]
        dgrown = [fine_nt(douts[n], nows[n]) for n in number]
        dshrunk = [fine_nt(news[n], laters[n]) for n in number]
        dots = [mm_nt(queries[n], keys[n]) for n in number]
        same = [mm_nt(keys[n], keys[n]) for n in number]
        dscores = [fine_nt(douts[n], news[n]) for n in number]
        dright_halves = [halves(v) for v in dright]
        dweighted = [-fine_nt(dright_halves[n], nows[n]) for n in number]
        dbelow = [fine_nt(dright_halves[n], news[n]) for n in number]
        keyed, moved = [], []
        for n in number:
            beta, spread = work[n][4], work[n][5]
            dscores[n] = dscores[n] * jnp.where(row >= col, spread, 0.0)
            dbelow[n] = dbelow[n] * jnp.where(row > col, -spread, 0.0)
            keyed.append(dbelow[n] * same[n])
            moved.append(dscores[n] * dots[n] + keyed[n] * beta)
            dbelow[n] = dbelow[n] * beta
        dq = [fine(dscores[n], keys[n]) for n in number]
        dk = [fine(dscores[n].T, queries[n]) for n in number]
        dk_same = [fine(dbelow[n] + dbelow[n].T, keys[n]) for n in number]
        for m in range(micro):
            pos, prev = (perm[b], m), (perm[jnp.maximum(b - 1, 0)], m)
            fill_taps(ext, m, proj, pos, prev, b == 0, qkv)
            conv_out = conv_rows(ext, m, conv, rows)
            sig = jax.nn.sigmoid(conv_out)
            act = conv_out * sig
            slope = sig * (1.0 + conv_out * (1.0 - sig))
            dtotal = jnp.zeros((rows, LANES), f32)
            dstrength = jnp.zeros((rows, LANES), f32)
            for h in range(local_heads):
                n = m * local_heads + h
                p, q, k, v, beta, spread, grow, shrink, carried = work[n]
                q32, k32, v32 = q.astype(f32), k.astype(f32), v.astype(f32)
                dquery = grow * dgrown[n] + dq[n]
                dkey = (beta * grow) * dweighted[n] + shrink * dshrunk[n] + dk[n] + dk_same[n]
                dvalue = beta * dright[n]
                weighed = dweighted[n] * k32 * grow
                shrunk = dshrunk[n] * k32 * shrink
                dstr = jnp.sum(dright[n] * v32 + weighed, axis=1, keepdims=True) + jnp.sum(
                    keyed[n], axis=1, keepdims=True
                )
                dtot = jnp.sum(
                    dgrown[n] * q32 * grow + weighed * beta - shrunk, axis=1, keepdims=True
                ) + jnp.sum(moved[n] - moved[n].T, axis=1, keepdims=True)
                end = jnp.sum(shrunk) + jnp.sum(carried * (states[b, p] * grad_states[b, p]))
                dtot = dtot + jnp.where(last, end, 0.0)
                dtotal = dtotal + jnp.where(lane == h, dtot, 0.0)
                dstrength = dstrength + jnp.where(lane == local_heads + h, dstr, 0.0)
                for part, grad in ((0, dquery), (1, dkey), (2, dvalue)):
                    at = part * cols + h * LANES
                    grad = grad.astype(low).astype(f32)
                    if part == 0:
                        grad = grad * scale
                    if part < 2:
                        raw = act[:, at : at + LANES]
                        root = lax.rsqrt(jnp.sum(raw * raw, axis=1, keepdims=True) + eps_key)
                        unit = raw * root
                        grad = root * (grad - unit * jnp.sum(unit * grad, axis=1, keepdims=True))
                    dext[m, 0:rows, at : at + LANES] = grad * slope[:, at : at + LANES]
            dext[m, rows : rows + 8, :] = ahead[m]
            dconv = dext[m, 0:rows, :]
            ahead[m] = dconv[0:8, :]
            du = conv[taps - 1 : taps, :] * dconv
            for j in range(taps - 1):
                du = du + conv[j : j + 1, :] * dext[m, taps - 1 - j : taps - 1 - j + rows, :]
            grad_proj[*pos, :, :qkv] = du.astype(low)
            for j in range(taps):
                term = dconv * ext[m, 9 - taps + j : 9 - taps + j + rows, :]
                conv_sum[j] += jnp.sum(term.reshape(rows // 8, 8, qkv), axis=0)
            logits = proj[*pos, :, 4 * cols :].astype(f32)
            ddecay = mm_exact(upto_t, dtotal)
            strength = gates[b, m]
            dlogit = jnp.where(
                lane < local_heads,
                -rates[...] * jax.nn.sigmoid(logits) * ddecay,
                strength * (1.0 - strength) * dstrength,
            )
            dlogit = jnp.where(lane < 2 * local_heads, dlogit, 0.0).astype(low)
            grad_proj[*pos, :, 4 * cols :] = dlogit
            grad_rates[...] -= jnp.sum(softplus(logits) * ddecay, axis=0, keepdims=True)
        return carry

    lax.fori_loop(0, blocks, finish, 0)
    for j in range(taps):
        grad_conv[j : j + 1, :] = jnp.sum(conv_sum[j], axis=0, keepdims=True)


def in_vmem():
    return pl.BlockSpec(memory_space=pltpu.VMEM)


def heads_forward(perm, proj, conv, rates, gain, local_heads):
    blocks, micro, rows, _ = proj.shape
    cols = local_heads * LANES
    chains = micro * local_heads

    def shape(dims, kind):
        return jax.ShapeDtypeStruct(dims, kind)

    return pl.pallas_call(
        partial(forward_kernel, local_heads, perm.shape[0]),
        out_shape=(
            shape((blocks, micro, rows, cols), low),
            shape((blocks, micro, rows, cols), low),
            shape((blocks, micro, rows, 3 * cols), low),
            shape((blocks, micro, rows, LANES), f32),
            shape((blocks, chains, rows, rows), f32),
            shape((blocks, chains, LANES, rows), f32),
            shape((blocks, chains, rows, LANES), f32),
            shape((blocks, chains, LANES, LANES), f32),
        ),
        in_specs=[pl.BlockSpec(memory_space=pltpu.SMEM)] + [in_vmem()] * 4,
        out_specs=(in_vmem(),) * 8,
        scratch_shapes=[
            pltpu.VMEM((PAIR * micro, rows + 8, 3 * cols), f32),
            pltpu.VMEM((blocks, chains, rows, LANES), f32),
            pltpu.VMEM((blocks, chains, rows, LANES), f32),
            pltpu.VMEM((blocks, chains, rows, rows), f32),
            pltpu.VMEM((blocks, chains, LANES, rows), f32),
            pltpu.VMEM((chains, LANES, LANES), f32),
        ],
        compiler_params=pltpu.CompilerParams(vmem_limit_bytes=50 * 1024 * 1024),
        name="heads_forward",
    )(perm, proj, conv, rates, gain)


def heads_backward(perm, grad_mixed, proj, conv, rates, gain, kept, local_heads):
    blocks, micro, rows, wide = proj.shape
    cols = local_heads * LANES
    chains = micro * local_heads
    taps = conv.shape[0]

    def shape(dims, kind):
        return jax.ShapeDtypeStruct(dims, kind)

    return pl.pallas_call(
        partial(backward_kernel, local_heads, perm.shape[0]),
        out_shape=(
            shape((blocks, micro, rows, wide), low),
            shape((taps, 3 * cols), f32),
            shape((1, LANES), f32),
            shape((1, LANES), f32),
        ),
        in_specs=[pl.BlockSpec(memory_space=pltpu.SMEM)] + [in_vmem()] * 12,
        out_specs=(in_vmem(),) * 4,
        scratch_shapes=[
            pltpu.VMEM((micro, rows + 8, 3 * cols), f32),
            pltpu.VMEM((micro, rows + 8, 3 * cols), f32),
            pltpu.VMEM((micro, 8, 3 * cols), f32),
            pltpu.VMEM((taps, 8, 3 * cols), f32),
            pltpu.VMEM((blocks, chains, rows, LANES), f32),
            pltpu.VMEM((blocks, chains, rows, LANES), f32),
            pltpu.VMEM((blocks, chains, LANES, LANES), f32),
            pltpu.VMEM((blocks, chains, rows, LANES), f32),
            pltpu.VMEM((blocks, chains, LANES, LANES), f32),
            pltpu.VMEM((chains, LANES, LANES), f32),
        ],
        compiler_params=pltpu.CompilerParams(vmem_limit_bytes=50 * 1024 * 1024),
        name="heads_backward",
    )(perm, grad_mixed, proj, conv, rates, gain, *kept)


both = ("dp", "seq")


def swap(value, axis, bit):
    return lax.ppermute(value, axis, [(i, i ^ bit) for i in range(lax.axis_size(axis))])


def tie(*values):
    return lax.optimization_barrier(values)


def gather_places():
    peers = lax.axis_size("seq")
    place = jnp.arange(peers, dtype=jnp.int32)
    if peers != 8:
        return place
    place = place ^ lax.axis_index("seq").astype(jnp.int32)
    return place // 2 + 4 * (place % 2)


def gather_seq(rows_in):
    if lax.axis_size("seq") != 8:
        return lax.all_gather(rows_in, "seq", axis=0, tiled=True)
    half = rows_in.shape[0] // 2
    top, bottom = rows_in[:half], rows_in[half:]
    top_x, bottom_y = swap(top, "seq", 2), swap(bottom, "seq", 4)
    top_y = swap(jnp.concatenate([top, top_x]), "seq", 4)
    bottom_x = swap(jnp.concatenate([bottom, bottom_y]), "seq", 2)
    near = jnp.concatenate(
        [top, bottom, top_x, bottom_x[:half], top_y[:half], bottom_y, top_y[half:], bottom_x[half:]]
    )
    return jnp.concatenate([near, swap(near, "seq", 1)])


def scatter_seq(partial_rows, beside=None):
    peers = lax.axis_size("seq")
    if peers != 8:
        total = lax.psum_scatter(
            partial_rows.astype(low), "seq", scatter_dimension=0, tiled=True
        ).astype(f32)
        return total if beside is None else (total, *beside)
    terms = partial_rows.astype(low).reshape(peers, -1, partial_rows.shape[-1])
    half = terms.shape[1] // 2
    near = terms[:4].astype(f32) + swap(terms[4:], "seq", 1).astype(f32)
    top, bottom = near[:, :half].astype(low), near[:, half:].astype(low)
    top_x = swap(top[1::2], "seq", 2)
    bottom_y = swap(bottom[2:], "seq", 4)
    top = near[0::2, :half] + top_x.astype(f32)
    bottom = near[:2, half:] + bottom_y.astype(f32)
    if beside is not None:
        top, bottom, *beside = tie(top, bottom, *beside)
    top_y = swap(top[1].astype(low), "seq", 4)
    bottom_x = swap(bottom[1].astype(low), "seq", 2)
    total = jnp.concatenate([top[0] + top_y.astype(f32), bottom[0] + bottom_x.astype(f32)])
    return total if beside is None else (total, *beside)


def sum_all(value):
    for axis in both:
        size, bit = lax.axis_size(axis), 1
        if size.bit_length() % 2 == 0:
            value, bit = value + swap(value, axis, 1), 2
        while bit < size:
            one, two, three = (swap(value, axis, k * bit) for k in (1, 2, 3))
            value, bit = (value + one) + (two + three), 4 * bit
    return value


def to_columns(pieces):
    rows_here = lax.all_to_all(pieces, "seq", split_axis=0, concat_axis=0, tiled=True)
    return rows_here.reshape(-1, pieces.shape[-1])


def gather_dp(rows_here):
    return lax.all_gather(rows_here, "dp", axis=0, tiled=True)


def sum_dp(term):
    return lax.psum_scatter(term.astype(low), "dp", scatter_dimension=0, tiled=True)


def to_owners(own):
    pieces = own.reshape(lax.axis_size("seq"), -1, own.shape[1])
    return lax.all_to_all(pieces, "seq", split_axis=0, concat_axis=0, tiled=True)


def widen(columns):
    extra = -columns.shape[-1] % LANES
    return jnp.pad(columns, [(0, 0)] * (columns.ndim - 1) + [(0, extra)])


def assemble_kernel(local_heads, pieces, whole):
    peers, _, wide = pieces.shape
    cols = (wide - LANES) // 4
    width = cols * peers
    logits = []
    for part in range(5):
        for j in range(peers):
            from_here = slice(part * cols, min((part + 1) * cols, wide))
            total = pieces[j, :, from_here].astype(f32)
            if part < 4:
                whole[:, part * width + j * cols : part * width + (j + 1) * cols] = total
            else:
                logits.append(total)
    for kind in range(2):
        here = slice(kind * local_heads, (kind + 1) * local_heads)
        for j in range(peers):
            at = 4 * width + kind * local_heads * peers + j * local_heads
            whole[:, at : at + local_heads] = logits[j][:, here]


def assemble(pieces, local_heads):
    peers, rows, wide = pieces.shape
    total = (wide - LANES) * peers + 2 * local_heads * peers
    return pl.pallas_call(
        partial(assemble_kernel, local_heads),
        out_shape=jax.ShapeDtypeStruct((rows, total), f32),
        in_specs=[in_vmem()],
        out_specs=in_vmem(),
        compiler_params=pltpu.CompilerParams(vmem_limit_bytes=30 * 1024 * 1024),
        name="assemble",
    )(pieces)


def order_kernel(units, pieces, whole):
    peers, rows, _ = pieces.shape
    wide = units + LANES // 2
    middle = lax.broadcasted_iota(jnp.int32, (rows, LANES), 1) < LANES // 2
    for kind in range(2):
        for j in range(0, peers, 2):
            if kind == 0:
                one = pieces[j, :, :wide].astype(f32)
                two = pltpu.roll(pieces[j + 1, :, :wide].astype(f32), LANES // 2, axis=1)
            else:
                start = 2 * units - wide
                one = pltpu.roll(pieces[j, :, start:].astype(f32), wide - LANES // 2, axis=1)
                two = pieces[j + 1, :, start:].astype(f32)
            at = (kind * peers + j) * units
            whole[:, at : at + wide - LANES] = one[:, : wide - LANES]
            at = at + wide - LANES
            whole[:, at : at + LANES] = jnp.where(middle, one[:, wide - LANES :], two[:, :LANES])
            at = at + LANES
            whole[:, at : at + wide - LANES] = two[:, LANES:]


def order_units(pieces, units):
    peers, rows, _ = pieces.shape
    if units % LANES != LANES // 2 or peers % 2 != 0:
        whole = pieces.reshape(peers, rows, 2, units).transpose(1, 2, 0, 3)
        return whole.reshape(rows, 2 * units * peers).astype(f32)
    return pl.pallas_call(
        partial(order_kernel, units),
        out_shape=jax.ShapeDtypeStruct((rows, 2 * units * peers), f32),
        in_specs=[in_vmem()],
        out_specs=in_vmem(),
        compiler_params=pltpu.CompilerParams(vmem_limit_bytes=30 * 1024 * 1024),
        name="order_units",
    )(pieces)


def pack_rows(blocks, logit_cols):
    rows, cols = blocks.shape[1], blocks.shape[2] - LANES
    below = blocks[:, :, cols : cols + logit_cols].swapaxes(1, 2)
    below = jnp.pad(below, ((0, 0), (0, 16 - logit_cols), (0, cols - rows)))
    return jnp.concatenate([blocks[:, :, :cols], below], axis=1).reshape(-1, cols)


def unpack_rows(packed, count):
    blocks = packed.reshape(count, -1, packed.shape[1])
    rows = blocks.shape[1] - 16
    logits = blocks[:, rows:, :rows].swapaxes(1, 2)
    logits = jnp.pad(logits, ((0, 0), (0, 0), (0, LANES - 16)))
    blocks = jnp.concatenate([blocks[:, :rows], logits], axis=2)
    return blocks.reshape(-1, blocks.shape[2])


def hop(step, back):
    groups, peers = lax.axis_size("dp"), lax.axis_size("seq")
    ratio = peers // groups
    pairs = [(s, (s + step) % groups * ratio + s // groups) for s in range(peers)]
    return [(b, a) for a, b in pairs] if back else pairs


def pick(parts, index):
    return lax.dynamic_index_in_dim(parts, index, 0, keepdims=False)


def out_rows_near(rows):
    return jnp.stack([rows] + [swap(rows, "dp", k) for k in range(1, lax.axis_size("dp"))])


def out_rows_here(parts):
    groups, ratio = lax.axis_size("dp"), lax.axis_size("seq") // lax.axis_size("dp")
    place, here = lax.axis_index("dp"), lax.axis_index("seq")
    got = jnp.stack(
        [
            lax.ppermute(pick(parts, (here + t) % groups ^ place), "seq", hop(t, False))
            for t in range(groups)
        ]
    )
    return jnp.concatenate([pick(got, (here // ratio - e) % groups) for e in range(groups)])


def out_rows_sent(term):
    groups, ratio = lax.axis_size("dp"), lax.axis_size("seq") // lax.axis_size("dp")
    here = lax.axis_index("seq")
    parts = term.reshape(groups, -1, term.shape[1])
    got = jnp.stack(
        [
            lax.ppermute(pick(parts, (here // ratio - t) % groups), "seq", hop(t, True))
            for t in range(groups)
        ]
    )
    return jnp.stack([pick(got, (z - here) % groups) for z in range(groups)])


def out_rows_sum(parts):
    place = lax.axis_index("dp")
    total = pick(parts, place).astype(f32)
    for k in range(1, lax.axis_size("dp")):
        total = total + swap(pick(parts, place ^ k), "dp", k).astype(f32)
    return total


def dot32(left, right):
    return jnp.dot(left, right, preferred_element_type=f32)


def dot_t(left, right):
    return lax.dot_general(left, right, (((1,), (1,)), ((), ())), preferred_element_type=f32)


def t_dot(left, right):
    return lax.dot_general(left, right, (((0,), (0,)), ((), ())), preferred_element_type=f32)


def shards(
    tokens,
    lengths,
    norm_gain,
    mix_weight,
    conv_weight,
    decay_rate,
    out_gain,
    out_weight,
    mlp_gain,
    mlp_in_weight,
    mlp_out_weight,
    grad_out,
):
    micro, seq_rows, width = tokens.shape
    heads = decay_rate.shape[0]
    groups = lax.axis_size("dp")
    peers = lax.axis_size("seq")
    here = lax.axis_index("seq")
    local_heads = heads // peers
    taps = conv_weight.shape[0]
    units = mlp_out_weight.shape[1]
    own_units = units // peers
    own_rows = mix_weight.shape[0]
    cols = width // peers
    logit_cols = 2 * local_heads

    positions = here * seq_rows + lax.broadcasted_iota(jnp.int32, (micro, seq_rows), 1)
    valid = (positions < lengths[:, None]).astype(f32).reshape(-1, 1)
    inputs = tokens.reshape(-1, width).astype(f32)

    main = mix_weight[:, : 4 * width].reshape(own_rows, 4, peers, cols).transpose(2, 0, 1, 3)
    logits = mix_weight[:, 4 * width :].reshape(own_rows, 2, peers, local_heads)
    logits = logits.transpose(2, 0, 1, 3).reshape(peers, own_rows, logit_cols)
    mix_rows = to_columns(
        jnp.concatenate([main.reshape(peers, own_rows, 4 * cols), widen(logits)], axis=2)
    )
    wide_cols = mix_rows.shape[1]
    normed, norm_back = jax.vjp(rms_scale, inputs, norm_gain)
    normed_low, out_mine = tie(normed.astype(low), out_weight)
    out_parts = out_rows_near(out_mine)
    mix_rows, normed_low, mlp_in_rows, mlp_out_rows = tie(
        mix_rows, normed_low, mlp_in_weight, mlp_out_weight
    )
    gate_up = mlp_in_rows.reshape(own_rows, 2, peers, own_units).transpose(2, 0, 1, 3)
    down = mlp_out_rows.reshape(own_rows, peers, 1, own_units).transpose(1, 0, 2, 3)
    mlp_pieces = jnp.concatenate([gate_up, down], axis=2).reshape(peers, own_rows, 3 * own_units)
    mix_here = gather_dp(pack_rows(mix_rows[None], logit_cols))
    normed_all = gather_seq(normed_low)
    mlp_pieces, out_parts = tie(mlp_pieces, out_parts)
    mlp_rows = to_columns(mlp_pieces)
    cotangent = valid * grad_out.reshape(-1, width).astype(f32)
    mix_here, out_parts, mlp_rows, normed_all, cot_low = tie(
        mix_here, out_parts, mlp_rows, normed_all, cotangent.astype(low)
    )
    mix_here = unpack_rows(mix_here, groups)
    out_here = out_rows_here(out_parts)
    in_here = gather_dp(mlp_rows[:, : 2 * own_units])
    down_here = gather_dp(mlp_rows[:, 2 * own_units :])

    projected = dot32(normed_all, mix_here).astype(low).reshape(peers, micro, seq_rows, -1)
    conv_here = lax.dynamic_index_in_dim(
        conv_weight.reshape(taps, 3, peers, cols), here, 2, keepdims=False
    ).reshape(taps, 3 * cols)
    rates_here = lax.dynamic_slice_in_dim(decay_rate, here * local_heads, local_heads)
    rate_lanes = jnp.pad(rates_here, (0, LANES - local_heads)).reshape(1, LANES)
    gain_row = out_gain.reshape(1, LANES)
    places = gather_places()
    mixed, *kept = heads_forward(
        places, projected, conv_here, rate_lanes, gain_row, local_heads
    )
    mixed, cot_low = tie(mixed, cot_low)
    mixed_low = mixed.reshape(-1, cols)
    branch, in_here = scatter_seq(dot32(mixed_low, out_here), (in_here,))
    hidden = inputs + branch

    second, second_back = jax.vjp(rms_scale, hidden, mlp_gain)
    second_all = gather_seq(second.astype(low))
    cot_all = gather_seq(cot_low)
    gate_up = dot32(second_all, in_here).astype(low)
    activated, swiglu_back = jax.vjp(swiglu, gate_up.astype(f32))
    activated_low = activated.astype(low)
    grad_down_term = t_dot(cot_all, activated_low).astype(low)
    cot_all, grad_down_term, down_here = tie(cot_all, grad_down_term, down_here)
    (grad_gate_up,) = swiglu_back(dot32(cot_all, down_here))
    grad_gate_low = grad_gate_up.astype(low)
    grad_second = scatter_seq(dot_t(grad_gate_low, in_here))
    grad_hidden_norm, grad_mlp_gain = second_back(grad_second)
    grad_hidden = cotangent + grad_hidden_norm
    branch_low = grad_hidden.astype(low)
    branch_all = gather_seq(branch_low)
    grad_down = sum_dp(grad_down_term)
    grad_in = sum_dp(t_dot(second_all, grad_gate_low))

    branch_all, activated_low = tie(branch_all, activated_low)
    grad_mixed = dot_t(branch_all, out_here).reshape(peers, micro, seq_rows, cols)
    grad_mixed, grad_down = tie(grad_mixed, grad_down)
    grad_projected, grad_conv, rate_sums, gain_sums = (
        heads_backward(
            places,
            grad_mixed,
            projected,
            conv_here,
            rate_lanes,
            gain_row,
            kept,
            local_heads,
        )
    )
    grad_projected = grad_projected.reshape(-1, wide_cols)
    grad_mix_term = t_dot(normed_all, grad_projected).astype(low)
    grad_mix_term, grad_projected = tie(grad_mix_term, grad_projected)
    mix_own = sum_dp(pack_rows(grad_mix_term.reshape(groups, -1, wide_cols), logit_cols))
    grad_normed, mixed_low = scatter_seq(dot_t(grad_projected, mix_here), (mixed_low,))
    grad_in = to_owners(grad_in)
    grad_down = to_owners(grad_down)
    out_parts = out_rows_sent(t_dot(mixed_low, branch_all).astype(low))
    grad_inputs_norm, grad_norm_gain = norm_back(grad_normed)
    grad_tokens = grad_hidden + grad_inputs_norm
    feed_out = scatter_seq(dot_t(activated_low, down_here))
    result = (valid * (hidden + feed_out)).astype(low)

    conv_terms = lax.dynamic_update_slice(
        jnp.zeros((taps, 3, peers, cols), f32),
        grad_conv.reshape(taps, 3, 1, cols),
        (0, 0, here, 0),
    )
    rate_terms = lax.dynamic_update_slice(
        jnp.zeros((LANES,), f32), rate_sums[0, :local_heads], (here * local_heads,)
    )
    sizes = [width, width, LANES, LANES, taps * 3 * width]
    summed = sum_all(
        jnp.concatenate(
            [
                grad_norm_gain,
                grad_mlp_gain,
                gain_sums[0],
                rate_terms,
                conv_terms.reshape(-1),
            ]
        ).reshape(-1, LANES)
    ).reshape(-1)
    mix_own, out_parts, summed, grad_in, grad_down = tie(
        mix_own, out_parts, summed, grad_in, grad_down
    )
    grad_mix = to_owners(unpack_rows(mix_own, 1))
    grad_out_own = out_rows_sum(out_parts)
    grad_in = order_units(grad_in, own_units)
    grad_down = grad_down.transpose(1, 0, 2).reshape(own_rows, units).astype(f32)
    ends = [sum(sizes[: i + 1]) for i in range(len(sizes))]
    sums = [summed[end - size : end] for end, size in zip(ends, sizes)]
    return (
        result.reshape(tokens.shape),
        grad_tokens.reshape(tokens.shape),
        sums[0],
        assemble(grad_mix, local_heads),
        sums[4].reshape(taps, 3 * width),
        sums[3][:heads],
        sums[2],
        grad_out_own,
        sums[1],
        grad_in,
        grad_down,
    )


def solution(mesh):
    in_specs = (
        P("dp", "seq", None),
        P("dp"),
        P(),
        P(("dp", "seq"), None),
        P(),
        P(),
        P(),
        P(("dp", "seq"), None),
        P(),
        P(("dp", "seq"), None),
        P(("dp", "seq"), None),
        P("dp", "seq", None),
    )
    out_specs = (
        P("dp", "seq", None),
        P("dp", "seq", None),
        P(),
        P(("dp", "seq"), None),
        P(),
        P(),
        P(),
        P(("dp", "seq"), None),
        P(),
        P(("dp", "seq"), None),
        P(("dp", "seq"), None),
    )
    return jax.shard_map(shards, mesh=mesh, in_specs=in_specs, out_specs=out_specs, check_vma=False)
```
